512 devices in a mesh: slide: 16 (over z, y_lo), strip: 32 (over y_hi, x, core).
Axes of the slice: x: 4, y: 8 (y_hi: 4, y_lo: 2; y = y_hi * 2 + y_lo), z: 8, core: 2. Of those that a mesh axis runs over, the one named last changes fastest.
Arguments:
- image: bfloat16 [16, 192, 64, 256], P('slide', 'strip'), may hold values from -6 to 6
- cotangent: bfloat16 [16, 192, 64, 256], P('slide', 'strip'), may hold values from -6 to 6
- kernel_tall: bfloat16 [51, 5, 256], replicated, may hold values from -0.375 to 0.375
- kernel_wide: bfloat16 [5, 51, 256], replicated, may hold values from -0.375 to 0.375
- layer_norm_gain: float32 [256], replicated, may hold values from 0.5 to 1.5
- layer_norm_bias: float32 [256], replicated, may hold values from -3 to 3
- w_in: bfloat16 [256, 1024], replicated, may hold values from -0.375 to 0.375
- b_in: float32 [1024], replicated, may hold values from -3 to 3
- w_out: bfloat16 [1024, 256], replicated, may hold values from -0.1875 to 0.1875
- b_out: float32 [256], replicated, may hold values from -3 to 3
Outputs:
- output: bfloat16 [16, 192, 64, 256], P('slide', 'strip')
- grad_image: bfloat16 [16, 192, 64, 256], P('slide', 'strip')
- grad_tall: float32 [51, 5, 256], replicated
- grad_wide: float32 [5, 51, 256], replicated
- grad_gain: float32 [256], replicated
- grad_shift: float32 [256], replicated
- grad_w_in: float32 [256, 1024], replicated
- grad_b_in: float32 [1024], replicated
- grad_w_out: float32 [1024, 256], replicated
- grad_b_out: float32 [256], replicated
The draws below stay inside these ranges and needn't reach their ends.
All inputs are finite; a program needn't handle non-finite values.
Results may differ from the reference program's by a relative error of at most 0.0085.
Values may be sent and summed in bfloat16 or wider, within the bound.
No kernel may reach another device: no remote copies, remote signals or barrier semaphores. Data moves between devices by JAX's collectives and lax.ppermute only.
A program may use at most 64 MiB of HBM per device.

```python
import jax
import jax.numpy as jnp
from jax import lax

C = 256
FF = 1024
LONG = 51
SHORT = 5
H = 192
W = 64
SLIDES = 16
CELLS = 196608


def levels(key, dims, shards, least, largest):
    level, own = 1.0, jax.random.fold_in(key, 6)
    for dim, blocks in shards:
        draws = jnp.exp(jax.random.uniform(jax.random.fold_in(own, dim), (blocks,), jnp.float32, least / len(shards), largest / len(shards)))
        level = level * jnp.repeat(draws, dims[dim] // blocks).reshape([-1 if axis == dim else 1 for axis in range(len(dims))])
    return level


def normal_values(stream_key, extent, scale, bound, pieces=(), dtype=jnp.bfloat16):
    values = jax.random.normal(stream_key, extent, jnp.float32) * scale
    if len(pieces) > 0:
        values = levels(stream_key, extent, pieces, -0.22, 0.18) * values
    return jnp.clip(values, min=-bound, max=bound).astype(dtype)


def setup_inputs(seed: int = 0) -> dict:
    streams_of = jax.random.split(jax.random.key(seed), 11)
    image = normal_values(streams_of[0], (SLIDES, H, W, C), 1.0, 6.0, ((0, 16), (1, 32)))
    cotangent = normal_values(streams_of[1], (SLIDES, H, W, C), 1.0, 6.0, ((0, 16), (1, 32)))
    kernel_tall = normal_values(streams_of[2], (LONG, SHORT, C), (LONG * SHORT) ** -0.5, 0.375)
    kernel_wide = normal_values(streams_of[3], (SHORT, LONG, C), (LONG * SHORT) ** -0.5, 0.375)
    layer_norm_gain = jnp.clip(jax.random.uniform(streams_of[4], (C,), jnp.float32, 0.5, 1.5), 0.5, 1.5)
    layer_norm_bias = normal_values(streams_of[5], (C,), 0.5, 3.0, (), jnp.float32)
    w_in = normal_values(streams_of[6], (C, FF), C ** -0.5, 0.375)
    b_in = normal_values(streams_of[7], (FF,), 0.5, 3.0, (), jnp.float32)
    w_out = normal_values(streams_of[8], (FF, C), FF ** -0.5, 0.1875)
    b_out = normal_values(streams_of[9], (C,), 0.5, 3.0, (), jnp.float32)
    return {"image": image, "cotangent": cotangent, "kernel_tall": kernel_tall, "kernel_wide": kernel_wide, "layer_norm_gain": layer_norm_gain, "layer_norm_bias": layer_norm_bias, "w_in": w_in, "b_in": b_in, "w_out": w_out, "b_out": b_out}


epsilon = 1e-06

def depth_conv(source, kernel, pad_rows, pad_cols):
    return lax.conv_general_dilated(source[None], kernel[:, :, None, :], (1, 1), ((pad_rows, pad_rows), (pad_cols, pad_cols)), dimension_numbers=('NHWC', 'HWIO', 'NHWC'), feature_group_count=source.shape[-1], preferred_element_type=jnp.float32)[0]

def kernel_grad(padded, upstream):
    return lax.conv_general_dilated(padded[None], upstream[:, :, None, :], (1, 1), 'VALID', dimension_numbers=('NHWC', 'HWIO', 'NHWC'), feature_group_count=padded.shape[-1], preferred_element_type=jnp.float32)[0]

def one_region(image, cotangent, kernel_tall, kernel_wide, layer_norm_gain, layer_norm_bias, w_in, b_in, w_out, b_out):
    tall_pad = (kernel_tall.shape[0] - 1) // 2
    rim_width = (kernel_tall.shape[1] - 1) // 2
    wide_pad = (kernel_wide.shape[1] - 1) // 2
    channels = image.shape[-1]
    mixed = depth_conv(image, kernel_tall, tall_pad, rim_width).astype(jnp.bfloat16)
    conv_out = depth_conv(mixed, kernel_wide, rim_width, wide_pad)
    mean_removed = conv_out - lax.optimization_barrier(jnp.mean(conv_out, axis=-1, keepdims=True))
    inverse_deviation = lax.rsqrt(lax.optimization_barrier(jnp.mean(mean_removed * mean_removed, axis=-1, keepdims=True)) + epsilon)
    standardized_input = mean_removed * inverse_deviation
    normalized_output = (standardized_input * layer_norm_gain + layer_norm_bias).astype(jnp.bfloat16)
    flat_normed = normalized_output.reshape(-1, channels)
    pre_act = jnp.dot(flat_normed, w_in, preferred_element_type=jnp.float32) + b_in
    cdf_value = 0.5 * (1.0 + lax.erf(pre_act * 0.7071067811865476))
    hidden = (pre_act * cdf_value).astype(jnp.bfloat16)
    branch = jnp.dot(hidden, w_out, preferred_element_type=jnp.float32) + b_out
    output = (image.astype(jnp.float32) + branch.reshape(image.shape)).astype(jnp.bfloat16)
    flat_cot = cotangent.reshape(-1, channels)
    g_w_out = jnp.dot(hidden.T, flat_cot, preferred_element_type=jnp.float32)
    g_b_out = lax.optimization_barrier(jnp.sum(flat_cot.astype(jnp.float32), axis=0))
    d_hidden = jnp.dot(flat_cot, w_out.T, preferred_element_type=jnp.float32)
    slope = cdf_value + pre_act * jnp.exp(-0.5 * pre_act * pre_act) * 0.3989422804014327
    d_pre = (d_hidden * slope).astype(jnp.bfloat16)
    g_w_in = jnp.dot(flat_normed.T, d_pre, preferred_element_type=jnp.float32)
    g_b_in = lax.optimization_barrier(jnp.sum(lax.optimization_barrier(d_pre).astype(jnp.float32), axis=0))
    grad_layer_norm = jnp.dot(d_pre, w_in.T, preferred_element_type=jnp.float32).reshape(image.shape)
    grad_norm_gain = lax.optimization_barrier(jnp.sum(grad_layer_norm * standardized_input, axis=(0, 1)))
    g_shift = lax.optimization_barrier(jnp.sum(grad_layer_norm, axis=(0, 1)))
    grad_standardized = grad_layer_norm * layer_norm_gain
    grad_depth_output = (inverse_deviation * (grad_standardized - lax.optimization_barrier(jnp.mean(grad_standardized, axis=-1, keepdims=True)) - standardized_input * lax.optimization_barrier(jnp.mean(grad_standardized * standardized_input, axis=-1, keepdims=True)))).astype(jnp.bfloat16)
    d_mixed = depth_conv(grad_depth_output, kernel_wide[::-1, ::-1], rim_width, wide_pad).astype(jnp.bfloat16)
    g_wide = kernel_grad(jnp.pad(mixed, ((rim_width, rim_width), (wide_pad, wide_pad), (0, 0))), grad_depth_output)
    d_image = depth_conv(d_mixed, kernel_tall[::-1, ::-1], tall_pad, rim_width).astype(jnp.bfloat16)
    g_tall = kernel_grad(jnp.pad(image, ((tall_pad, tall_pad), (rim_width, rim_width), (0, 0))), d_mixed)
    grad_image = (cotangent.astype(jnp.float32) + lax.optimization_barrier(d_image).astype(jnp.float32)).astype(jnp.bfloat16)
    return (output, grad_image, (g_tall, g_wide, grad_norm_gain, g_shift, g_w_in, g_b_in, g_w_out, g_b_out))

def reference(image, cotangent, kernel_tall, kernel_wide, layer_norm_gain, layer_norm_bias, w_in, b_in, w_out, b_out):

    def per_region(pair):
        return one_region(pair[0], pair[1], kernel_tall, kernel_wide, layer_norm_gain, layer_norm_bias, w_in, b_in, w_out, b_out)
    output, grad_image, grads = lax.map(per_region, (image, cotangent))
    scale_multiplier = jnp.float32(CELLS) ** (-0.5)
    summed = [lax.optimization_barrier(jnp.sum(item, axis=0)) * scale_multiplier for item in grads]
    return (output, grad_image, summed[0], summed[1], summed[2], summed[3], summed[4], summed[5], summed[6], summed[7])
```

```python
import functools

import jax
import jax.numpy as jnp
from jax import lax
from jax.experimental import pallas as pl
from jax.experimental.pallas import tpu as pltpu
from jax.sharding import PartitionSpec as P

F32 = jnp.float32
BF16 = jnp.bfloat16
STRIPS = 32
ROWS = 6
COLS = 64
H = STRIPS * ROWS
C = 256
FF = 1024
LONG = 51
SHORT = 5
PAIRS = 4
BAND = 64
REACH = 32
MSG = ROWS * PAIRS
CELLS = ROWS * COLS
epsilon = 1e-06

PARAMS = pltpu.CompilerParams(vmem_limit_bytes=48 * 1024 * 1024)


def call(kernel, out_shape, scratch=()):
    return pl.pallas_call(
        kernel,
        out_shape=out_shape,
        scratch_shapes=list(scratch),
        compiler_params=PARAMS,
    )


def put_rows(block, k, scr):
    tall = jnp.concatenate([block[:, :128], block[:, 128:]], axis=0).T
    for cp in range(PAIRS):
        scr[pl.ds(k * PAIRS + cp, STRIPS, stride=MSG), :] = tall[cp * STRIPS : (cp + 1) * STRIPS]


def get_rows(scr, k):
    tall = jnp.concatenate(
        [scr[pl.ds(k * PAIRS + cp, STRIPS, stride=MSG), :] for cp in range(PAIRS)], axis=0
    ).T
    return jnp.concatenate([tall[:COLS], tall[COLS:]], axis=1)


def half_masks(shape):
    lane = lax.broadcasted_iota(jnp.int32, shape, len(shape) - 1)
    return lane, lane < COLS


def shifted(x, by):
    if by == 0:
        return x
    column = lax.broadcasted_iota(jnp.int32, x.shape, 1) % COLS + by
    return jnp.where((column >= 0) & (column < COLS), pltpu.roll(x, (-by) % 128, 1), 0.0)


def sloped(row, first_shift, count):
    eight = pltpu.roll(jnp.broadcast_to(row, (8, 128)), 0, 1, stride=1, stride_axis=0)
    return jnp.concatenate(
        [pltpu.roll(eight, (first_shift + i) % 128, 1) for i in range(0, count, 8)], axis=0
    )


def tall_matrix(taps_ref, q, c):
    return sloped(taps_ref[q * 8 + c : q * 8 + c + 1, :], REACH - (LONG - 1) // 2, BAND)


def wide_matrix(taps_ref, p, cp, in_block):
    first = -((LONG - 1) // 2)
    turned = jnp.concatenate(
        [
            sloped(taps_ref[n : n + 1, :], first + COLS * c2, COLS)
            for c2, n in enumerate((p * 8 + cp, p * 8 + 4 + cp))
        ],
        axis=0,
    )
    return jnp.where(in_block, turned, 0.0)


def block_mask():
    row = lax.broadcasted_iota(jnp.int32, (128, 128), 0)
    lane = lax.broadcasted_iota(jnp.int32, (128, 128), 1)
    return (row < COLS) == (lane < COLS)


def tall_conv(padded, taps_ref, cp, sign):
    matrix = jnp.concatenate(
        [
            jnp.concatenate([tall_matrix(taps_ref, q, c2 * 4 + cp) for c2 in range(2)], axis=1)
            for q in range(SHORT)
        ],
        axis=0,
    ).astype(BF16)
    _, first = half_masks((128, 128))
    zero = jnp.zeros((128, 128), BF16)
    sides = []
    for b in range(H // BAND):
        window = padded[b * BAND : b * BAND + 128]
        sides.append(
            jnp.concatenate([jnp.where(first, window, zero), jnp.where(first, zero, window)], axis=0)
        )
    product = jnp.dot(matrix, jnp.concatenate(sides, axis=1), preferred_element_type=F32)
    bands = []
    for b in range(H // BAND):
        total = None
        for q in range(SHORT):
            part = product[q * BAND : (q + 1) * BAND, b * 128 : (b + 1) * 128]
            part = shifted(part, sign * (q - 2))
            total = part if total is None else total + part
        bands.append(total)
    return jnp.concatenate(bands, axis=0)


def wide_conv(scr, taps_ref, cp, sign, in_block):
    source = jnp.concatenate(
        [scr[8 + sign * (p - 2) : 8 + sign * (p - 2) + H, :].astype(BF16) for p in range(SHORT)],
        axis=1,
    )
    matrix = jnp.concatenate(
        [wide_matrix(taps_ref, p, cp, in_block) for p in range(SHORT)], axis=0
    ).astype(BF16)
    return jnp.dot(source, matrix, preferred_element_type=F32)


def pad_rows(x):
    zero = jnp.zeros((REACH, 128), x.dtype)
    return jnp.concatenate([zero, x, zero], axis=0)


def pack_kernel(image_ref, out_ref, scr):
    for k in range(ROWS):
        put_rows(image_ref[k].astype(F32), k, scr)
    out_ref[...] = scr[...].astype(BF16)


def forward_kernel(image_ref, tall_ref, wide_ref, conv_ref, mixed_ref, scr, pad, out):
    scr[...] = image_ref[...].astype(F32)
    in_block = block_mask()
    pad[0:8, :] = jnp.zeros((8, 128), F32)
    pad[H + 8 : H + 16, :] = jnp.zeros((8, 128), F32)
    for cp in range(PAIRS):
        source = scr[pl.ds(cp, H, stride=PAIRS), :].astype(BF16)
        mixed = tall_conv(pad_rows(source), tall_ref, cp, 1).astype(BF16)
        mixed_ref[cp] = mixed
        pad[8 : H + 8, :] = mixed.astype(F32)
        out[pl.ds(cp, H, stride=PAIRS), :] = wide_conv(pad, wide_ref, cp, 1, in_block)
    conv_ref[...] = out[...].astype(BF16)


def diagonal(x, offset):
    total = None
    for i in range(0, x.shape[0], 8):
        part = pltpu.roll(x[i : i + 8], (offset - i) % 128, 1)
        total = part if total is None else total + part
    row = lax.broadcasted_iota(jnp.int32, (8, 128), 0)
    for bit in (1, 2, 4):
        total = jnp.where(row & bit != 0, pltpu.roll(total, 128 - bit, 1), total)
    return jnp.sum(total, axis=0, keepdims=True)


def backward_kernel(
    scale,
    d_conv_ref,
    image_ref,
    mixed_ref,
    tall_ref,
    wide_ref,
    small_ref,
    d_image_ref,
    grads_ref,
    d_scr,
    i_scr,
    d_pad,
    m_pad,
    out,
    g_scr,
):
    d_scr[...] = d_conv_ref[...].astype(F32)
    i_scr[...] = image_ref[...].astype(F32)
    in_block = block_mask()
    for ref in (d_pad, m_pad):
        ref[0:8, :] = jnp.zeros((8, 128), F32)
        ref[H + 8 : H + 16, :] = jnp.zeros((8, 128), F32)
    g_scr[40:48, :] = jnp.zeros((8, 128), F32)
    g_scr[48:64, :] = small_ref[...]
    lane, first = half_masks((1, 128))
    lane_b, first_b = half_masks((BAND, 128))
    for cp in range(PAIRS):
        d_conv = d_scr[pl.ds(cp, H, stride=PAIRS), :]
        d_pad[8 : H + 8, :] = d_conv
        m_pad[8 : H + 8, :] = mixed_ref[cp].astype(F32)
        source = pad_rows(i_scr[pl.ds(cp, H, stride=PAIRS), :].astype(BF16))
        d_mixed = wide_conv(d_pad, wide_ref, cp, -1, in_block).astype(BF16)
        moved = jnp.concatenate(
            [m_pad[6 + p : 6 + p + H, :].astype(BF16) for p in range(SHORT)], axis=1
        )
        corr = lax.dot_general(
            d_conv.astype(BF16), moved, (((0,), (0,)), ((), ())), preferred_element_type=F32
        )
        for p in range(SHORT):
            part = jnp.where(in_block, corr[:, p * 128 : (p + 1) * 128], 0.0)
            low = diagonal(part[:COLS], 32)
            high = diagonal(part[COLS:], 32)
            row = 20 + p * PAIRS + cp
            g_scr[row : row + 1, :] = jnp.where(first, low, high) * scale
        parts = []
        d_mixed_f = d_mixed.astype(F32)
        for q in range(SHORT):
            parts.append(shifted(d_mixed_f, 2 - q))
        left = []
        for c2 in range(2):
            for q in range(SHORT):
                bands = []
                for b in range(H // BAND):
                    band = parts[q][b * BAND : (b + 1) * BAND]
                    bands.append(jnp.where(first_b == (c2 == 0), band, 0.0))
                left.append(jnp.concatenate(bands, axis=1))
        left = jnp.concatenate(left, axis=0).astype(BF16)
        right = jnp.concatenate(
            [source[b * BAND : b * BAND + 128] for b in range(H // BAND)], axis=1
        )
        corr = lax.dot_general(
            left, right, (((1,), (1,)), ((), ())), preferred_element_type=F32
        )
        for q in range(SHORT):
            low = diagonal(corr[q * BAND : (q + 1) * BAND], 0)
            high = diagonal(corr[(SHORT + q) * BAND : (SHORT + q + 1) * BAND], COLS)
            row = q * PAIRS + cp
            g_scr[row : row + 1, :] = jnp.where(first, low, high) * scale
        out[pl.ds(cp, H, stride=PAIRS), :] = tall_conv(pad_rows(d_mixed), tall_ref, cp, -1)
    d_image_ref[...] = out[...].astype(BF16)
    grads_ref[...] = g_scr[...].astype(BF16)


def mlp_kernel(
    scale,
    conv_ref,
    image_ref,
    cot_ref,
    gain_ref,
    bias_ref,
    w_in_ref,
    b_in_ref,
    w_out_ref,
    b_out_ref,
    output_ref,
    d_conv_ref,
    grads_ref,
    small_ref,
    scr,
    xhat_scr,
    inv_scr,
    normed_scr,
    hidden_scr,
    d_pre_scr,
    out,
):
    scr[...] = conv_ref[...].astype(F32)
    gain, bias = gain_ref[...], bias_ref[...]
    sums = [jnp.zeros((1, C), F32), jnp.zeros((1, C), F32), jnp.zeros((1, C), F32)]
    g_b_in = jnp.zeros((1, FF), F32)
    step = 2
    for k in range(0, ROWS, step):
        rows = slice(k * COLS, (k + step) * COLS)
        conv = jnp.concatenate([get_rows(scr, k + i) for i in range(step)], axis=0)
        centred = conv - jnp.mean(conv, axis=1, keepdims=True)
        inverse = lax.rsqrt(jnp.mean(centred * centred, axis=1, keepdims=True) + epsilon)
        xhat = centred * inverse
        normed = (xhat * gain + bias).astype(BF16)
        normed_scr[rows, :] = normed
        pre_act = jnp.dot(normed, w_in_ref[...], preferred_element_type=F32) + b_in_ref[...]
        cdf = 0.5 * (1.0 + lax.erf(pre_act * 0.7071067811865476))
        hidden = (pre_act * cdf).astype(BF16)
        hidden_scr[rows, :] = hidden
        branch = jnp.dot(hidden, w_out_ref[...], preferred_element_type=F32) + b_out_ref[...]
        cot = cot_ref[rows, :]
        output_ref[rows, :] = (image_ref[rows, :].astype(F32) + branch).astype(BF16)
        d_hidden = lax.dot_general(
            cot, w_out_ref[...], (((1,), (1,)), ((), ())), preferred_element_type=F32
        )
        slope = cdf + pre_act * jnp.exp(-0.5 * pre_act * pre_act) * 0.3989422804014327
        d_pre = (d_hidden * slope).astype(BF16)
        d_pre_scr[rows, :] = d_pre
        g_b_in = g_b_in + jnp.sum(d_pre.astype(F32), axis=0, keepdims=True)
        d_norm = lax.dot_general(
            d_pre, w_in_ref[...], (((1,), (1,)), ((), ())), preferred_element_type=F32
        )
        sums[0] = sums[0] + jnp.sum(d_norm * xhat, axis=0, keepdims=True)
        sums[1] = sums[1] + jnp.sum(d_norm, axis=0, keepdims=True)
        sums[2] = sums[2] + jnp.sum(cot.astype(F32), axis=0, keepdims=True)
        g = d_norm * gain
        d_conv = inverse * (
            g
            - jnp.mean(g, axis=1, keepdims=True)
            - xhat * jnp.mean(g * xhat, axis=1, keepdims=True)
        )
        for i in range(step):
            put_rows(d_conv[i * COLS : (i + 1) * COLS], k + i, out)
    d_conv_ref[...] = out[...].astype(BF16)
    contract = (((0,), (0,)), ((), ()))
    grads_ref[0:C, :] = (
        lax.dot_general(normed_scr[...], d_pre_scr[...], contract, preferred_element_type=F32)
        * scale
    ).astype(BF16)
    grads_ref[C : 2 * C, :] = (
        lax.dot_general(cot_ref[...], hidden_scr[...], contract, preferred_element_type=F32)
        * scale
    ).astype(BF16)
    small_ref[...] = jnp.zeros((16, 128), F32)
    for i in range(FF // 128):
        small_ref[i : i + 1, :] = g_b_in[:, i * 128 : (i + 1) * 128] * scale
    for n in range(3):
        for i in range(2):
            row = 8 + 2 * n + i
            small_ref[row : row + 1, :] = sums[n][:, i * 128 : (i + 1) * 128] * scale


def strip_sum_kernel(parts_ref, grads_ref, out_ref):
    total = parts_ref[0].astype(F32)
    for i in range(1, STRIPS):
        total = total + parts_ref[i].astype(F32)
    for i in range(FF // 128):
        out_ref[i * 16 : (i + 1) * 16, :] = total[:, i * 128 : (i + 1) * 128].astype(BF16)
    out_ref[128:192, :] = grads_ref[...]


def slide_sum_kernel(parts_ref, out_ref):
    total = parts_ref[0].astype(F32)
    for i in range(1, parts_ref.shape[0]):
        total = total + parts_ref[i].astype(F32)
    out_ref[...] = total.astype(BF16)


SHARE = 192


def finish_kernel(
    parts_ref, tall_ref, wide_ref, small_ref, w_in_ref, w_out_ref, scr, turn
):
    for d in range(STRIPS):
        part = parts_ref[d].astype(F32)
        scr[d * SHARE : (d + 1) * SHARE, :] = part
        for i in range(FF // 128):
            piece = part[i * 16 : (i + 1) * 16]
            if d < 16:
                w_in_ref[d * 16 : (d + 1) * 16, i * 128 : (i + 1) * 128] = piece
            else:
                turn[(d - 16) * 16 : (d - 15) * 16, i * 128 : (i + 1) * 128] = piece
    for half in range(2):
        for i in range(FF // 128):
            w_out_ref[i * 128 : (i + 1) * 128, half * 128 : (half + 1) * 128] = turn[
                half * 128 : (half + 1) * 128, i * 128 : (i + 1) * 128
            ].T
    for q in range(SHORT):
        for start, ref in ((0, tall_ref), (20, wide_ref)):
            rows = jnp.concatenate(
                [
                    scr[pl.ds(128 + start + q * PAIRS + cp, STRIPS, stride=SHARE), :]
                    for cp in range(PAIRS)
                ],
                axis=0,
            ).T
            ref[q] = jnp.concatenate([rows[:COLS], rows[COLS:]], axis=1)
    total = scr[176:192, :]
    for d in range(1, STRIPS):
        total = total + scr[d * SHARE + 176 : d * SHARE + 192, :]
    small_ref[...] = total


def residual_kernel(d_image_ref, cot_ref, out_ref, scr):
    scr[...] = d_image_ref[...].astype(F32)
    for k in range(ROWS):
        out_ref[k] = (cot_ref[k].astype(F32) + get_rows(scr, k)).astype(BF16)


def exchange(x, axis):
    return lax.all_to_all(x, axis, 0, 0, tiled=True)


def messages(x):
    return exchange(x.reshape(STRIPS, MSG, 128), "strip").reshape(STRIPS * MSG, 128)


def shape(dims, dtype):
    return jax.ShapeDtypeStruct(dims, dtype)


def local(
    image,
    cotangent,
    kernel_tall,
    kernel_wide,
    layer_norm_gain,
    layer_norm_bias,
    w_in,
    b_in,
    w_out,
    b_out,
):
    source = image[0]
    upstream = cotangent[0]
    slides = lax.axis_size("slide")
    scale = float(CELLS * slides * STRIPS) ** (-0.5)
    packed_f = pltpu.VMEM((STRIPS * MSG, 128), F32)
    packed_b = shape((STRIPS * MSG, 128), BF16)
    edge = pltpu.VMEM((H + 16, 128), F32)

    image_msg = call(pack_kernel, packed_b, [packed_f])(source)
    me = lax.axis_index("strip")
    own = jnp.arange(8)[:, None] * STRIPS + me == jnp.arange(C)[None, :]
    own = own.astype(BF16)

    def taps(kernel, spec):
        picked = jnp.einsum(spec, kernel, own, preferred_element_type=F32)
        picked = picked.reshape(SHORT * 8, LONG)
        pad = ((0, 0), (0, 128 - LONG))
        return jnp.pad(picked, pad), jnp.pad(picked[:, ::-1], pad)

    tall, tall_flipped = taps(kernel_tall, "pqc,kc->qkp")
    wide, wide_flipped = taps(kernel_wide, "pqc,kc->pkq")

    image_ch = messages(image_msg)
    conv_ch, mixed = call(
        forward_kernel,
        (packed_b, shape((PAIRS, H, 128), BF16)),
        [packed_f, edge, packed_f],
    )(image_ch, tall, wide_flipped)
    conv = messages(conv_ch)
    output, d_conv_msg, grads, small = call(
        functools.partial(mlp_kernel, scale),
        (
            shape((CELLS, C), BF16),
            packed_b,
            shape((2 * C, FF), BF16),
            shape((16, 128), F32),
        ),
        [
            packed_f,
            pltpu.VMEM((8, 128), F32),
            pltpu.VMEM((8, 128), F32),
            pltpu.VMEM((CELLS, C), BF16),
            pltpu.VMEM((CELLS, FF), BF16),
            pltpu.VMEM((CELLS, FF), BF16),
            packed_f,
        ],
    )(
        conv,
        source.reshape(CELLS, C),
        upstream.reshape(CELLS, C),
        layer_norm_gain[None],
        layer_norm_bias[None],
        w_in,
        b_in[None],
        w_out,
        b_out[None],
    )
    d_conv = messages(d_conv_msg)
    grad_parts = exchange(grads.reshape(STRIPS, 16, FF), "strip")
    d_image_msg, own_grads = call(
        functools.partial(backward_kernel, scale),
        (packed_b, shape((64, 128), BF16)),
        [packed_f, packed_f, edge, edge, packed_f, pltpu.VMEM((64, 128), F32)],
    )(d_conv, image_ch, mixed, tall_flipped, wide, small)
    d_image = messages(d_image_msg)
    share = call(strip_sum_kernel, shape((SHARE, 128), BF16))(grad_parts, own_grads)
    shares = exchange(jnp.broadcast_to(share[None], (slides, SHARE, 128)), "slide")
    total = call(slide_sum_kernel, shape((SHARE, 128), BF16))(shares)
    totals = exchange(jnp.broadcast_to(total[None], (STRIPS, SHARE, 128)), "strip")
    long_tall, long_wide, small_sum, g_w_in, g_w_out = call(
        finish_kernel,
        (
            shape((SHORT, COLS, C), F32),
            shape((SHORT, COLS, C), F32),
            shape((16, 128), F32),
            shape((C, FF), F32),
            shape((FF, C), F32),
        ),
        [pltpu.VMEM((STRIPS * SHARE, 128), F32), pltpu.VMEM((C, FF), F32)],
    )(totals)
    grad_image = call(residual_kernel, shape((ROWS, COLS, C), BF16), [packed_f])(d_image, upstream)
    g_tall = jnp.transpose(long_tall[:, 7 : 7 + LONG], (1, 0, 2))
    g_wide = long_wide[:, 7 : 7 + LONG]
    g_b_in = small_sum[:8].reshape(FF)
    g_gain, g_shift, g_b_out = (small_sum[8 + 2 * i : 10 + 2 * i].reshape(C) for i in range(3))
    return (
        output.reshape(image.shape),
        grad_image[None],
        g_tall,
        g_wide,
        g_gain,
        g_shift,
        g_w_in,
        g_b_in,
        g_w_out,
        g_b_out,
    )


def solution(mesh):
    cells = P("slide", "strip", None, None)
    return jax.shard_map(
        local,
        mesh=mesh,
        in_specs=(cells, cells) + (P(),) * 8,
        out_specs=(cells, cells) + (P(),) * 8,
        check_vma=False,
    )
```

```python
import functools

import jax
import jax.numpy as jnp
from jax import lax
from jax.experimental import pallas as pl
from jax.experimental.pallas import tpu as pltpu
from jax.sharding import PartitionSpec as P

F32 = jnp.float32
BF16 = jnp.bfloat16
CORES = 2
CHIPS = 16
STRIPS = CORES * CHIPS
ROWS = 6
COLS = 64
H = STRIPS * ROWS
C = 256
FF = 1024
LONG = 51
SHORT = 5
PAIRS = 4
BAND = 64
REACH = 32
MSG = ROWS * PAIRS
CELLS = ROWS * COLS
DATA = CORES * MSG
GRADS = C * FF // 128
OWN = GRADS // CHIPS
SHARE = OWN + 64
LAST = DATA + SHARE
epsilon = 1e-06

PARAMS = pltpu.CompilerParams(vmem_limit_bytes=48 * 1024 * 1024)


def call(kernel, out_shape, scratch=(), scalars=0):
    extra = {}
    if scalars:
        vmem = pl.BlockSpec(memory_space=pltpu.VMEM)
        smem = pl.BlockSpec(memory_space=pltpu.SMEM)
        extra["in_specs"] = [smem] + [vmem] * scalars
    return pl.pallas_call(
        kernel,
        out_shape=out_shape,
        **extra,
        scratch_shapes=list(scratch),
        compiler_params=PARAMS,
    )


def turned_rows(block):
    return jnp.concatenate([block[:, :128], block[:, 128:]], axis=0).T


def put_by_strip(block, k, scr):
    rows = turned_rows(block)
    for cp in range(PAIRS):
        for core in range(CORES):
            first = cp * STRIPS + core * CHIPS
            at = pl.ds(core * MSG + k * PAIRS + cp, CHIPS, stride=CORES * MSG)
            scr[at, :] = rows[first : first + CHIPS]


def put_by_core(block, k, scr):
    rows = turned_rows(block)
    for cp in range(PAIRS):
        scr[pl.ds(k * PAIRS + cp, STRIPS, stride=MSG), :] = rows[cp * STRIPS : (cp + 1) * STRIPS]


def untwisted(parts):
    rows = jnp.concatenate(parts, axis=0).T
    return jnp.concatenate([rows[:COLS], rows[COLS:]], axis=1)


def half_masks(shape):
    lane = lax.broadcasted_iota(jnp.int32, shape, len(shape) - 1)
    return lane, lane < COLS


def shifted(x, by):
    if by == 0:
        return x
    column = lax.broadcasted_iota(jnp.int32, x.shape, 1) % COLS + by
    return jnp.where((column >= 0) & (column < COLS), pltpu.roll(x, (-by) % 128, 1), 0.0)


def sloped(row, first_shift, count):
    eight = pltpu.roll(jnp.broadcast_to(row, (8, 128)), 0, 1, stride=1, stride_axis=0)
    return jnp.concatenate(
        [pltpu.roll(eight, (first_shift + i) % 128, 1) for i in range(0, count, 8)], axis=0
    )


def tall_matrix(taps_ref, q, c):
    return sloped(taps_ref[q * 8 + c : q * 8 + c + 1, :], REACH - (LONG - 1) // 2, BAND)


def wide_matrix(taps_ref, p, cp, in_block):
    first = -((LONG - 1) // 2)
    turned = jnp.concatenate(
        [
            sloped(taps_ref[n : n + 1, :], first + COLS * c2, COLS)
            for c2, n in enumerate((p * 8 + cp, p * 8 + 4 + cp))
        ],
        axis=0,
    )
    return jnp.where(in_block, turned, 0.0)


def block_mask():
    row = lax.broadcasted_iota(jnp.int32, (128, 128), 0)
    lane = lax.broadcasted_iota(jnp.int32, (128, 128), 1)
    return (row < COLS) == (lane < COLS)


def tall_conv(padded, taps_ref, cp, sign):
    matrix = jnp.concatenate(
        [
            jnp.concatenate([tall_matrix(taps_ref, q, c2 * 4 + cp) for c2 in range(2)], axis=1)
            for q in range(SHORT)
        ],
        axis=0,
    ).astype(BF16)
    _, first = half_masks((128, 128))
    zero = jnp.zeros((128, 128), BF16)
    sides = []
    for b in range(H // BAND):
        window = padded[b * BAND : b * BAND + 128]
        sides.append(
            jnp.concatenate([jnp.where(first, window, zero), jnp.where(first, zero, window)], axis=0)
        )
    product = jnp.dot(matrix, jnp.concatenate(sides, axis=1), preferred_element_type=F32)
    bands = []
    for b in range(H // BAND):
        total = None
        for q in range(SHORT):
            part = product[q * BAND : (q + 1) * BAND, b * 128 : (b + 1) * 128]
            part = shifted(part, sign * (q - 2))
            total = part if total is None else total + part
        bands.append(total)
    return jnp.concatenate(bands, axis=0)


def wide_conv(scr, taps_ref, cp, sign, in_block):
    source = jnp.concatenate(
        [scr[8 + sign * (p - 2) : 8 + sign * (p - 2) + H, :].astype(BF16) for p in range(SHORT)],
        axis=1,
    )
    matrix = jnp.concatenate(
        [wide_matrix(taps_ref, p, cp, in_block) for p in range(SHORT)], axis=0
    ).astype(BF16)
    return jnp.dot(source, matrix, preferred_element_type=F32)


def pad_rows(x):
    zero = jnp.zeros((REACH, 128), x.dtype)
    return jnp.concatenate([zero, x, zero], axis=0)


def pack_kernel(image_ref, out_ref, scr):
    for k in range(ROWS):
        put_by_strip(image_ref[k].astype(F32), k, scr)
    out_ref[...] = scr[...].astype(BF16)


def forward_kernel(image_ref, tall_ref, wide_ref, conv_ref, mixed_ref, scr, pad, out):
    scr[...] = image_ref[...].astype(F32)
    in_block = block_mask()
    pad[0:8, :] = jnp.zeros((8, 128), F32)
    pad[H + 8 : H + 16, :] = jnp.zeros((8, 128), F32)
    for cp in range(PAIRS):
        source = scr[pl.ds(cp, H, stride=PAIRS), :].astype(BF16)
        mixed = tall_conv(pad_rows(source), tall_ref, cp, 1).astype(BF16)
        mixed_ref[cp] = mixed
        pad[8 : H + 8, :] = mixed.astype(F32)
        out[pl.ds(cp, H, stride=PAIRS), :] = wide_conv(pad, wide_ref, cp, 1, in_block)
    conv_ref[...] = out[...].astype(BF16)


def diagonal(x, offset):
    total = None
    for i in range(0, x.shape[0], 8):
        part = pltpu.roll(x[i : i + 8], (offset - i) % 128, 1)
        total = part if total is None else total + part
    row = lax.broadcasted_iota(jnp.int32, (8, 128), 0)
    for bit in (1, 2, 4):
        total = jnp.where(row & bit != 0, pltpu.roll(total, 128 - bit, 1), total)
    return jnp.sum(total, axis=0, keepdims=True)


def backward_kernel(
    scale,
    parts_ref,
    image_ref,
    mixed_ref,
    tall_ref,
    wide_ref,
    small_ref,
    d_image_ref,
    share_ref,
    d_scr,
    i_scr,
    d_pad,
    m_pad,
    out,
    g_scr,
):
    total = None
    for i in range(CHIPS):
        part = parts_ref[i].astype(F32)
        d_scr[i * DATA : (i + 1) * DATA, :] = part[:DATA]
        total = part[DATA:] if total is None else total + part[DATA:]
    share_ref[0:OWN, :] = total.astype(BF16)
    i_scr[...] = image_ref[...].astype(F32)
    in_block = block_mask()
    for ref in (d_pad, m_pad):
        ref[0:8, :] = jnp.zeros((8, 128), F32)
        ref[H + 8 : H + 16, :] = jnp.zeros((8, 128), F32)
    g_scr[40:48, :] = jnp.zeros((8, 128), F32)
    g_scr[48:64, :] = small_ref[...]
    lane, first = half_masks((1, 128))
    lane_b, first_b = half_masks((BAND, 128))
    for cp in range(PAIRS):
        d_conv = d_scr[pl.ds(cp, H, stride=PAIRS), :]
        d_pad[8 : H + 8, :] = d_conv
        m_pad[8 : H + 8, :] = mixed_ref[cp].astype(F32)
        source = pad_rows(i_scr[pl.ds(cp, H, stride=PAIRS), :].astype(BF16))
        d_mixed = wide_conv(d_pad, wide_ref, cp, -1, in_block).astype(BF16)
        moved = jnp.concatenate(
            [m_pad[6 + p : 6 + p + H, :].astype(BF16) for p in range(SHORT)], axis=1
        )
        corr = lax.dot_general(
            d_conv.astype(BF16), moved, (((0,), (0,)), ((), ())), preferred_element_type=F32
        )
        for p in range(SHORT):
            part = jnp.where(in_block, corr[:, p * 128 : (p + 1) * 128], 0.0)
            low = diagonal(part[:COLS], 32)
            high = diagonal(part[COLS:], 32)
            row = 20 + p * PAIRS + cp
            g_scr[row : row + 1, :] = jnp.where(first, low, high) * scale
        parts = []
        d_mixed_f = d_mixed.astype(F32)
        for q in range(SHORT):
            parts.append(shifted(d_mixed_f, 2 - q))
        left = []
        for c2 in range(2):
            for q in range(SHORT):
                bands = []
                for b in range(H // BAND):
                    band = parts[q][b * BAND : (b + 1) * BAND]
                    bands.append(jnp.where(first_b == (c2 == 0), band, 0.0))
                left.append(jnp.concatenate(bands, axis=1))
        left = jnp.concatenate(left, axis=0).astype(BF16)
        right = jnp.concatenate(
            [source[b * BAND : b * BAND + 128] for b in range(H // BAND)], axis=1
        )
        corr = lax.dot_general(
            left, right, (((1,), (1,)), ((), ())), preferred_element_type=F32
        )
        for q in range(SHORT):
            low = diagonal(corr[q * BAND : (q + 1) * BAND], 0)
            high = diagonal(corr[(SHORT + q) * BAND : (SHORT + q + 1) * BAND], COLS)
            row = q * PAIRS + cp
            g_scr[row : row + 1, :] = jnp.where(first, low, high) * scale
        out[pl.ds(cp, H, stride=PAIRS), :] = tall_conv(pad_rows(d_mixed), tall_ref, cp, -1)
    d_image_ref[...] = out[...].astype(BF16)
    share_ref[OWN:SHARE, :] = g_scr[...].astype(BF16)


def mlp_kernel(
    scale,
    core_ref,
    conv_ref,
    image_ref,
    cot_ref,
    gain_ref,
    bias_ref,
    w_in_ref,
    b_in_ref,
    w_out_ref,
    b_out_ref,
    output_ref,
    theirs_ref,
    mine_ref,
    left_ref,
    right_ref,
    small_ref,
    scr,
    out,
):
    core = core_ref[0]
    scr[...] = conv_ref[...].astype(F32)
    gain, bias = gain_ref[...], bias_ref[...]
    sums = [jnp.zeros((1, C), F32), jnp.zeros((1, C), F32), jnp.zeros((1, C), F32)]
    g_b_in = jnp.zeros((1, FF), F32)
    step = 2
    for k in range(0, ROWS, step):
        rows = slice(k * COLS, (k + step) * COLS)
        conv = jnp.concatenate(
            [
                untwisted(
                    [
                        scr[pl.ds(c * MSG + i * PAIRS + cp, CHIPS, stride=CORES * MSG), :]
                        for cp in range(PAIRS)
                        for c in range(CORES)
                    ]
                )
                for i in range(k, k + step)
            ],
            axis=0,
        )
        centred = conv - jnp.mean(conv, axis=1, keepdims=True)
        inverse = lax.rsqrt(jnp.mean(centred * centred, axis=1, keepdims=True) + epsilon)
        xhat = centred * inverse
        normed = (xhat * gain + bias).astype(BF16)
        left_ref[0, rows, :] = normed
        pre_act = jnp.dot(normed, w_in_ref[...], preferred_element_type=F32) + b_in_ref[...]
        cdf = 0.5 * (1.0 + lax.erf(pre_act * 0.7071067811865476))
        hidden = (pre_act * cdf).astype(BF16)
        right_ref[1, rows, :] = hidden
        branch = jnp.dot(hidden, w_out_ref[...], preferred_element_type=F32) + b_out_ref[...]
        cot = cot_ref[rows, :]
        left_ref[1, rows, :] = cot
        output_ref[rows, :] = (image_ref[rows, :].astype(F32) + branch).astype(BF16)
        d_hidden = lax.dot_general(
            cot, w_out_ref[...], (((1,), (1,)), ((), ())), preferred_element_type=F32
        )
        slope = cdf + pre_act * jnp.exp(-0.5 * pre_act * pre_act) * 0.3989422804014327
        d_pre = (d_hidden * slope).astype(BF16)
        right_ref[0, rows, :] = d_pre
        g_b_in = g_b_in + jnp.sum(d_pre.astype(F32), axis=0, keepdims=True)
        d_norm = lax.dot_general(
            d_pre, w_in_ref[...], (((1,), (1,)), ((), ())), preferred_element_type=F32
        )
        sums[0] = sums[0] + jnp.sum(d_norm * xhat, axis=0, keepdims=True)
        sums[1] = sums[1] + jnp.sum(d_norm, axis=0, keepdims=True)
        sums[2] = sums[2] + jnp.sum(cot.astype(F32), axis=0, keepdims=True)
        g = d_norm * gain
        d_conv = inverse * (
            g
            - jnp.mean(g, axis=1, keepdims=True)
            - xhat * jnp.mean(g * xhat, axis=1, keepdims=True)
        )
        for i in range(step):
            put_by_core(d_conv[i * COLS : (i + 1) * COLS], k + i, out)
    half = CHIPS * MSG
    theirs_ref[GRADS : GRADS + half, :] = out[pl.ds((1 - core) * half, half), :].astype(BF16)
    mine_ref[...] = out[pl.ds(core * half, half), :].astype(BF16)
    weight_grads(scale, left_ref, right_ref, 1 - core, theirs_ref)
    small_ref[...] = jnp.zeros((16, 128), F32)
    for i in range(FF // 128):
        small_ref[i : i + 1, :] = g_b_in[:, i * 128 : (i + 1) * 128] * scale
    for n in range(3):
        for i in range(2):
            row = 8 + 2 * n + i
            small_ref[row : row + 1, :] = sums[n][:, i * 128 : (i + 1) * 128] * scale


def weight_grads(scale, left_ref, right_ref, which, out_ref):
    grads = lax.dot_general(
        left_ref[which], right_ref[which], (((0,), (0,)), ((), ())), preferred_element_type=F32
    )
    grads = (grads * scale).astype(out_ref.dtype)
    for i in range(CHIPS):
        for j in range(FF // 128):
            at = (i * (FF // 128) + j) * 16
            out_ref[at : at + 16, :] = grads[i * 16 : (i + 1) * 16, j * 128 : (j + 1) * 128]


def own_grads_kernel(scale, core_ref, left_ref, right_ref, out_ref):
    weight_grads(scale, left_ref, right_ref, core_ref[0], out_ref)


def merge_kernel(core_ref, mine_ref, grads_ref, got_ref, out_ref):
    half = CHIPS * MSG
    mine = mine_ref[...].astype(F32)
    got = got_ref[GRADS : GRADS + half, :].astype(F32)
    low = core_ref[0] == 0
    one, two = jnp.where(low, mine, got), jnp.where(low, got, mine)
    for i in range(CHIPS):
        rows = slice(i * MSG, (i + 1) * MSG)
        out_ref[i, 0:DATA, :] = jnp.concatenate([one[rows], two[rows]], axis=0).astype(BF16)
        rows = slice(i * OWN, (i + 1) * OWN)
        out_ref[i, DATA : DATA + OWN, :] = (grads_ref[rows, :] + got_ref[rows, :].astype(F32)).astype(BF16)


def pair_sum_kernel(mine_ref, got_ref, out_ref):
    total = (mine_ref[...].astype(F32) + got_ref[...].astype(F32)).astype(BF16)
    for i in range(out_ref.shape[0]):
        out_ref[i] = total


def gather_kernel(parts_ref, d_image_ref, out_ref):
    total = parts_ref[0].astype(F32)
    for i in range(1, parts_ref.shape[0]):
        total = total + parts_ref[i].astype(F32)
    total = total.astype(BF16)
    for i in range(CHIPS):
        out_ref[i, 0:DATA, :] = d_image_ref[i * DATA : (i + 1) * DATA, :]
        out_ref[i, DATA : DATA + SHARE, :] = total


def finish_kernel(
    core_ref,
    mine_ref,
    got_ref,
    cot_ref,
    out_ref,
    tall_ref,
    wide_ref,
    gain_ref,
    shift_ref,
    w_in_ref,
    b_in_ref,
    w_out_ref,
    b_out_ref,
    scr,
    turn,
):
    core = core_ref[0]
    for i in range(CHIPS):
        rows = slice(i * LAST, (i + 1) * LAST)
        scr[core, rows, :] = mine_ref[i].astype(F32)
        scr[1 - core, rows, :] = got_ref[i].astype(F32)
    for k in range(ROWS):
        d_image = untwisted(
            [
                scr.at[c][pl.ds(core * MSG + k * PAIRS + cp, CHIPS, stride=LAST), :]
                for cp in range(PAIRS)
                for c in range(CORES)
            ]
        )
        out_ref[k] = (cot_ref[k].astype(F32) + d_image).astype(BF16)
    for i in range(CHIPS):
        for j in range(FF // 128):
            at = i * LAST + DATA + j * 16
            w_in_ref[i * 16 : (i + 1) * 16, j * 128 : (j + 1) * 128] = scr[0, at : at + 16, :]
            turn[i * 16 : (i + 1) * 16, j * 128 : (j + 1) * 128] = scr[1, at : at + 16, :]
    for half in range(2):
        for j in range(FF // 128):
            w_out_ref[j * 128 : (j + 1) * 128, half * 128 : (half + 1) * 128] = turn[
                half * 128 : (half + 1) * 128, j * 128 : (j + 1) * 128
            ].T
    for q in range(SHORT):
        for start, is_tall in ((0, True), (20, False)):
            taps = untwisted(
                [
                    scr.at[c][pl.ds(DATA + OWN + start + q * PAIRS + cp, CHIPS, stride=LAST), :]
                    for cp in range(PAIRS)
                    for c in range(CORES)
                ]
            )[7 : 7 + LONG]
            if is_tall:
                tall_ref[:, q, :] = taps
            else:
                wide_ref[q] = taps
    total = None
    for c in range(CORES):
        for i in range(CHIPS):
            at = i * LAST + LAST - 16
            part = scr[c, at : at + 16, :]
            total = part if total is None else total + part
    for i in range(FF // 128):
        b_in_ref[:, i * 128 : (i + 1) * 128] = total[i : i + 1]
    for n, ref in enumerate((gain_ref, shift_ref, b_out_ref)):
        for i in range(2):
            ref[:, i * 128 : (i + 1) * 128] = total[8 + 2 * n + i : 9 + 2 * n + i]


def messages(x):
    x = lax.all_to_all(x.reshape(STRIPS, MSG, 128), "strip", 0, 0, tiled=True)
    return x.reshape(STRIPS * MSG, 128)


def between_chips(x):
    groups = [[CORES * i + c for i in range(CHIPS)] for c in range(CORES)]
    return lax.all_to_all(x, "strip", 0, 0, axis_index_groups=groups, tiled=True)


def between_cores(x):
    return lax.ppermute(x, "strip", [(i, i ^ 1) for i in range(STRIPS)])


def shape(dims, dtype):
    return jax.ShapeDtypeStruct(dims, dtype)


def local(
    image,
    cotangent,
    kernel_tall,
    kernel_wide,
    layer_norm_gain,
    layer_norm_bias,
    w_in,
    b_in,
    w_out,
    b_out,
):
    source = image[0]
    upstream = cotangent[0]
    slides = lax.axis_size("slide")
    scale = float(CELLS * slides * STRIPS) ** (-0.5)
    packed_f = pltpu.VMEM((STRIPS * MSG, 128), F32)
    packed_b = shape((STRIPS * MSG, 128), BF16)
    edge = pltpu.VMEM((H + 16, 128), F32)

    image_msg = call(pack_kernel, packed_b, [packed_f])(source)
    me = lax.axis_index("strip")
    core = (me % CORES).reshape(1)
    me = (me % CORES) * CHIPS + me // CORES
    own = jnp.arange(8)[:, None] * STRIPS + me == jnp.arange(C)[None, :]
    own = own.astype(BF16)

    def taps(kernel, spec):
        picked = jnp.einsum(spec, kernel, own, preferred_element_type=F32)
        picked = picked.reshape(SHORT * 8, LONG)
        pad = ((0, 0), (0, 128 - LONG))
        return jnp.pad(picked, pad), jnp.pad(picked[:, ::-1], pad)

    tall, tall_flipped = taps(kernel_tall, "pqc,kc->qkp")
    wide, wide_flipped = taps(kernel_wide, "pqc,kc->pkq")

    image_ch = messages(image_msg)
    conv_ch, mixed = call(
        forward_kernel,
        (packed_b, shape((PAIRS, H, 128), BF16)),
        [packed_f, edge, packed_f],
    )(image_ch, tall, wide_flipped)
    conv = messages(conv_ch)
    output, theirs, mine, left, right, small = call(
        functools.partial(mlp_kernel, scale),
        (
            shape((CELLS, C), BF16),
            shape((GRADS + CHIPS * MSG, 128), BF16),
            shape((CHIPS * MSG, 128), BF16),
            shape((2, CELLS, C), BF16),
            shape((2, CELLS, FF), BF16),
            shape((16, 128), F32),
        ),
        [packed_f, packed_f],
        9,
    )(
        core,
        conv,
        source.reshape(CELLS, C),
        upstream.reshape(CELLS, C),
        layer_norm_gain[None],
        layer_norm_bias[None],
        w_in,
        b_in[None],
        w_out,
        b_out[None],
    )
    got = between_cores(theirs)
    chip_grads = call(
        functools.partial(own_grads_kernel, scale), shape((GRADS, 128), F32), (), 2
    )(core, left, right)
    merged = call(merge_kernel, shape((CHIPS, DATA + OWN, 128), BF16), (), 3)(
        core, mine, chip_grads, got
    )
    d_image_msg, share = call(
        functools.partial(backward_kernel, scale),
        (packed_b, shape((SHARE, 128), BF16)),
        [packed_f, packed_f, edge, edge, packed_f, pltpu.VMEM((64, 128), F32)],
    )(between_chips(merged), image_ch, mixed, tall_flipped, wide, small)
    got = lax.ppermute(share, "slide", [(i, i ^ 1) for i in range(slides)])
    half = slides // 2
    copies = call(pair_sum_kernel, shape((half, SHARE, 128), BF16))(share, got)
    groups = [[2 * i + j for i in range(half)] for j in range(2)]
    parts = lax.all_to_all(copies, "slide", 0, 0, axis_index_groups=groups, tiled=True)
    last = call(gather_kernel, shape((CHIPS, LAST, 128), BF16))(parts, d_image_msg)
    last = between_chips(last)
    got = between_cores(last)
    grad_image, g_tall, g_wide, g_gain, g_shift, g_w_in, g_b_in, g_w_out, g_b_out = call(
        finish_kernel,
        (
            shape((ROWS, COLS, C), BF16),
            shape((LONG, SHORT, C), F32),
            shape((SHORT, LONG, C), F32),
            shape((1, C), F32),
            shape((1, C), F32),
            shape((C, FF), F32),
            shape((1, FF), F32),
            shape((FF, C), F32),
            shape((1, C), F32),
        ),
        [pltpu.VMEM((CORES, CHIPS * LAST, 128), F32), pltpu.VMEM((C, FF), F32)],
        3,
    )(core, last, got, upstream)
    return (
        output.reshape(image.shape),
        grad_image[None],
        g_tall,
        g_wide,
        g_gain[0],
        g_shift[0],
        g_w_in,
        g_b_in[0],
        g_w_out,
        g_b_out[0],
    )


def solution(mesh):
    cells = P("slide", "strip", None, None)
    return jax.shard_map(
        local,
        mesh=mesh,
        in_specs=(cells, cells) + (P(),) * 8,
        out_specs=(cells, cells) + (P(),) * 8,
        check_vma=False,
    )
```

```python
import functools

import jax
import jax.numpy as jnp
from jax import lax
from jax.experimental import pallas as pl
from jax.experimental.pallas import tpu as pltpu
from jax.sharding import PartitionSpec as P

F32 = jnp.float32
BF16 = jnp.bfloat16
CORES = 2
CHIPS = 16
STRIPS = CORES * CHIPS
ROWS = 6
COLS = 64
H = STRIPS * ROWS
C = 256
FF = 1024
LONG = 51
SHORT = 5
PAIRS = 4
BAND = 64
REACH = 32
MSG = ROWS * PAIRS
CELLS = ROWS * COLS
DATA = CORES * MSG
GRADS = C * FF // 128
OWN = GRADS // CHIPS
SHARE = OWN + 48
LAST = DATA + SHARE
epsilon = 1e-06

PARAMS = pltpu.CompilerParams(vmem_limit_bytes=48 * 1024 * 1024)


VMEM = pl.BlockSpec(memory_space=pltpu.VMEM)
SMEM = pl.BlockSpec(memory_space=pltpu.SMEM)
ANY = pl.BlockSpec(memory_space=pl.ANY)


def call(kernel, out_shape, scratch=(), in_specs=None, out_specs=None):
    specs = {}
    if in_specs is not None:
        specs["in_specs"] = in_specs
    if out_specs is not None:
        specs["out_specs"] = out_specs
    return pl.pallas_call(
        kernel,
        out_shape=out_shape,
        scratch_shapes=list(scratch),
        compiler_params=PARAMS,
        **specs,
    )


def turned_rows(block):
    return jnp.concatenate([block[:, :128], block[:, 128:]], axis=0).T


def put_by_strip(block, k, scr):
    rows = turned_rows(block)
    for cp in range(PAIRS):
        for core in range(CORES):
            first = cp * STRIPS + core * CHIPS
            at = pl.ds(core * MSG + k * PAIRS + cp, CHIPS, stride=CORES * MSG)
            scr[at, :] = rows[first : first + CHIPS]


def put_by_core(block, k, scr):
    rows = turned_rows(block)
    for cp in range(PAIRS):
        scr[pl.ds(k * PAIRS + cp, STRIPS, stride=MSG), :] = rows[cp * STRIPS : (cp + 1) * STRIPS]


def untwisted(parts):
    rows = jnp.concatenate(parts, axis=0).T
    return jnp.concatenate([rows[:COLS], rows[COLS:]], axis=1)


def half_masks(shape):
    lane = lax.broadcasted_iota(jnp.int32, shape, len(shape) - 1)
    return lane, lane < COLS


def shifted(x, by):
    if by == 0:
        return x
    column = lax.broadcasted_iota(jnp.int32, x.shape, 1) % COLS + by
    return jnp.where((column >= 0) & (column < COLS), pltpu.roll(x, (-by) % 128, 1), 0.0)


def sloped(row, first_shift, count):
    eight = pltpu.roll(jnp.broadcast_to(row, (8, 128)), 0, 1, stride=1, stride_axis=0)
    return jnp.concatenate(
        [pltpu.roll(eight, (first_shift + i) % 128, 1) for i in range(0, count, 8)], axis=0
    )


def tall_matrix(taps_ref, q, c):
    return sloped(taps_ref[q * 8 + c : q * 8 + c + 1, :], REACH - (LONG - 1) // 2, BAND)


def wide_matrix(taps_ref, p, cp, in_block):
    first = -((LONG - 1) // 2)
    turned = jnp.concatenate(
        [
            sloped(taps_ref[n : n + 1, :], first + COLS * c2, COLS)
            for c2, n in enumerate((p * 8 + cp, p * 8 + 4 + cp))
        ],
        axis=0,
    )
    return jnp.where(in_block, turned, 0.0)


def block_mask():
    row = lax.broadcasted_iota(jnp.int32, (128, 128), 0)
    lane = lax.broadcasted_iota(jnp.int32, (128, 128), 1)
    return (row < COLS) == (lane < COLS)


def tall_conv(padded, matrix, sign):
    _, first = half_masks((128, 128))
    zero = jnp.zeros((128, 128), BF16)
    sides = []
    for b in range(H // BAND):
        window = padded[b * BAND : b * BAND + 128]
        sides.append(
            jnp.concatenate([jnp.where(first, window, zero), jnp.where(first, zero, window)], axis=0)
        )
    product = jnp.dot(matrix, jnp.concatenate(sides, axis=1), preferred_element_type=F32)
    bands = []
    for b in range(H // BAND):
        total = None
        for q in range(SHORT):
            part = product[q * BAND : (q + 1) * BAND, b * 128 : (b + 1) * 128]
            part = shifted(part, sign * (q - 2))
            total = part if total is None else total + part
        bands.append(total)
    return jnp.concatenate(bands, axis=0)


def moved_rows(scr, sign):
    return jnp.concatenate(
        [scr[8 + sign * (p - 2) : 8 + sign * (p - 2) + H, :].astype(BF16) for p in range(SHORT)],
        axis=1,
    )


def matrix_kernel(tall_ref, wide_ref, tall_out, wide_out):
    in_block = block_mask()
    for cp in range(PAIRS):
        for q in range(SHORT):
            rows = slice(q * BAND, (q + 1) * BAND)
            for c2 in range(2):
                lanes = slice(c2 * 128, (c2 + 1) * 128)
                tall_out[cp, rows, lanes] = tall_matrix(tall_ref, q, c2 * 4 + cp).astype(BF16)
            wide_out[cp, q * 128 : (q + 1) * 128, :] = wide_matrix(
                wide_ref, q, cp, in_block
            ).astype(BF16)


def pad_rows(x):
    zero = jnp.zeros((REACH, 128), x.dtype)
    return jnp.concatenate([zero, x, zero], axis=0)


def pack_kernel(image_ref, out_ref, rows, scr, sems):
    copies = [pltpu.make_async_copy(image_ref.at[k], rows.at[k], sems.at[k]) for k in range(ROWS)]
    for copy in copies:
        copy.start()
    for k in range(ROWS):
        copies[k].wait()
        put_by_strip(rows[k].astype(F32), k, scr)
    out_ref[...] = scr[...].astype(BF16)


def forward_kernel(image_ref, tall_ref, wide_ref, conv_ref, moved_ref, padded_ref, scr, pad, out):
    scr[...] = image_ref[...].astype(F32)
    pad[0:8, :] = jnp.zeros((8, 128), F32)
    pad[H + 8 : H + 16, :] = jnp.zeros((8, 128), F32)
    for cp in range(PAIRS):
        padded = pad_rows(scr[pl.ds(cp, H, stride=PAIRS), :].astype(BF16))
        padded_ref[cp] = padded
        pad[8 : H + 8, :] = tall_conv(padded, tall_ref[cp], 1).astype(BF16).astype(F32)
        moved = moved_rows(pad, 1)
        moved_ref[cp] = moved
        out[pl.ds(cp, H, stride=PAIRS), :] = jnp.dot(
            moved, wide_ref[cp], preferred_element_type=F32
        )
    conv_ref[...] = out[...].astype(BF16)


def diagonal(x, offset):
    total = None
    for i in range(0, x.shape[0], 8):
        part = pltpu.roll(x[i : i + 8], (offset - i) % 128, 1)
        total = part if total is None else total + part
    row = lax.broadcasted_iota(jnp.int32, (8, 128), 0)
    for bit in (1, 2, 4):
        total = jnp.where(row & bit != 0, pltpu.roll(total, 128 - bit, 1), total)
    return jnp.sum(total, axis=0, keepdims=True)


def backward_kernel(
    scale,
    parts_ref,
    padded_ref,
    moved_ref,
    wide_ref,
    small_ref,
    d_mixed_ref,
    share_ref,
    d_scr,
    d_pad,
    g_scr,
):
    total = None
    for i in range(CHIPS):
        part = parts_ref[i].astype(F32)
        d_scr[i * DATA : (i + 1) * DATA, :] = part[:DATA]
        total = part[DATA:] if total is None else total + part[DATA:]
    share_ref[0:OWN, :] = total.astype(BF16)
    in_block = block_mask()
    d_pad[0:8, :] = jnp.zeros((8, 128), F32)
    d_pad[H + 8 : H + 16, :] = jnp.zeros((8, 128), F32)
    g_scr[40:48, :] = small_ref[...]
    lane, first = half_masks((1, 128))
    lane_b, first_b = half_masks((BAND, 128))
    for cp in range(PAIRS):
        d_conv = d_scr[pl.ds(cp, H, stride=PAIRS), :]
        d_pad[8 : H + 8, :] = d_conv
        d_mixed = jnp.dot(
            moved_rows(d_pad, -1), wide_ref[cp], preferred_element_type=F32
        ).astype(BF16)
        d_mixed_ref[cp] = d_mixed
        corr = lax.dot_general(
            d_conv.astype(BF16), moved_ref[cp], (((0,), (0,)), ((), ())), preferred_element_type=F32
        )
        for p in range(SHORT):
            part = jnp.where(in_block, corr[:, p * 128 : (p + 1) * 128], 0.0)
            low = diagonal(part[:COLS], 32)
            high = diagonal(part[COLS:], 32)
            row = 20 + p * PAIRS + cp
            g_scr[row : row + 1, :] = jnp.where(first, low, high) * scale
        parts = []
        d_mixed_f = d_mixed.astype(F32)
        for q in range(SHORT):
            parts.append(shifted(d_mixed_f, 2 - q))
        left = []
        for c2 in range(2):
            for q in range(SHORT):
                bands = []
                for b in range(H // BAND):
                    band = parts[q][b * BAND : (b + 1) * BAND]
                    bands.append(jnp.where(first_b == (c2 == 0), band, 0.0))
                left.append(jnp.concatenate(bands, axis=1))
        left = jnp.concatenate(left, axis=0).astype(BF16)
        right = jnp.concatenate(
            [padded_ref[cp, b * BAND : b * BAND + 128, :] for b in range(H // BAND)], axis=1
        )
        corr = lax.dot_general(
            left, right, (((1,), (1,)), ((), ())), preferred_element_type=F32
        )
        for q in range(SHORT):
            low = diagonal(corr[q * BAND : (q + 1) * BAND], 0)
            high = diagonal(corr[(SHORT + q) * BAND : (SHORT + q + 1) * BAND], COLS)
            row = q * PAIRS + cp
            g_scr[row : row + 1, :] = jnp.where(first, low, high) * scale
    share_ref[OWN:SHARE, :] = g_scr[...].astype(BF16)


def d_image_kernel(d_mixed_ref, tall_ref, d_image_ref, out):
    for cp in range(PAIRS):
        out[pl.ds(cp, H, stride=PAIRS), :] = tall_conv(
            pad_rows(d_mixed_ref[cp]), tall_ref[cp], -1
        )
    d_image_ref[...] = out[...].astype(BF16)


def mlp_kernel(
    scale,
    core_ref,
    conv_ref,
    image_ref,
    cot_ref,
    gain_ref,
    bias_ref,
    w_in_ref,
    b_in_ref,
    w_out_ref,
    b_out_ref,
    output_ref,
    theirs_ref,
    mine_ref,
    left_ref,
    right_ref,
    small_ref,
    scr,
    out,
    small,
):
    core = core_ref[0]
    scr[...] = conv_ref[...].astype(F32)
    gain, bias = gain_ref[...], bias_ref[...]
    sums = [jnp.zeros((1, C), F32), jnp.zeros((1, C), F32), jnp.zeros((1, C), F32)]
    g_b_in = jnp.zeros((1, FF), F32)
    step = 2
    for k in range(0, ROWS, step):
        rows = slice(k * COLS, (k + step) * COLS)
        conv = jnp.concatenate(
            [
                untwisted(
                    [
                        scr[pl.ds(c * MSG + i * PAIRS + cp, CHIPS, stride=CORES * MSG), :]
                        for cp in range(PAIRS)
                        for c in range(CORES)
                    ]
                )
                for i in range(k, k + step)
            ],
            axis=0,
        )
        centred = conv - jnp.mean(conv, axis=1, keepdims=True)
        inverse = lax.rsqrt(jnp.mean(centred * centred, axis=1, keepdims=True) + epsilon)
        xhat = centred * inverse
        normed = (xhat * gain + bias).astype(BF16)
        left_ref[0, rows, :] = normed
        pre_act = jnp.dot(normed, w_in_ref[...], preferred_element_type=F32) + b_in_ref[...]
        cdf = 0.5 * (1.0 + lax.erf(pre_act * 0.7071067811865476))
        hidden = (pre_act * cdf).astype(BF16)
        right_ref[1, rows, :] = hidden
        branch = jnp.dot(hidden, w_out_ref[...], preferred_element_type=F32) + b_out_ref[...]
        cot = cot_ref[rows, :]
        left_ref[1, rows, :] = cot
        output_ref[rows, :] = (image_ref[rows, :].astype(F32) + branch).astype(BF16)
        d_hidden = lax.dot_general(
            cot, w_out_ref[...], (((1,), (1,)), ((), ())), preferred_element_type=F32
        )
        slope = cdf + pre_act * jnp.exp(-0.5 * pre_act * pre_act) * 0.3989422804014327
        d_pre = (d_hidden * slope).astype(BF16)
        right_ref[0, rows, :] = d_pre
        g_b_in = g_b_in + jnp.sum(d_pre.astype(F32), axis=0, keepdims=True)
        d_norm = lax.dot_general(
            d_pre, w_in_ref[...], (((1,), (1,)), ((), ())), preferred_element_type=F32
        )
        sums[0] = sums[0] + jnp.sum(d_norm * xhat, axis=0, keepdims=True)
        sums[1] = sums[1] + jnp.sum(d_norm, axis=0, keepdims=True)
        sums[2] = sums[2] + jnp.sum(cot.astype(F32), axis=0, keepdims=True)
        g = d_norm * gain
        d_conv = inverse * (
            g
            - jnp.mean(g, axis=1, keepdims=True)
            - xhat * jnp.mean(g * xhat, axis=1, keepdims=True)
        )
        for i in range(step):
            put_by_core(d_conv[i * COLS : (i + 1) * COLS], k + i, out)
    half = CHIPS * MSG
    theirs_ref[GRADS : GRADS + half, :] = out[pl.ds((1 - core) * half, half), :].astype(BF16)
    mine_ref[...] = out[pl.ds(core * half, half), :].astype(BF16)
    weight_grads(scale, left_ref, right_ref, 1 - core, theirs_ref)
    small[...] = jnp.zeros((16, 128), F32)
    for i in range(FF // 128):
        small[i : i + 1, :] = g_b_in[:, i * 128 : (i + 1) * 128] * scale
    for n in range(3):
        for i in range(2):
            row = 8 + 2 * n + i
            small[row : row + 1, :] = sums[n][:, i * 128 : (i + 1) * 128] * scale
    small_ref[...] = small[pl.ds(core * 8, 8), :]
    other = small[pl.ds((1 - core) * 8, 8), :]
    theirs_ref[GRADS + half : GRADS + half + 16, :] = jnp.concatenate(
        [other, jnp.zeros((8, 128), F32)], axis=0
    ).astype(BF16)


def weight_grads(scale, left_ref, right_ref, which, out_ref):
    grads = lax.dot_general(
        left_ref[which], right_ref[which], (((0,), (0,)), ((), ())), preferred_element_type=F32
    )
    grads = (grads * scale).astype(out_ref.dtype)
    for i in range(CHIPS):
        for j in range(FF // 128):
            at = (i * (FF // 128) + j) * 16
            out_ref[at : at + 16, :] = grads[i * 16 : (i + 1) * 16, j * 128 : (j + 1) * 128]


def own_grads_kernel(scale, core_ref, left_ref, right_ref, out_ref):
    weight_grads(scale, left_ref, right_ref, core_ref[0], out_ref)


def merge_kernel(core_ref, mine_ref, grads_ref, small_ref, got_ref, out_ref, small_out):
    half = CHIPS * MSG
    mine = mine_ref[...].astype(F32)
    got = got_ref[GRADS : GRADS + half, :].astype(F32)
    other = got_ref[GRADS + half : GRADS + half + 16, :].astype(F32)
    small_out[...] = small_ref[...] + other[:8]
    low = core_ref[0] == 0
    one, two = jnp.where(low, mine, got), jnp.where(low, got, mine)
    for i in range(CHIPS):
        rows = slice(i * MSG, (i + 1) * MSG)
        out_ref[i, 0:DATA, :] = jnp.concatenate([one[rows], two[rows]], axis=0).astype(BF16)
        rows = slice(i * OWN, (i + 1) * OWN)
        out_ref[i, DATA : DATA + OWN, :] = (grads_ref[rows, :] + got_ref[rows, :].astype(F32)).astype(BF16)


def pair_sum_kernel(mine_ref, got_ref, out_ref):
    total = (mine_ref[...].astype(F32) + got_ref[...].astype(F32)).astype(BF16)
    for i in range(out_ref.shape[0]):
        out_ref[i] = total


def gather_kernel(parts_ref, d_image_ref, out_ref):
    total = parts_ref[0].astype(F32)
    for i in range(1, parts_ref.shape[0]):
        total = total + parts_ref[i].astype(F32)
    total = total.astype(BF16)
    for i in range(CHIPS):
        out_ref[i, 0:DATA, :] = d_image_ref[i * DATA : (i + 1) * DATA, :]
        out_ref[i, DATA : DATA + SHARE, :] = total


def finish_kernel(
    core_ref,
    mine_ref,
    got_ref,
    cot_ref,
    out_ref,
    tall_ref,
    wide_ref,
    gain_ref,
    shift_ref,
    w_in_hbm,
    b_in_ref,
    w_out_hbm,
    b_out_ref,
    scr,
    turn,
    w_in,
    w_out,
    sems,
):
    core = core_ref[0]
    low = core == 0
    rest = LAST - OWN
    totals = [None, None]
    for i in range(CHIPS):
        mine, got = mine_ref[i].astype(F32), got_ref[i].astype(F32)
        sides = (jnp.where(low, mine, got), jnp.where(low, got, mine))
        for c, (side, into) in enumerate(zip(sides, (w_in, turn), strict=True)):
            for j in range(FF // 128):
                piece = side[DATA + j * 16 : DATA + (j + 1) * 16]
                into[i * 16 : (i + 1) * 16, j * 128 : (j + 1) * 128] = piece
            scr[c, i * rest : i * rest + DATA, :] = side[:DATA]
            scr[c, i * rest + DATA : (i + 1) * rest, :] = side[DATA + OWN :]
            part = side[LAST - 8 :]
            totals[c] = part if totals[c] is None else totals[c] + part
    copies = [pltpu.make_async_copy(w_in, w_in_hbm, sems.at[0])]
    copies[0].start()
    step = FF // 2
    for n in range(2):
        for j in range(n * step // 128, (n + 1) * step // 128):
            for half in range(2):
                w_out[j * 128 : (j + 1) * 128, half * 128 : (half + 1) * 128] = turn[
                    half * 128 : (half + 1) * 128, j * 128 : (j + 1) * 128
                ].T
        rows = pl.ds(n * step, step)
        copy = pltpu.make_async_copy(w_out.at[rows], w_out_hbm.at[rows], sems.at[n + 1])
        copy.start()
        copies.append(copy)
    for k in range(ROWS):
        d_image = untwisted(
            [
                scr.at[c][pl.ds(core * MSG + k * PAIRS + cp, CHIPS, stride=rest), :]
                for cp in range(PAIRS)
                for c in range(CORES)
            ]
        )
        out_ref[k] = (cot_ref[k].astype(F32) + d_image).astype(BF16)
    for q in range(SHORT):
        for start, ref in ((0, tall_ref), (20, wide_ref)):
            ref[q] = untwisted(
                [
                    scr.at[c][pl.ds(DATA + start + q * PAIRS + cp, CHIPS, stride=rest), :]
                    for cp in range(PAIRS)
                    for c in range(CORES)
                ]
            )[7 : 7 + LONG]
    for i in range(FF // 128):
        b_in_ref[:, i * 128 : (i + 1) * 128] = totals[0][i : i + 1]
    for n, ref in enumerate((gain_ref, shift_ref, b_out_ref)):
        for i in range(2):
            ref[:, i * 128 : (i + 1) * 128] = totals[1][2 * n + i : 2 * n + i + 1]
    for copy in copies:
        copy.wait()


def messages(x):
    x = lax.all_to_all(x.reshape(STRIPS, MSG, 128), "strip", 0, 0, tiled=True)
    return x.reshape(STRIPS * MSG, 128)


def between_chips(x):
    groups = [[CORES * i + c for i in range(CHIPS)] for c in range(CORES)]
    return lax.all_to_all(x, "strip", 0, 0, axis_index_groups=groups, tiled=True)


def between_cores(x):
    return lax.ppermute(x, "strip", [(i, i ^ 1) for i in range(STRIPS)])


def shape(dims, dtype):
    return jax.ShapeDtypeStruct(dims, dtype)


def local(
    image,
    cotangent,
    kernel_tall,
    kernel_wide,
    layer_norm_gain,
    layer_norm_bias,
    w_in,
    b_in,
    w_out,
    b_out,
):
    source = image[0]
    upstream = cotangent[0]
    slides = lax.axis_size("slide")
    scale = float(CELLS * slides * STRIPS) ** (-0.5)
    packed_f = pltpu.VMEM((STRIPS * MSG, 128), F32)
    packed_b = shape((STRIPS * MSG, 128), BF16)
    edge = pltpu.VMEM((H + 16, 128), F32)

    image_msg = call(
        pack_kernel,
        packed_b,
        [pltpu.VMEM((ROWS, COLS, C), BF16), packed_f, pltpu.SemaphoreType.DMA((ROWS,))],
        [ANY],
    )(source)
    me = lax.axis_index("strip")
    core = (me % CORES).reshape(1)
    me = (me % CORES) * CHIPS + me // CORES
    own = jnp.arange(8)[:, None] * STRIPS + me == jnp.arange(C)[None, :]
    own = own.astype(BF16)

    def taps(kernel, spec):
        picked = jnp.einsum(spec, kernel, own, preferred_element_type=F32)
        picked = picked.reshape(SHORT * 8, LONG)
        pad = ((0, 0), (0, 128 - LONG))
        return jnp.pad(picked, pad), jnp.pad(picked[:, ::-1], pad)

    tall, tall_flipped = taps(kernel_tall, "pqc,kc->qkp")
    wide, wide_flipped = taps(kernel_wide, "pqc,kc->pkq")

    matrices = call(
        matrix_kernel, (shape((PAIRS, SHORT * BAND, C), BF16), shape((PAIRS, SHORT * 128, 128), BF16))
    )
    tall_fwd, wide_fwd = matrices(tall, wide_flipped)
    tall_bwd, wide_bwd = matrices(tall_flipped, wide)

    image_ch = messages(image_msg)
    conv_ch, moved, padded = call(
        forward_kernel,
        (
            packed_b,
            shape((PAIRS, H, SHORT * 128), BF16),
            shape((PAIRS, H + 2 * REACH, 128), BF16),
        ),
        [packed_f, edge, packed_f],
    )(image_ch, tall_fwd, wide_fwd)
    conv = messages(conv_ch)
    output, theirs, mine, left, right, small = call(
        functools.partial(mlp_kernel, scale),
        (
            shape((CELLS, C), BF16),
            shape((GRADS + CHIPS * MSG + 16, 128), BF16),
            shape((CHIPS * MSG, 128), BF16),
            shape((2, CELLS, C), BF16),
            shape((2, CELLS, FF), BF16),
            shape((8, 128), F32),
        ),
        [packed_f, packed_f, pltpu.VMEM((16, 128), F32)],
        [SMEM] + [VMEM] * 9,
    )(
        core,
        conv,
        source.reshape(CELLS, C),
        upstream.reshape(CELLS, C),
        layer_norm_gain[None],
        layer_norm_bias[None],
        w_in,
        b_in[None],
        w_out,
        b_out[None],
    )
    got = between_cores(theirs)
    chip_grads = call(
        functools.partial(own_grads_kernel, scale), shape((GRADS, 128), F32), (), [SMEM] + [VMEM] * 2
    )(core, left, right)
    merged, small = call(
        merge_kernel,
        (shape((CHIPS, DATA + OWN, 128), BF16), shape((8, 128), F32)),
        (),
        [SMEM] + [VMEM] * 4,
    )(core, mine, chip_grads, small, got)
    d_mixed, share = call(
        functools.partial(backward_kernel, scale),
        (shape((PAIRS, H, 128), BF16), shape((SHARE, 128), BF16)),
        [packed_f, edge, pltpu.VMEM((48, 128), F32)],
    )(between_chips(merged), padded, moved, wide_bwd, small)
    got = lax.ppermute(share, "slide", [(i, i ^ 1) for i in range(slides)])
    d_image_msg = call(d_image_kernel, packed_b, [packed_f])(d_mixed, tall_bwd)
    half = slides // 2
    copies = call(pair_sum_kernel, shape((half, SHARE, 128), BF16))(share, got)
    groups = [[2 * i + j for i in range(half)] for j in range(2)]
    parts = lax.all_to_all(copies, "slide", 0, 0, axis_index_groups=groups, tiled=True)
    last = call(gather_kernel, shape((CHIPS, LAST, 128), BF16))(parts, d_image_msg)
    last = between_chips(last)
    got = between_cores(last)
    grad_image, g_tall, g_wide, g_gain, g_shift, g_w_in, g_b_in, g_w_out, g_b_out = call(
        finish_kernel,
        (
            shape((ROWS, COLS, C), BF16),
            shape((SHORT, LONG, C), F32),
            shape((SHORT, LONG, C), F32),
            shape((1, C), F32),
            shape((1, C), F32),
            shape((C, FF), F32),
            shape((1, FF), F32),
            shape((FF, C), F32),
            shape((1, C), F32),
        ),
        [
            pltpu.VMEM((CORES, CHIPS * (LAST - OWN), 128), F32),
            pltpu.VMEM((C, FF), F32),
            pltpu.VMEM((C, FF), F32),
            pltpu.VMEM((FF, C), F32),
            pltpu.SemaphoreType.DMA((3,)),
        ],
        [SMEM] + [VMEM] * 3,
        (VMEM,) * 5 + (ANY, VMEM, ANY, VMEM),
    )(core, last, got, upstream)
    return (
        output.reshape(image.shape),
        grad_image[None],
        jnp.transpose(g_tall, (1, 0, 2)),
        g_wide,
        g_gain[0],
        g_shift[0],
        g_w_in,
        g_b_in[0],
        g_w_out,
        g_b_out[0],
    )


def solution(mesh):
    cells = P("slide", "strip", None, None)
    return jax.shard_map(
        local,
        mesh=mesh,
        in_specs=(cells, cells) + (P(),) * 8,
        out_specs=(cells, cells) + (P(),) * 8,
        check_vma=False,
    )
```

```python
import functools

import jax
import jax.numpy as jnp
from jax import lax
from jax.experimental import pallas as pl
from jax.experimental.pallas import tpu as pltpu
from jax.sharding import PartitionSpec as P

F32 = jnp.float32
BF16 = jnp.bfloat16
CORES = 2
CHIPS = 16
STRIPS = CORES * CHIPS
ROWS = 6
COLS = 64
H = STRIPS * ROWS
C = 256
FF = 1024
LONG = 51
SHORT = 5
PAIRS = 4
BAND = 64
REACH = 32
MSG = ROWS * PAIRS
CELLS = ROWS * COLS
DATA = CORES * MSG
GRADS = C * FF // 128
OWN = GRADS // CHIPS
SHARE = OWN + 48
LAST = DATA + SHARE
epsilon = 1e-06

PARAMS = pltpu.CompilerParams(vmem_limit_bytes=24 * 1024 * 1024)


VMEM = pl.BlockSpec(memory_space=pltpu.VMEM)
SMEM = pl.BlockSpec(memory_space=pltpu.SMEM)
HBM = pl.BlockSpec(memory_space=pltpu.HBM)


def call(kernel, out_shape, scratch=(), in_specs=None, out_specs=None):
    specs = {}
    if in_specs is not None:
        specs["in_specs"] = in_specs
    if out_specs is not None:
        specs["out_specs"] = out_specs
    return pl.pallas_call(
        kernel,
        out_shape=out_shape,
        scratch_shapes=list(scratch),
        compiler_params=PARAMS,
        **specs,
    )


def turned_rows(block):
    return jnp.concatenate([block[:, :128], block[:, 128:]], axis=0).T


def put_by_strip(block, k, scr):
    rows = turned_rows(block)
    for cp in range(PAIRS):
        for core in range(CORES):
            first = cp * STRIPS + core * CHIPS
            at = pl.ds(core * MSG + k * PAIRS + cp, CHIPS, stride=CORES * MSG)
            scr[at, :] = rows[first : first + CHIPS]


def put_by_core(block, k, scr):
    rows = turned_rows(block)
    for cp in range(PAIRS):
        scr[pl.ds(k * PAIRS + cp, STRIPS, stride=MSG), :] = rows[cp * STRIPS : (cp + 1) * STRIPS]


def untwisted(parts):
    rows = jnp.concatenate(parts, axis=0).T
    return jnp.concatenate([rows[:COLS], rows[COLS:]], axis=1)


def half_masks(shape):
    lane = lax.broadcasted_iota(jnp.int32, shape, len(shape) - 1)
    return lane, lane < COLS


def shifted(x, by):
    if by == 0:
        return x
    column = lax.broadcasted_iota(jnp.int32, x.shape, 1) % COLS + by
    return jnp.where((column >= 0) & (column < COLS), pltpu.roll(x, (-by) % 128, 1), 0.0)


def sloped(row, first_shift, count):
    eight = pltpu.roll(jnp.broadcast_to(row, (8, 128)), 0, 1, stride=1, stride_axis=0)
    return jnp.concatenate(
        [pltpu.roll(eight, (first_shift + i) % 128, 1) for i in range(0, count, 8)], axis=0
    )


def tall_matrix(taps_ref, q, c):
    return sloped(taps_ref[q * 8 + c : q * 8 + c + 1, :], REACH - (LONG - 1) // 2, BAND)


def wide_matrix(taps_ref, p, cp, in_block):
    first = -((LONG - 1) // 2)
    turned = jnp.concatenate(
        [
            sloped(taps_ref[n : n + 1, :], first + COLS * c2, COLS)
            for c2, n in enumerate((p * 8 + cp, p * 8 + 4 + cp))
        ],
        axis=0,
    )
    return jnp.where(in_block, turned, 0.0)


def block_mask():
    row = lax.broadcasted_iota(jnp.int32, (128, 128), 0)
    lane = lax.broadcasted_iota(jnp.int32, (128, 128), 1)
    return (row < COLS) == (lane < COLS)


def tall_conv(padded, matrix, sign):
    _, first = half_masks((128, 128))
    zero = jnp.zeros((128, 128), BF16)
    sides = []
    for b in range(H // BAND):
        window = padded[b * BAND : b * BAND + 128]
        sides.append(
            jnp.concatenate([jnp.where(first, window, zero), jnp.where(first, zero, window)], axis=0)
        )
    product = jnp.dot(matrix, jnp.concatenate(sides, axis=1), preferred_element_type=F32)
    bands = []
    for b in range(H // BAND):
        total = None
        for q in range(SHORT):
            part = product[q * BAND : (q + 1) * BAND, b * 128 : (b + 1) * 128]
            part = shifted(part, sign * (q - 2))
            total = part if total is None else total + part
        bands.append(total)
    return jnp.concatenate(bands, axis=0)


def moved_rows(scr, sign):
    return jnp.concatenate(
        [scr[8 + sign * (p - 2) : 8 + sign * (p - 2) + H, :].astype(BF16) for p in range(SHORT)],
        axis=1,
    )


def flipped(taps_ref):
    a = lax.broadcasted_iota(jnp.int32, (128, 128), 0)
    b = lax.broadcasted_iota(jnp.int32, (128, 128), 1)
    turn = (a + b == LONG - 1).astype(BF16)
    return jnp.dot(taps_ref[...].astype(BF16), turn, preferred_element_type=F32)


def tall_matrices(taps, cp):
    return jnp.concatenate(
        [
            jnp.concatenate([tall_matrix(taps, q, c2 * 4 + cp) for c2 in range(2)], axis=1)
            for q in range(SHORT)
        ],
        axis=0,
    ).astype(BF16)


def wide_matrices(taps, cp, in_block):
    return jnp.concatenate(
        [wide_matrix(taps, p, cp, in_block) for p in range(SHORT)], axis=0
    ).astype(BF16)


def matrix_kernel(tall_ref, wide_ref, tall_out, wide_out):
    in_block = block_mask()
    tall, wide = tall_ref[...], flipped(wide_ref)
    for cp in range(PAIRS):
        tall_out[cp] = tall_matrices(tall, cp)
        wide_out[cp] = wide_matrices(wide, cp, in_block)


def pad_rows(x):
    zero = jnp.zeros((REACH, 128), x.dtype)
    return jnp.concatenate([zero, x, zero], axis=0)


def pack_kernel(image_ref, out_ref, scr):
    for k in range(ROWS):
        put_by_strip(image_ref[k].astype(F32), k, scr)
    out_ref[...] = scr[...].astype(BF16)


def forward_kernel(image_ref, tall_ref, wide_ref, conv_ref, mixed_ref, padded_ref, scr, pad, out):
    scr[...] = image_ref[...].astype(F32)
    pad[0:8, :] = jnp.zeros((8, 128), F32)
    pad[H + 8 : H + 16, :] = jnp.zeros((8, 128), F32)
    for cp in range(PAIRS):
        padded = pad_rows(scr[pl.ds(cp, H, stride=PAIRS), :].astype(BF16))
        padded_ref[cp] = padded
        mixed = tall_conv(padded, tall_ref[cp], 1).astype(BF16)
        mixed_ref[cp] = mixed
        pad[8 : H + 8, :] = mixed.astype(F32)
        out[pl.ds(cp, H, stride=PAIRS), :] = jnp.dot(
            moved_rows(pad, 1), wide_ref[cp], preferred_element_type=F32
        )
    conv_ref[...] = out[...].astype(BF16)


def beside_kernel(padded_ref, wide_ref, shifted_ref, wide_out):
    in_block = block_mask()
    wide = wide_ref[...]
    for cp in range(PAIRS):
        padded = padded_ref[cp].astype(F32)
        for q in range(SHORT):
            shifted_ref[cp, q] = shifted(padded, q - 2).astype(BF16)
        wide_out[cp] = wide_matrices(wide, cp, in_block)


def fold(x, offset):
    total = None
    for i in range(0, x.shape[0], 8):
        part = pltpu.roll(x[i : i + 8], (offset - i) % 128, 1)
        total = part if total is None else total + part
    return total


def diagonal_sums(folds, count):
    total = folds[pl.ds(0, count, stride=8), :]
    for i in range(1, 8):
        total = total + pltpu.roll(folds[pl.ds(i, count, stride=8), :], 128 - i, 1)
    return total


def backward_kernel(
    scale,
    parts_ref,
    shifted_ref,
    mixed_ref,
    wide_ref,
    small_ref,
    d_mixed_ref,
    share_ref,
    d_scr,
    d_pad,
    m_pad,
    folds,
):
    total = None
    for i in range(CHIPS):
        part = parts_ref[i].astype(F32)
        d_scr[i * DATA : (i + 1) * DATA, :] = part[:DATA]
        total = part[DATA:] if total is None else total + part[DATA:]
    share_ref[0:OWN, :] = total.astype(BF16)
    for ref in (d_pad, m_pad):
        ref[0:8, :] = jnp.zeros((8, 128), F32)
        ref[H + 8 : H + 16, :] = jnp.zeros((8, 128), F32)
    row = lax.broadcasted_iota(jnp.int32, (BAND, 128), 0)
    lane = lax.broadcasted_iota(jnp.int32, (BAND, 128), 1)
    half = (LONG - 1) // 2
    low_band = (lane - row >= 7) & (lane - row <= 57)
    near = jnp.abs(lane % COLS - row) <= half
    low_near = near & (lane < COLS)
    high_near = near & (lane >= COLS)
    first = lax.broadcasted_iota(jnp.int32, (H, 128), 1) < COLS
    zero = jnp.zeros((H, 128), BF16)
    for cp in range(PAIRS):
        d_conv = d_scr[pl.ds(cp, H, stride=PAIRS), :]
        d_pad[8 : H + 8, :] = d_conv
        m_pad[8 : H + 8, :] = mixed_ref[cp].astype(F32)
        d_mixed = jnp.dot(
            moved_rows(d_pad, -1), wide_ref[cp], preferred_element_type=F32
        ).astype(BF16)
        d_mixed_ref[cp] = d_mixed
        corr = lax.dot_general(
            d_conv.astype(BF16),
            moved_rows(m_pad, 1),
            (((0,), (0,)), ((), ())),
            preferred_element_type=F32,
        )
        for p in range(SHORT):
            part = corr[:, p * 128 : (p + 1) * 128]
            part = jnp.where(low_near, part[:COLS], jnp.where(high_near, part[COLS:], 0.0))
            at = (20 + p * PAIRS + cp) * 8
            folds[at : at + 8, :] = fold(part, 7 + half)
        sides = []
        for c2 in range(2):
            own = jnp.where(first, d_mixed, zero) if c2 == 0 else jnp.where(first, zero, d_mixed)
            own = jnp.concatenate([own[b * BAND : (b + 1) * BAND] for b in range(H // BAND)], axis=1)
            windows = jnp.concatenate(
                [
                    jnp.concatenate(
                        [
                            shifted_ref[cp, q, b * BAND + at : b * BAND + at + BAND, :]
                            for b in range(H // BAND)
                        ],
                        axis=1,
                    )
                    for q in range(SHORT)
                    for at in ((0, BAND) if c2 == 0 else (BAND, 0))
                ],
                axis=0,
            )
            sides.append(
                lax.dot_general(
                    own, windows, (((1,), (1,)), ((), ())), preferred_element_type=F32
                )
            )
        for q in range(SHORT):
            low, high = (side[:, q * 128 : (q + 1) * 128] for side in sides)
            at = (q * PAIRS + cp) * 8
            folds[at : at + 8, :] = fold(jnp.where(low_band, low, high), 0)
    grads = diagonal_sums(folds, 40) * scale
    share_ref[OWN:SHARE, :] = jnp.concatenate([grads, small_ref[...]], axis=0).astype(BF16)


def d_image_kernel(d_mixed_ref, tall_ref, d_image_ref, out):
    taps = flipped(tall_ref)
    for cp in range(PAIRS):
        out[pl.ds(cp, H, stride=PAIRS), :] = tall_conv(
            pad_rows(d_mixed_ref[cp]), tall_matrices(taps, cp), -1
        )
    d_image_ref[...] = out[...].astype(BF16)


def mlp_kernel(
    scale,
    core_ref,
    conv_ref,
    image_ref,
    cot_ref,
    gain_ref,
    bias_ref,
    w_in_ref,
    b_in_ref,
    w_out_ref,
    b_out_ref,
    output_ref,
    theirs_ref,
    mine_ref,
    left_ref,
    right_ref,
    small_ref,
    scr,
    out,
    small,
):
    core = core_ref[0]
    scr[...] = conv_ref[...].astype(F32)
    gain, bias = gain_ref[...], bias_ref[...]
    sums = [jnp.zeros((1, C), F32), jnp.zeros((1, C), F32), jnp.zeros((1, C), F32)]
    g_b_in = jnp.zeros((1, FF), F32)
    step = 2
    for k in range(0, ROWS, step):
        rows = slice(k * COLS, (k + step) * COLS)
        conv = jnp.concatenate(
            [
                untwisted(
                    [
                        scr[pl.ds(c * MSG + i * PAIRS + cp, CHIPS, stride=CORES * MSG), :]
                        for cp in range(PAIRS)
                        for c in range(CORES)
                    ]
                )
                for i in range(k, k + step)
            ],
            axis=0,
        )
        centred = conv - jnp.mean(conv, axis=1, keepdims=True)
        inverse = lax.rsqrt(jnp.mean(centred * centred, axis=1, keepdims=True) + epsilon)
        xhat = centred * inverse
        normed = (xhat * gain + bias).astype(BF16)
        left_ref[0, rows, :] = normed
        pre_act = jnp.dot(normed, w_in_ref[...], preferred_element_type=F32) + b_in_ref[...]
        cdf = 0.5 * (1.0 + lax.erf(pre_act * 0.7071067811865476))
        hidden = (pre_act * cdf).astype(BF16)
        right_ref[1, rows, :] = hidden
        branch = jnp.dot(hidden, w_out_ref[...], preferred_element_type=F32) + b_out_ref[...]
        cot = cot_ref[rows, :]
        left_ref[1, rows, :] = cot
        output_ref[rows, :] = (image_ref[rows, :].astype(F32) + branch).astype(BF16)
        d_hidden = lax.dot_general(
            cot, w_out_ref[...], (((1,), (1,)), ((), ())), preferred_element_type=F32
        )
        slope = cdf + pre_act * jnp.exp(-0.5 * pre_act * pre_act) * 0.3989422804014327
        d_pre = (d_hidden * slope).astype(BF16)
        right_ref[0, rows, :] = d_pre
        g_b_in = g_b_in + jnp.sum(d_pre.astype(F32), axis=0, keepdims=True)
        d_norm = lax.dot_general(
            d_pre, w_in_ref[...], (((1,), (1,)), ((), ())), preferred_element_type=F32
        )
        sums[0] = sums[0] + jnp.sum(d_norm * xhat, axis=0, keepdims=True)
        sums[1] = sums[1] + jnp.sum(d_norm, axis=0, keepdims=True)
        sums[2] = sums[2] + jnp.sum(cot.astype(F32), axis=0, keepdims=True)
        g = d_norm * gain
        d_conv = inverse * (
            g
            - jnp.mean(g, axis=1, keepdims=True)
            - xhat * jnp.mean(g * xhat, axis=1, keepdims=True)
        )
        for i in range(step):
            put_by_core(d_conv[i * COLS : (i + 1) * COLS], k + i, out)
    half = CHIPS * MSG
    theirs_ref[GRADS : GRADS + half, :] = out[pl.ds((1 - core) * half, half), :].astype(BF16)
    mine_ref[...] = out[pl.ds(core * half, half), :].astype(BF16)
    weight_grads(scale, left_ref, right_ref, 1 - core, theirs_ref)
    small[...] = jnp.zeros((16, 128), F32)
    for i in range(FF // 128):
        small[i : i + 1, :] = g_b_in[:, i * 128 : (i + 1) * 128] * scale
    for n in range(3):
        for i in range(2):
            row = 8 + 2 * n + i
            small[row : row + 1, :] = sums[n][:, i * 128 : (i + 1) * 128] * scale
    small_ref[...] = small[pl.ds(core * 8, 8), :]
    other = small[pl.ds((1 - core) * 8, 8), :]
    theirs_ref[GRADS + half : GRADS + half + 16, :] = jnp.concatenate(
        [other, jnp.zeros((8, 128), F32)], axis=0
    ).astype(BF16)


def weight_grads(scale, left_ref, right_ref, which, out_ref):
    grads = lax.dot_general(
        left_ref[which], right_ref[which], (((0,), (0,)), ((), ())), preferred_element_type=F32
    )
    grads = (grads * scale).astype(out_ref.dtype)
    for i in range(CHIPS):
        for j in range(FF // 128):
            at = (i * (FF // 128) + j) * 16
            out_ref[at : at + 16, :] = grads[i * 16 : (i + 1) * 16, j * 128 : (j + 1) * 128]


def own_grads_kernel(scale, core_ref, left_ref, right_ref, out_ref):
    weight_grads(scale, left_ref, right_ref, core_ref[0], out_ref)


def merge_kernel(core_ref, mine_ref, grads_ref, small_ref, got_ref, out_ref, small_out):
    half = CHIPS * MSG
    mine = mine_ref[...].astype(F32)
    got = got_ref[GRADS : GRADS + half, :].astype(F32)
    other = got_ref[GRADS + half : GRADS + half + 16, :].astype(F32)
    small_out[...] = small_ref[...] + other[:8]
    low = core_ref[0] == 0
    one, two = jnp.where(low, mine, got), jnp.where(low, got, mine)
    for i in range(CHIPS):
        rows = slice(i * MSG, (i + 1) * MSG)
        out_ref[i, 0:DATA, :] = jnp.concatenate([one[rows], two[rows]], axis=0).astype(BF16)
        rows = slice(i * OWN, (i + 1) * OWN)
        out_ref[i, DATA : DATA + OWN, :] = (grads_ref[rows, :] + got_ref[rows, :].astype(F32)).astype(BF16)


def pair_sum_kernel(mine_ref, got_ref, out_ref):
    total = (mine_ref[...].astype(F32) + got_ref[...].astype(F32)).astype(BF16)
    for i in range(out_ref.shape[0]):
        out_ref[i] = total


def gather_kernel(parts_ref, d_image_ref, out_ref):
    total = parts_ref[0].astype(F32)
    for i in range(1, parts_ref.shape[0]):
        total = total + parts_ref[i].astype(F32)
    total = total.astype(BF16)
    for i in range(CHIPS):
        out_ref[i, 0:DATA, :] = d_image_ref[i * DATA : (i + 1) * DATA, :]
        out_ref[i, DATA : DATA + SHARE, :] = total


def finish_kernel(
    core_ref,
    mine_ref,
    got_ref,
    cot_ref,
    out_ref,
    tall_ref,
    wide_ref,
    gain_ref,
    shift_ref,
    w_in_hbm,
    b_in_ref,
    w_out_hbm,
    b_out_ref,
    scr,
    turn,
    w_in,
    w_out,
    sems,
):
    core = core_ref[0]
    low = core == 0
    rest = LAST - OWN
    totals = [None, None]
    for i in range(CHIPS):
        mine, got = mine_ref[i].astype(F32), got_ref[i].astype(F32)
        sides = (jnp.where(low, mine, got), jnp.where(low, got, mine))
        for c, (side, into) in enumerate(zip(sides, (w_in, turn), strict=True)):
            for j in range(FF // 128):
                piece = side[DATA + j * 16 : DATA + (j + 1) * 16]
                into[i * 16 : (i + 1) * 16, j * 128 : (j + 1) * 128] = piece
            scr[c, i * rest : i * rest + DATA, :] = side[:DATA]
            scr[c, i * rest + DATA : (i + 1) * rest, :] = side[DATA + OWN :]
            part = side[LAST - 8 :]
            totals[c] = part if totals[c] is None else totals[c] + part
    copies = [pltpu.make_async_copy(w_in, w_in_hbm, sems.at[0])]
    copies[0].start()
    step = FF // 2
    for n in range(2):
        for j in range(n * step // 128, (n + 1) * step // 128):
            for half in range(2):
                w_out[j * 128 : (j + 1) * 128, half * 128 : (half + 1) * 128] = turn[
                    half * 128 : (half + 1) * 128, j * 128 : (j + 1) * 128
                ].T
        rows = pl.ds(n * step, step)
        copy = pltpu.make_async_copy(w_out.at[rows], w_out_hbm.at[rows], sems.at[n + 1])
        copy.start()
        copies.append(copy)
    for k in range(ROWS):
        d_image = untwisted(
            [
                scr.at[c][pl.ds(core * MSG + k * PAIRS + cp, CHIPS, stride=rest), :]
                for cp in range(PAIRS)
                for c in range(CORES)
            ]
        )
        out_ref[k] = (cot_ref[k].astype(F32) + d_image).astype(BF16)
    for q in range(SHORT):
        for start, ref in ((0, tall_ref), (20, wide_ref)):
            ref[q] = untwisted(
                [
                    scr.at[c][pl.ds(DATA + start + q * PAIRS + cp, CHIPS, stride=rest), :]
                    for cp in range(PAIRS)
                    for c in range(CORES)
                ]
            )[7 : 7 + LONG]
    for i in range(FF // 128):
        b_in_ref[:, i * 128 : (i + 1) * 128] = totals[0][i : i + 1]
    for n, ref in enumerate((gain_ref, shift_ref, b_out_ref)):
        for i in range(2):
            ref[:, i * 128 : (i + 1) * 128] = totals[1][2 * n + i : 2 * n + i + 1]
    for copy in copies:
        copy.wait()


def messages(x):
    x = lax.all_to_all(x.reshape(STRIPS, MSG, 128), "strip", 0, 0, tiled=True)
    return x.reshape(STRIPS * MSG, 128)


def between_chips(x):
    groups = [[CORES * i + c for i in range(CHIPS)] for c in range(CORES)]
    return lax.all_to_all(x, "strip", 0, 0, axis_index_groups=groups, tiled=True)


def between_cores(x):
    return lax.ppermute(x, "strip", [(i, i ^ 1) for i in range(STRIPS)])


def shape(dims, dtype):
    return jax.ShapeDtypeStruct(dims, dtype)


def local(
    image,
    cotangent,
    kernel_tall,
    kernel_wide,
    layer_norm_gain,
    layer_norm_bias,
    w_in,
    b_in,
    w_out,
    b_out,
):
    source = image[0]
    upstream = cotangent[0]
    slides = lax.axis_size("slide")
    scale = float(CELLS * slides * STRIPS) ** (-0.5)
    packed_f = pltpu.VMEM((STRIPS * MSG, 128), F32)
    packed_b = shape((STRIPS * MSG, 128), BF16)
    edge = pltpu.VMEM((H + 16, 128), F32)

    image_msg = call(
        pack_kernel,
        packed_b,
        [packed_f],
    )(source)
    me = lax.axis_index("strip")
    core = (me % CORES).reshape(1)
    me = (me % CORES) * CHIPS + me // CORES
    own = jnp.arange(8)[:, None] * STRIPS + me == jnp.arange(C)[None, :]
    own = own.astype(BF16)

    def taps(kernel, spec):
        picked = jnp.einsum(spec, kernel, own, preferred_element_type=F32)
        picked = picked.reshape(SHORT * 8, LONG)
        return jnp.pad(picked, ((0, 0), (0, 128 - LONG)))

    tall = taps(kernel_tall, "pqc,kc->qkp")
    wide = taps(kernel_wide, "pqc,kc->pkq")
    tall_fwd, wide_fwd = call(
        matrix_kernel, (shape((PAIRS, SHORT * BAND, C), BF16), shape((PAIRS, SHORT * 128, 128), BF16))
    )(tall, wide)

    image_ch = messages(image_msg)
    conv_ch, mixed, padded = call(
        forward_kernel,
        (
            packed_b,
            shape((PAIRS, H, 128), BF16),
            shape((PAIRS, H + 2 * REACH, 128), BF16),
        ),
        [packed_f, edge, packed_f],
    )(image_ch, tall_fwd, wide_fwd)
    conv = messages(conv_ch)
    output, theirs, mine, left, right, small = call(
        functools.partial(mlp_kernel, scale),
        (
            shape((CELLS, C), BF16),
            shape((GRADS + CHIPS * MSG + 16, 128), BF16),
            shape((CHIPS * MSG, 128), BF16),
            shape((2, CELLS, C), BF16),
            shape((2, CELLS, FF), BF16),
            shape((8, 128), F32),
        ),
        [packed_f, packed_f, pltpu.VMEM((16, 128), F32)],
        [SMEM] + [VMEM] * 9,
    )(
        core,
        conv,
        source.reshape(CELLS, C),
        upstream.reshape(CELLS, C),
        layer_norm_gain[None],
        layer_norm_bias[None],
        w_in,
        b_in[None],
        w_out,
        b_out[None],
    )
    got = between_cores(theirs)
    chip_grads = call(
        functools.partial(own_grads_kernel, scale), shape((GRADS, 128), F32), (), [SMEM] + [VMEM] * 2
    )(core, left, right)
    merged, small = call(
        merge_kernel,
        (shape((CHIPS, DATA + OWN, 128), BF16), shape((8, 128), F32)),
        (),
        [SMEM] + [VMEM] * 4,
    )(core, mine, chip_grads, small, got)
    shifts, wide_bwd = call(
        beside_kernel,
        (shape((PAIRS, SHORT, H + 2 * REACH, 128), BF16), shape((PAIRS, SHORT * 128, 128), BF16)),
    )(padded, wide)
    d_mixed, share = call(
        functools.partial(backward_kernel, scale),
        (shape((PAIRS, H, 128), BF16), shape((SHARE, 128), BF16)),
        [packed_f, edge, edge, pltpu.VMEM((40 * 8, 128), F32)],
    )(between_chips(merged), shifts, mixed, wide_bwd, small)
    got = lax.ppermute(share, "slide", [(i, i ^ 1) for i in range(slides)])
    d_image_msg = call(d_image_kernel, packed_b, [packed_f])(d_mixed, tall)
    half = slides // 2
    copies = call(pair_sum_kernel, shape((half, SHARE, 128), BF16))(share, got)
    groups = [[2 * i + j for i in range(half)] for j in range(2)]
    parts = lax.all_to_all(copies, "slide", 0, 0, axis_index_groups=groups, tiled=True)
    last = call(gather_kernel, shape((CHIPS, LAST, 128), BF16))(parts, d_image_msg)
    last = between_chips(last)
    got = between_cores(last)
    grad_image, g_tall, g_wide, g_gain, g_shift, g_w_in, g_b_in, g_w_out, g_b_out = call(
        finish_kernel,
        (
            shape((ROWS, COLS, C), BF16),
            shape((SHORT, LONG, C), F32),
            shape((SHORT, LONG, C), F32),
            shape((1, C), F32),
            shape((1, C), F32),
            shape((C, FF), F32),
            shape((1, FF), F32),
            shape((FF, C), F32),
            shape((1, C), F32),
        ),
        [
            pltpu.VMEM((CORES, CHIPS * (LAST - OWN), 128), F32),
            pltpu.VMEM((C, FF), F32),
            pltpu.VMEM((C, FF), F32),
            pltpu.VMEM((FF, C), F32),
            pltpu.SemaphoreType.DMA((3,)),
        ],
        [SMEM] + [VMEM] * 3,
        (VMEM,) * 5 + (HBM, VMEM, HBM, VMEM),
    )(core, last, got, upstream)
    return (
        output.reshape(image.shape),
        grad_image[None],
        jnp.transpose(g_tall, (1, 0, 2)),
        g_wide,
        g_gain[0],
        g_shift[0],
        g_w_in,
        g_b_in[0],
        g_w_out,
        g_b_out[0],
    )


def solution(mesh):
    cells = P("slide", "strip", None, None)
    return jax.shard_map(
        local,
        mesh=mesh,
        in_specs=(cells, cells) + (P(),) * 8,
        out_specs=(cells, cells) + (P(),) * 8,
        check_vma=False,
    )
```

```python
import functools

import jax
import jax.numpy as jnp
from jax import lax
from jax.experimental import pallas as pl
from jax.experimental.pallas import tpu as pltpu
from jax.sharding import PartitionSpec as P

F32 = jnp.float32
BF16 = jnp.bfloat16
CORES = 2
CHIPS = 16
STRIPS = CORES * CHIPS
ROWS = 6
COLS = 64
H = STRIPS * ROWS
C = 256
FF = 1024
LONG = 51
SHORT = 5
PAIRS = 4
BAND = 64
REACH = 32
MSG = ROWS * PAIRS
CELLS = ROWS * COLS
DATA = CORES * MSG
GRADS = C * FF // 128
OWN = GRADS // CHIPS
SHARE = OWN + 48
LAST = DATA + SHARE
epsilon = 1e-06

PARAMS = pltpu.CompilerParams(vmem_limit_bytes=24 * 1024 * 1024)


VMEM = pl.BlockSpec(memory_space=pltpu.VMEM)
SMEM = pl.BlockSpec(memory_space=pltpu.SMEM)
HBM = pl.BlockSpec(memory_space=pltpu.HBM)


def call(kernel, out_shape, scratch=(), in_specs=None, out_specs=None):
    specs = {}
    if in_specs is not None:
        specs["in_specs"] = in_specs
    if out_specs is not None:
        specs["out_specs"] = out_specs
    return pl.pallas_call(
        kernel,
        out_shape=out_shape,
        scratch_shapes=list(scratch),
        compiler_params=PARAMS,
        **specs,
    )


def turned_rows(block):
    return jnp.concatenate([block[:, :128], block[:, 128:]], axis=0).T


def put_by_strip(block, k, scr):
    rows = turned_rows(block)
    for cp in range(PAIRS):
        for core in range(CORES):
            first = cp * STRIPS + core * CHIPS
            at = pl.ds(core * MSG + k * PAIRS + cp, CHIPS, stride=CORES * MSG)
            scr[at, :] = rows[first : first + CHIPS]


def put_by_core(block, k, scr):
    rows = turned_rows(block)
    for cp in range(PAIRS):
        scr[pl.ds(k * PAIRS + cp, STRIPS, stride=MSG), :] = rows[cp * STRIPS : (cp + 1) * STRIPS]


def untwisted(parts):
    rows = jnp.concatenate(parts, axis=0).T
    return jnp.concatenate([rows[:COLS], rows[COLS:]], axis=1)


def half_masks(shape):
    lane = lax.broadcasted_iota(jnp.int32, shape, len(shape) - 1)
    return lane, lane < COLS


def shifted(x, by):
    if by == 0:
        return x
    column = lax.broadcasted_iota(jnp.int32, x.shape, 1) % COLS + by
    return jnp.where((column >= 0) & (column < COLS), pltpu.roll(x, (-by) % 128, 1), 0.0)


def sloped(row, first_shift, count):
    eight = pltpu.roll(jnp.broadcast_to(row, (8, 128)), 0, 1, stride=1, stride_axis=0)
    return jnp.concatenate(
        [pltpu.roll(eight, (first_shift + i) % 128, 1) for i in range(0, count, 8)], axis=0
    )


def tall_matrix(taps_ref, q, c):
    return sloped(taps_ref[q * 8 + c : q * 8 + c + 1, :], REACH - (LONG - 1) // 2, BAND)


def wide_matrix(taps_ref, p, cp, in_block):
    first = -((LONG - 1) // 2)
    turned = jnp.concatenate(
        [
            sloped(taps_ref[n : n + 1, :], first + COLS * c2, COLS)
            for c2, n in enumerate((p * 8 + cp, p * 8 + 4 + cp))
        ],
        axis=0,
    )
    return jnp.where(in_block, turned, 0.0)


def block_mask():
    row = lax.broadcasted_iota(jnp.int32, (128, 128), 0)
    lane = lax.broadcasted_iota(jnp.int32, (128, 128), 1)
    return (row < COLS) == (lane < COLS)


def tall_conv(padded, matrix, sign):
    _, first = half_masks((128, 128))
    zero = jnp.zeros((128, 128), BF16)
    sides = []
    for b in range(H // BAND):
        window = padded[b * BAND : b * BAND + 128]
        sides.append(
            jnp.concatenate([jnp.where(first, window, zero), jnp.where(first, zero, window)], axis=0)
        )
    product = jnp.dot(matrix, jnp.concatenate(sides, axis=1), preferred_element_type=F32)
    bands = []
    for b in range(H // BAND):
        total = None
        for q in range(SHORT):
            part = product[q * BAND : (q + 1) * BAND, b * 128 : (b + 1) * 128]
            part = shifted(part, sign * (q - 2))
            total = part if total is None else total + part
        bands.append(total)
    return jnp.concatenate(bands, axis=0)


def moved_rows(scr, sign):
    return jnp.concatenate(
        [scr[8 + sign * (p - 2) : 8 + sign * (p - 2) + H, :].astype(BF16) for p in range(SHORT)],
        axis=1,
    )


def flipped(taps_ref):
    a = lax.broadcasted_iota(jnp.int32, (128, 128), 0)
    b = lax.broadcasted_iota(jnp.int32, (128, 128), 1)
    turn = (a + b == LONG - 1).astype(BF16)
    return jnp.dot(taps_ref[...].astype(BF16), turn, preferred_element_type=F32)


def tall_matrices(taps, cp):
    return jnp.concatenate(
        [
            jnp.concatenate([tall_matrix(taps, q, c2 * 4 + cp) for c2 in range(2)], axis=1)
            for q in range(SHORT)
        ],
        axis=0,
    ).astype(BF16)


def wide_matrices(taps, cp, in_block):
    return jnp.concatenate(
        [wide_matrix(taps, p, cp, in_block) for p in range(SHORT)], axis=0
    ).astype(BF16)


def matrix_kernel(tall_ref, wide_ref, tall_out, wide_out):
    in_block = block_mask()
    tall, wide = tall_ref[...], flipped(wide_ref)
    for cp in range(PAIRS):
        tall_out[cp] = tall_matrices(tall, cp)
        wide_out[cp] = wide_matrices(wide, cp, in_block)


def pad_rows(x):
    zero = jnp.zeros((REACH, 128), x.dtype)
    return jnp.concatenate([zero, x, zero], axis=0)


def pack_kernel(image_ref, out_ref, scr):
    for k in range(ROWS):
        put_by_strip(image_ref[0, k].astype(F32), k, scr)
    out_ref[...] = scr[...].astype(BF16)


def forward_kernel(image_ref, tall_ref, wide_ref, conv_ref, mixed_ref, scr, pad, out):
    scr[...] = image_ref[...].astype(F32)
    pad[0:8, :] = jnp.zeros((8, 128), F32)
    pad[H + 8 : H + 16, :] = jnp.zeros((8, 128), F32)
    for cp in range(PAIRS):
        padded = pad_rows(scr[pl.ds(cp, H, stride=PAIRS), :].astype(BF16))
        mixed = tall_conv(padded, tall_ref[cp], 1).astype(BF16)
        mixed_ref[cp] = mixed
        pad[8 : H + 8, :] = mixed.astype(F32)
        out[pl.ds(cp, H, stride=PAIRS), :] = jnp.dot(
            moved_rows(pad, 1), wide_ref[cp], preferred_element_type=F32
        )
    conv_ref[...] = out[...].astype(BF16)


def beside_kernel(image_ref, wide_ref, shifted_ref, wide_out, scr):
    in_block = block_mask()
    wide = wide_ref[...]
    scr[...] = image_ref[...].astype(F32)
    for cp in range(PAIRS):
        padded = pad_rows(scr[pl.ds(cp, H, stride=PAIRS), :])
        for q in range(SHORT):
            shifted_ref[cp, q] = shifted(padded, q - 2).astype(BF16)
        wide_out[cp] = wide_matrices(wide, cp, in_block)


def fold(x, offset):
    total = None
    for i in range(0, x.shape[0], 8):
        part = pltpu.roll(x[i : i + 8], (offset - i) % 128, 1)
        total = part if total is None else total + part
    return total


def diagonal_sums(folds, count):
    total = folds[pl.ds(0, count, stride=8), :]
    for i in range(1, 8):
        total = total + pltpu.roll(folds[pl.ds(i, count, stride=8), :], 128 - i, 1)
    return total


def backward_kernel(
    scale,
    parts_ref,
    shifted_ref,
    mixed_ref,
    wide_ref,
    small_ref,
    d_mixed_ref,
    share_ref,
    d_scr,
    d_pad,
    m_pad,
    folds,
):
    total = None
    for i in range(CHIPS):
        part = parts_ref[i].astype(F32)
        d_scr[i * DATA : (i + 1) * DATA, :] = part[:DATA]
        total = part[DATA:] if total is None else total + part[DATA:]
    share_ref[0:OWN, :] = total.astype(BF16)
    for ref in (d_pad, m_pad):
        ref[0:8, :] = jnp.zeros((8, 128), F32)
        ref[H + 8 : H + 16, :] = jnp.zeros((8, 128), F32)
    row = lax.broadcasted_iota(jnp.int32, (BAND, 128), 0)
    lane = lax.broadcasted_iota(jnp.int32, (BAND, 128), 1)
    half = (LONG - 1) // 2
    low_band = (lane - row >= 7) & (lane - row <= 57)
    near = jnp.abs(lane % COLS - row) <= half
    low_near = near & (lane < COLS)
    high_near = near & (lane >= COLS)
    first = lax.broadcasted_iota(jnp.int32, (H, 128), 1) < COLS
    zero = jnp.zeros((H, 128), BF16)
    for cp in range(PAIRS):
        d_conv = d_scr[pl.ds(cp, H, stride=PAIRS), :]
        d_pad[8 : H + 8, :] = d_conv
        m_pad[8 : H + 8, :] = mixed_ref[cp].astype(F32)
        d_mixed = jnp.dot(
            moved_rows(d_pad, -1), wide_ref[cp], preferred_element_type=F32
        ).astype(BF16)
        d_mixed_ref[cp] = d_mixed
        corr = lax.dot_general(
            d_conv.astype(BF16),
            moved_rows(m_pad, 1),
            (((0,), (0,)), ((), ())),
            preferred_element_type=F32,
        )
        for p in range(SHORT):
            part = corr[:, p * 128 : (p + 1) * 128]
            part = jnp.where(low_near, part[:COLS], jnp.where(high_near, part[COLS:], 0.0))
            at = (20 + p * PAIRS + cp) * 8
            folds[at : at + 8, :] = fold(part, 7 + half)
        sides = []
        for c2 in range(2):
            own = jnp.where(first, d_mixed, zero) if c2 == 0 else jnp.where(first, zero, d_mixed)
            own = jnp.concatenate([own[b * BAND : (b + 1) * BAND] for b in range(H // BAND)], axis=1)
            windows = jnp.concatenate(
                [
                    jnp.concatenate(
                        [
                            shifted_ref[cp, q, b * BAND + at : b * BAND + at + BAND, :]
                            for b in range(H // BAND)
                        ],
                        axis=1,
                    )
                    for q in range(SHORT)
                    for at in ((0, BAND) if c2 == 0 else (BAND, 0))
                ],
                axis=0,
            )
            sides.append(
                lax.dot_general(
                    own, windows, (((1,), (1,)), ((), ())), preferred_element_type=F32
                )
            )
        for q in range(SHORT):
            low, high = (side[:, q * 128 : (q + 1) * 128] for side in sides)
            at = (q * PAIRS + cp) * 8
            folds[at : at + 8, :] = fold(jnp.where(low_band, low, high), 0)
    grads = diagonal_sums(folds, 40) * scale
    share_ref[OWN:SHARE, :] = jnp.concatenate([grads, small_ref[...]], axis=0).astype(BF16)


def d_image_kernel(d_mixed_ref, tall_ref, d_image_ref, out):
    taps = flipped(tall_ref)
    for cp in range(PAIRS):
        out[pl.ds(cp, H, stride=PAIRS), :] = tall_conv(
            pad_rows(d_mixed_ref[cp]), tall_matrices(taps, cp), -1
        )
    d_image_ref[...] = out[...].astype(BF16)


def mlp_kernel(
    scale,
    core_ref,
    conv_ref,
    image_ref,
    cot_ref,
    gain_ref,
    bias_ref,
    w_in_ref,
    b_in_ref,
    w_out_ref,
    b_out_ref,
    output_ref,
    theirs_ref,
    mine_ref,
    normed_ref,
    right_ref,
    small_ref,
    scr,
    out,
    small,
):
    core = core_ref[0]
    scr[...] = conv_ref[...].astype(F32)
    gain, bias = gain_ref[...], bias_ref[...]
    sums = [jnp.zeros((1, C), F32), jnp.zeros((1, C), F32), jnp.zeros((1, C), F32)]
    g_b_in = jnp.zeros((1, FF), F32)
    step = 2
    for k in range(0, ROWS, step):
        rows = slice(k * COLS, (k + step) * COLS)
        conv = jnp.concatenate(
            [
                untwisted(
                    [
                        scr[pl.ds(c * MSG + i * PAIRS + cp, CHIPS, stride=CORES * MSG), :]
                        for cp in range(PAIRS)
                        for c in range(CORES)
                    ]
                )
                for i in range(k, k + step)
            ],
            axis=0,
        )
        centred = conv - jnp.mean(conv, axis=1, keepdims=True)
        inverse = lax.rsqrt(jnp.mean(centred * centred, axis=1, keepdims=True) + epsilon)
        xhat = centred * inverse
        normed = (xhat * gain + bias).astype(BF16)
        normed_ref[rows, :] = normed
        pre_act = jnp.dot(normed, w_in_ref[...], preferred_element_type=F32) + b_in_ref[...]
        cdf = 0.5 * (1.0 + lax.erf(pre_act * 0.7071067811865476))
        hidden = (pre_act * cdf).astype(BF16)
        right_ref[1, rows, :] = hidden
        branch = jnp.dot(hidden, w_out_ref[...], preferred_element_type=F32) + b_out_ref[...]
        cot = cot_ref[rows, :]
        output_ref[rows, :] = (image_ref[rows, :].astype(F32) + branch).astype(BF16)
        d_hidden = lax.dot_general(
            cot, w_out_ref[...], (((1,), (1,)), ((), ())), preferred_element_type=F32
        )
        slope = cdf + pre_act * jnp.exp(-0.5 * pre_act * pre_act) * 0.3989422804014327
        d_pre = (d_hidden * slope).astype(BF16)
        right_ref[0, rows, :] = d_pre
        g_b_in = g_b_in + jnp.sum(d_pre.astype(F32), axis=0, keepdims=True)
        d_norm = lax.dot_general(
            d_pre, w_in_ref[...], (((1,), (1,)), ((), ())), preferred_element_type=F32
        )
        sums[0] = sums[0] + jnp.sum(d_norm * xhat, axis=0, keepdims=True)
        sums[1] = sums[1] + jnp.sum(d_norm, axis=0, keepdims=True)
        sums[2] = sums[2] + jnp.sum(cot.astype(F32), axis=0, keepdims=True)
        g = d_norm * gain
        d_conv = inverse * (
            g
            - jnp.mean(g, axis=1, keepdims=True)
            - xhat * jnp.mean(g * xhat, axis=1, keepdims=True)
        )
        for i in range(step):
            put_by_core(d_conv[i * COLS : (i + 1) * COLS], k + i, out)
    half = CHIPS * MSG
    theirs_ref[GRADS : GRADS + half, :] = out[pl.ds((1 - core) * half, half), :].astype(BF16)
    mine_ref[...] = out[pl.ds(core * half, half), :].astype(BF16)
    weight_grads(scale, normed_ref, cot_ref, right_ref, 1 - core, theirs_ref)
    small[...] = jnp.zeros((16, 128), F32)
    for i in range(FF // 128):
        small[i : i + 1, :] = g_b_in[:, i * 128 : (i + 1) * 128] * scale
    for n in range(3):
        for i in range(2):
            row = 8 + 2 * n + i
            small[row : row + 1, :] = sums[n][:, i * 128 : (i + 1) * 128] * scale
    small_ref[...] = small[pl.ds(core * 8, 8), :]
    other = small[pl.ds((1 - core) * 8, 8), :]
    theirs_ref[GRADS + half : GRADS + half + 16, :] = jnp.concatenate(
        [other, jnp.zeros((8, 128), F32)], axis=0
    ).astype(BF16)


def weight_grads(scale, normed_ref, cot_ref, right_ref, which, out_ref):
    grads = lax.dot_general(
        jnp.where(which == 0, normed_ref[...], cot_ref[...]),
        right_ref[which],
        (((0,), (0,)), ((), ())),
        preferred_element_type=F32,
    )
    grads = (grads * scale).astype(out_ref.dtype)
    for i in range(CHIPS):
        for j in range(FF // 128):
            at = (i * (FF // 128) + j) * 16
            out_ref[at : at + 16, :] = grads[i * 16 : (i + 1) * 16, j * 128 : (j + 1) * 128]


def own_grads_kernel(scale, core_ref, normed_ref, cot_ref, right_ref, out_ref):
    weight_grads(scale, normed_ref, cot_ref, right_ref, core_ref[0], out_ref)


def merge_kernel(core_ref, mine_ref, grads_ref, small_ref, got_ref, out_ref, small_out):
    half = CHIPS * MSG
    mine = mine_ref[...].astype(F32)
    got = got_ref[GRADS : GRADS + half, :].astype(F32)
    other = got_ref[GRADS + half : GRADS + half + 16, :].astype(F32)
    small_out[...] = small_ref[...] + other[:8]
    low = core_ref[0] == 0
    one, two = jnp.where(low, mine, got), jnp.where(low, got, mine)
    for i in range(CHIPS):
        rows = slice(i * MSG, (i + 1) * MSG)
        out_ref[i, 0:DATA, :] = jnp.concatenate([one[rows], two[rows]], axis=0).astype(BF16)
        rows = slice(i * OWN, (i + 1) * OWN)
        out_ref[i, DATA : DATA + OWN, :] = (grads_ref[rows, :] + got_ref[rows, :].astype(F32)).astype(BF16)


def pair_sum_kernel(mine_ref, got_ref, out_ref, total, sems):
    total[...] = (mine_ref[...].astype(F32) + got_ref[...].astype(F32)).astype(BF16)
    count = out_ref.shape[0]
    copies = [pltpu.make_async_copy(total, out_ref.at[i], sems.at[i]) for i in range(count)]
    for copy in copies:
        copy.start()
    for copy in copies:
        copy.wait()


def gather_kernel(parts_ref, d_image_ref, out_ref):
    total = parts_ref[0].astype(F32)
    for i in range(1, parts_ref.shape[0]):
        total = total + parts_ref[i].astype(F32)
    total = total.astype(BF16)
    for i in range(CHIPS):
        out_ref[i, 0:DATA, :] = d_image_ref[i * DATA : (i + 1) * DATA, :]
        out_ref[i, DATA : DATA + SHARE, :] = total


def finish_kernel(
    core_ref,
    mine_ref,
    got_ref,
    cot_ref,
    out_ref,
    tall_ref,
    wide_ref,
    gain_ref,
    shift_ref,
    w_in_hbm,
    b_in_ref,
    w_out_hbm,
    b_out_ref,
    scr,
    turn,
    w_in,
    w_out,
    sems,
):
    core = core_ref[0]
    rest = LAST - OWN

    def place(core_0_ref, core_1_ref):
        for i in range(CHIPS):
            for c, (ref, into) in enumerate(((core_0_ref, w_in), (core_1_ref, turn))):
                side = ref[i].astype(F32)
                for j in range(FF // 128):
                    piece = side[DATA + j * 16 : DATA + (j + 1) * 16]
                    into[i * 16 : (i + 1) * 16, j * 128 : (j + 1) * 128] = piece
                scr[c, i * rest : i * rest + DATA, :] = side[:DATA]
                scr[c, i * rest + DATA : (i + 1) * rest, :] = side[DATA + OWN :]

    @pl.when(core == 0)
    def _():
        place(mine_ref, got_ref)

    @pl.when(core == 1)
    def _():
        place(got_ref, mine_ref)

    copies = [pltpu.make_async_copy(w_in, w_in_hbm, sems.at[0])]
    copies[0].start()
    step = FF // 2
    for n in range(2):
        for j in range(n * step // 128, (n + 1) * step // 128):
            for half in range(2):
                w_out[j * 128 : (j + 1) * 128, half * 128 : (half + 1) * 128] = turn[
                    half * 128 : (half + 1) * 128, j * 128 : (j + 1) * 128
                ].T
        rows = pl.ds(n * step, step)
        copy = pltpu.make_async_copy(w_out.at[rows], w_out_hbm.at[rows], sems.at[n + 1])
        copy.start()
        copies.append(copy)
    for k in range(ROWS):
        d_image = untwisted(
            [
                scr.at[c][pl.ds(core * MSG + k * PAIRS + cp, CHIPS, stride=rest), :]
                for cp in range(PAIRS)
                for c in range(CORES)
            ]
        )
        out_ref[k] = (cot_ref[k].astype(F32) + d_image).astype(BF16)
    for q in range(SHORT):
        for start, ref in ((0, tall_ref), (20, wide_ref)):
            ref[q] = untwisted(
                [
                    scr.at[c][pl.ds(DATA + start + q * PAIRS + cp, CHIPS, stride=rest), :]
                    for cp in range(PAIRS)
                    for c in range(CORES)
                ]
            )[7 : 7 + LONG]
    totals = []
    for c in range(CORES):
        total = None
        for i in range(CHIPS):
            part = scr[c, (i + 1) * rest - 8 : (i + 1) * rest, :]
            total = part if total is None else total + part
        totals.append(total)
    for i in range(FF // 128):
        b_in_ref[:, i * 128 : (i + 1) * 128] = totals[0][i : i + 1]
    for n, ref in enumerate((gain_ref, shift_ref, b_out_ref)):
        for i in range(2):
            ref[:, i * 128 : (i + 1) * 128] = totals[1][2 * n + i : 2 * n + i + 1]
    for copy in copies:
        copy.wait()


def messages(x):
    x = lax.all_to_all(x.reshape(STRIPS, MSG, 128), "strip", 0, 0, tiled=True)
    return x.reshape(STRIPS * MSG, 128)


def between_chips(x):
    groups = [[CORES * i + c for i in range(CHIPS)] for c in range(CORES)]
    return lax.all_to_all(x, "strip", 0, 0, axis_index_groups=groups, tiled=True)


def between_cores(x):
    return lax.ppermute(x, "strip", [(i, i ^ 1) for i in range(STRIPS)])


def shape(dims, dtype):
    return jax.ShapeDtypeStruct(dims, dtype)


def local(
    image,
    cotangent,
    kernel_tall,
    kernel_wide,
    layer_norm_gain,
    layer_norm_bias,
    w_in,
    b_in,
    w_out,
    b_out,
):
    source = image[0]
    upstream = cotangent[0]
    slides = lax.axis_size("slide")
    scale = float(CELLS * slides * STRIPS) ** (-0.5)
    packed_f = pltpu.VMEM((STRIPS * MSG, 128), F32)
    packed_b = shape((STRIPS * MSG, 128), BF16)
    edge = pltpu.VMEM((H + 16, 128), F32)

    image_msg = call(
        pack_kernel,
        packed_b,
        [packed_f],
    )(image)
    me = lax.axis_index("strip")
    core = (me % CORES).reshape(1)
    me = (me % CORES) * CHIPS + me // CORES
    own = jnp.arange(8)[:, None] * STRIPS + me == jnp.arange(C)[None, :]
    own = own.astype(BF16)

    def taps(kernel, spec):
        picked = jnp.einsum(spec, kernel, own, preferred_element_type=F32)
        picked = picked.reshape(SHORT * 8, LONG)
        return jnp.pad(picked, ((0, 0), (0, 128 - LONG)))

    tall = taps(kernel_tall, "pqc,kc->qkp")
    wide = taps(kernel_wide, "pqc,kc->pkq")
    tall_fwd, wide_fwd = call(
        matrix_kernel, (shape((PAIRS, SHORT * BAND, C), BF16), shape((PAIRS, SHORT * 128, 128), BF16))
    )(tall, wide)

    image_ch = messages(image_msg)
    conv_ch, mixed = call(
        forward_kernel,
        (
            packed_b,
            shape((PAIRS, H, 128), BF16),
        ),
        [packed_f, edge, packed_f],
    )(image_ch, tall_fwd, wide_fwd)
    conv = messages(conv_ch)
    output, theirs, mine, normed, right, small = call(
        functools.partial(mlp_kernel, scale),
        (
            shape((CELLS, C), BF16),
            shape((GRADS + CHIPS * MSG + 16, 128), BF16),
            shape((CHIPS * MSG, 128), BF16),
            shape((CELLS, C), BF16),
            shape((2, CELLS, FF), BF16),
            shape((8, 128), F32),
        ),
        [packed_f, packed_f, pltpu.VMEM((16, 128), F32)],
        [SMEM] + [VMEM] * 9,
    )(
        core,
        conv,
        source.reshape(CELLS, C),
        upstream.reshape(CELLS, C),
        layer_norm_gain[None],
        layer_norm_bias[None],
        w_in,
        b_in[None],
        w_out,
        b_out[None],
    )
    got = between_cores(theirs)
    chip_grads = call(
        functools.partial(own_grads_kernel, scale), shape((GRADS, 128), F32), (), [SMEM] + [VMEM] * 3
    )(core, normed, upstream.reshape(CELLS, C), right)
    merged, small = call(
        merge_kernel,
        (shape((CHIPS, DATA + OWN, 128), BF16), shape((8, 128), F32)),
        (),
        [SMEM] + [VMEM] * 4,
    )(core, mine, chip_grads, small, got)
    shifts, wide_bwd = call(
        beside_kernel,
        (shape((PAIRS, SHORT, H + 2 * REACH, 128), BF16), shape((PAIRS, SHORT * 128, 128), BF16)),
        [packed_f],
    )(image_ch, wide)
    d_mixed, share = call(
        functools.partial(backward_kernel, scale),
        (shape((PAIRS, H, 128), BF16), shape((SHARE, 128), BF16)),
        [packed_f, edge, edge, pltpu.VMEM((40 * 8, 128), F32)],
    )(between_chips(merged), shifts, mixed, wide_bwd, small)
    got = lax.ppermute(share, "slide", [(i, i ^ 1) for i in range(slides)])
    d_image_msg = call(d_image_kernel, packed_b, [packed_f])(d_mixed, tall)
    half = slides // 2
    copies = call(
        pair_sum_kernel,
        shape((half, SHARE, 128), BF16),
        [pltpu.VMEM((SHARE, 128), BF16), pltpu.SemaphoreType.DMA((half,))],
        [VMEM, VMEM],
        HBM,
    )(share, got)
    groups = [[2 * i + j for i in range(half)] for j in range(2)]
    parts = lax.all_to_all(copies, "slide", 0, 0, axis_index_groups=groups, tiled=True)
    last = call(gather_kernel, shape((CHIPS, LAST, 128), BF16))(parts, d_image_msg)
    last = between_chips(last)
    got = between_cores(last)
    grad_image, g_tall, g_wide, g_gain, g_shift, g_w_in, g_b_in, g_w_out, g_b_out = call(
        finish_kernel,
        (
            shape((ROWS, COLS, C), BF16),
            shape((SHORT, LONG, C), F32),
            shape((SHORT, LONG, C), F32),
            shape((1, C), F32),
            shape((1, C), F32),
            shape((C, FF), F32),
            shape((1, FF), F32),
            shape((FF, C), F32),
            shape((1, C), F32),
        ),
        [
            pltpu.VMEM((CORES, CHIPS * (LAST - OWN), 128), F32),
            pltpu.VMEM((C, FF), F32),
            pltpu.VMEM((C, FF), F32),
            pltpu.VMEM((FF, C), F32),
            pltpu.SemaphoreType.DMA((3,)),
        ],
        [SMEM] + [VMEM] * 3,
        (VMEM,) * 5 + (HBM, VMEM, HBM, VMEM),
    )(core, last, got, upstream)
    return (
        output.reshape(image.shape),
        grad_image[None],
        jnp.transpose(g_tall, (1, 0, 2)),
        g_wide,
        g_gain[0],
        g_shift[0],
        g_w_in,
        g_b_in[0],
        g_w_out,
        g_b_out[0],
    )


def solution(mesh):
    cells = P("slide", "strip", None, None)
    return jax.shard_map(
        local,
        mesh=mesh,
        in_specs=(cells, cells) + (P(),) * 8,
        out_specs=(cells, cells) + (P(),) * 8,
        check_vma=False,
    )
```

```python
import functools

import jax
import jax.numpy as jnp
from jax import lax
from jax.experimental import pallas as pl
from jax.experimental.pallas import tpu as pltpu
from jax.sharding import PartitionSpec as P

F32 = jnp.float32
BF16 = jnp.bfloat16
CORES = 2
CHIPS = 16
STRIPS = CORES * CHIPS
ROWS = 6
COLS = 64
H = STRIPS * ROWS
C = 256
FF = 1024
LONG = 51
SHORT = 5
PAIRS = 4
BAND = 64
REACH = 32
MSG = ROWS * PAIRS
CELLS = ROWS * COLS
DATA = CORES * MSG
GRADS = C * FF // 128
OWN = GRADS // CHIPS
SHARE = OWN + 48
LAST = DATA + SHARE
epsilon = 1e-06

PARAMS = pltpu.CompilerParams(vmem_limit_bytes=24 * 1024 * 1024)


VMEM = pl.BlockSpec(memory_space=pltpu.VMEM)
SMEM = pl.BlockSpec(memory_space=pltpu.SMEM)
HBM = pl.BlockSpec(memory_space=pltpu.HBM)


def call(kernel, out_shape, scratch=(), in_specs=None, out_specs=None, aliases=None):
    specs = {}
    if in_specs is not None:
        specs["in_specs"] = in_specs
    if out_specs is not None:
        specs["out_specs"] = out_specs
    if aliases is not None:
        specs["input_output_aliases"] = aliases
    return pl.pallas_call(
        kernel,
        out_shape=out_shape,
        scratch_shapes=list(scratch),
        compiler_params=PARAMS,
        **specs,
    )


def turned_rows(block):
    return jnp.concatenate([block[:, :128], block[:, 128:]], axis=0).T


def put_by_strip(block, k, scr):
    rows = turned_rows(block)
    for cp in range(PAIRS):
        for core in range(CORES):
            first = cp * STRIPS + core * CHIPS
            at = pl.ds(core * MSG + k * PAIRS + cp, CHIPS, stride=CORES * MSG)
            scr[at, :] = rows[first : first + CHIPS]


def put_by_core(block, k, scr):
    rows = turned_rows(block)
    for cp in range(PAIRS):
        scr[pl.ds(k * PAIRS + cp, STRIPS, stride=MSG), :] = rows[cp * STRIPS : (cp + 1) * STRIPS]


def untwisted(parts):
    rows = jnp.concatenate(parts, axis=0).T
    return jnp.concatenate([rows[:COLS], rows[COLS:]], axis=1)


def half_masks(shape):
    lane = lax.broadcasted_iota(jnp.int32, shape, len(shape) - 1)
    return lane, lane < COLS


def shifted(x, by):
    if by == 0:
        return x
    column = lax.broadcasted_iota(jnp.int32, x.shape, 1) % COLS + by
    return jnp.where((column >= 0) & (column < COLS), pltpu.roll(x, (-by) % 128, 1), 0.0)


def sloped(row, first_shift, count):
    eight = pltpu.roll(jnp.broadcast_to(row, (8, 128)), 0, 1, stride=1, stride_axis=0)
    return jnp.concatenate(
        [pltpu.roll(eight, (first_shift + i) % 128, 1) for i in range(0, count, 8)], axis=0
    )


def tall_matrix(taps_ref, q, c):
    return sloped(taps_ref[q * 8 + c : q * 8 + c + 1, :], REACH - (LONG - 1) // 2, BAND)


def wide_matrix(taps_ref, p, cp, in_block):
    first = -((LONG - 1) // 2)
    turned = jnp.concatenate(
        [
            sloped(taps_ref[n : n + 1, :], first + COLS * c2, COLS)
            for c2, n in enumerate((p * 8 + cp, p * 8 + 4 + cp))
        ],
        axis=0,
    )
    return jnp.where(in_block, turned, 0.0)


def block_mask():
    row = lax.broadcasted_iota(jnp.int32, (128, 128), 0)
    lane = lax.broadcasted_iota(jnp.int32, (128, 128), 1)
    return (row < COLS) == (lane < COLS)


def tall_conv(padded, matrix, sign):
    _, first = half_masks((128, 128))
    zero = jnp.zeros((128, 128), BF16)
    sides = []
    for b in range(H // BAND):
        window = padded[b * BAND : b * BAND + 128]
        sides.append(
            jnp.concatenate([jnp.where(first, window, zero), jnp.where(first, zero, window)], axis=0)
        )
    product = jnp.dot(matrix, jnp.concatenate(sides, axis=1), preferred_element_type=F32)
    bands = []
    for b in range(H // BAND):
        total = None
        for q in range(SHORT):
            part = product[q * BAND : (q + 1) * BAND, b * 128 : (b + 1) * 128]
            part = shifted(part, sign * (q - 2))
            total = part if total is None else total + part
        bands.append(total)
    return jnp.concatenate(bands, axis=0)


def moved_rows(scr, sign):
    return jnp.concatenate(
        [scr[8 + sign * (p - 2) : 8 + sign * (p - 2) + H, :].astype(BF16) for p in range(SHORT)],
        axis=1,
    )


def flipped(taps_ref):
    a = lax.broadcasted_iota(jnp.int32, (128, 128), 0)
    b = lax.broadcasted_iota(jnp.int32, (128, 128), 1)
    turn = (a + b == LONG - 1).astype(BF16)
    return jnp.dot(taps_ref[...].astype(BF16), turn, preferred_element_type=F32)


def tall_matrices(taps, cp):
    return jnp.concatenate(
        [
            jnp.concatenate([tall_matrix(taps, q, c2 * 4 + cp) for c2 in range(2)], axis=1)
            for q in range(SHORT)
        ],
        axis=0,
    ).astype(BF16)


def wide_matrices(taps, cp, in_block):
    return jnp.concatenate(
        [wide_matrix(taps, p, cp, in_block) for p in range(SHORT)], axis=0
    ).astype(BF16)


def matrix_kernel(tall_ref, wide_ref, tall_out, wide_out):
    in_block = block_mask()
    tall, wide = tall_ref[...], flipped(wide_ref)
    for cp in range(PAIRS):
        tall_out[cp] = tall_matrices(tall, cp)
        wide_out[cp] = wide_matrices(wide, cp, in_block)


def pad_rows(x):
    zero = jnp.zeros((REACH, 128), x.dtype)
    return jnp.concatenate([zero, x, zero], axis=0)


def pack_kernel(image_ref, out_ref, scr):
    for k in range(ROWS):
        put_by_strip(image_ref[0, k].astype(F32), k, scr)
    out_ref[...] = scr[...].astype(BF16)


def forward_kernel(image_ref, tall_ref, wide_ref, conv_ref, mixed_ref, scr, pad, out):
    scr[...] = image_ref[...].astype(F32)
    pad[0:8, :] = jnp.zeros((8, 128), F32)
    pad[H + 8 : H + 16, :] = jnp.zeros((8, 128), F32)
    for cp in range(PAIRS):
        padded = pad_rows(scr[pl.ds(cp, H, stride=PAIRS), :].astype(BF16))
        mixed = tall_conv(padded, tall_ref[cp], 1).astype(BF16)
        mixed_ref[cp] = mixed
        pad[8 : H + 8, :] = mixed.astype(F32)
        out[pl.ds(cp, H, stride=PAIRS), :] = jnp.dot(
            moved_rows(pad, 1), wide_ref[cp], preferred_element_type=F32
        )
    conv_ref[...] = out[...].astype(BF16)


def beside_kernel(image_ref, wide_ref, shifted_ref, wide_out, scr):
    in_block = block_mask()
    wide = wide_ref[...]
    scr[...] = image_ref[...].astype(F32)
    for cp in range(PAIRS):
        padded = pad_rows(scr[pl.ds(cp, H, stride=PAIRS), :])
        for q in range(SHORT):
            shifted_ref[cp, q] = shifted(padded, q - 2).astype(BF16)
        wide_out[cp] = wide_matrices(wide, cp, in_block)


def fold(x, offset):
    total = None
    for i in range(0, x.shape[0], 8):
        part = pltpu.roll(x[i : i + 8], (offset - i) % 128, 1)
        total = part if total is None else total + part
    return total


def diagonal_sums(folds, count):
    total = folds[pl.ds(0, count, stride=8), :]
    for i in range(1, 8):
        total = total + pltpu.roll(folds[pl.ds(i, count, stride=8), :], 128 - i, 1)
    return total


def backward_kernel(
    scale,
    parts_ref,
    shifted_ref,
    mixed_ref,
    wide_ref,
    small_ref,
    d_mixed_ref,
    share_ref,
    d_scr,
    d_pad,
    m_pad,
    folds,
):
    total = None
    for i in range(CHIPS):
        part = parts_ref[i].astype(F32)
        d_scr[i * DATA : (i + 1) * DATA, :] = part[:DATA]
        total = part[DATA:] if total is None else total + part[DATA:]
    share_ref[0:OWN, :] = total.astype(BF16)
    for ref in (d_pad, m_pad):
        ref[0:8, :] = jnp.zeros((8, 128), F32)
        ref[H + 8 : H + 16, :] = jnp.zeros((8, 128), F32)
    row = lax.broadcasted_iota(jnp.int32, (BAND, 128), 0)
    lane = lax.broadcasted_iota(jnp.int32, (BAND, 128), 1)
    half = (LONG - 1) // 2
    low_band = (lane - row >= 7) & (lane - row <= 57)
    near = jnp.abs(lane % COLS - row) <= half
    low_near = near & (lane < COLS)
    high_near = near & (lane >= COLS)
    first = lax.broadcasted_iota(jnp.int32, (H, 128), 1) < COLS
    zero = jnp.zeros((H, 128), BF16)
    for cp in range(PAIRS):
        d_conv = d_scr[pl.ds(cp, H, stride=PAIRS), :]
        d_pad[8 : H + 8, :] = d_conv
        m_pad[8 : H + 8, :] = mixed_ref[cp].astype(F32)
        d_mixed = jnp.dot(
            moved_rows(d_pad, -1), wide_ref[cp], preferred_element_type=F32
        ).astype(BF16)
        d_mixed_ref[cp] = d_mixed
        corr = lax.dot_general(
            d_conv.astype(BF16),
            moved_rows(m_pad, 1),
            (((0,), (0,)), ((), ())),
            preferred_element_type=F32,
        )
        for p in range(SHORT):
            part = corr[:, p * 128 : (p + 1) * 128]
            part = jnp.where(low_near, part[:COLS], jnp.where(high_near, part[COLS:], 0.0))
            at = (20 + p * PAIRS + cp) * 8
            folds[at : at + 8, :] = fold(part, 7 + half)
        sides = []
        for c2 in range(2):
            own = jnp.where(first, d_mixed, zero) if c2 == 0 else jnp.where(first, zero, d_mixed)
            own = jnp.concatenate([own[b * BAND : (b + 1) * BAND] for b in range(H // BAND)], axis=1)
            windows = jnp.concatenate(
                [
                    jnp.concatenate(
                        [
                            shifted_ref[cp, q, b * BAND + at : b * BAND + at + BAND, :]
                            for b in range(H // BAND)
                        ],
                        axis=1,
                    )
                    for q in range(SHORT)
                    for at in ((0, BAND) if c2 == 0 else (BAND, 0))
                ],
                axis=0,
            )
            sides.append(
                lax.dot_general(
                    own, windows, (((1,), (1,)), ((), ())), preferred_element_type=F32
                )
            )
        for q in range(SHORT):
            low, high = (side[:, q * 128 : (q + 1) * 128] for side in sides)
            at = (q * PAIRS + cp) * 8
            folds[at : at + 8, :] = fold(jnp.where(low_band, low, high), 0)
    grads = diagonal_sums(folds, 40) * scale
    share_ref[OWN:SHARE, :] = jnp.concatenate([grads, small_ref[...]], axis=0).astype(BF16)


def d_image_kernel(d_mixed_ref, tall_ref, d_image_ref, out):
    taps = flipped(tall_ref)
    for cp in range(PAIRS):
        out[pl.ds(cp, H, stride=PAIRS), :] = tall_conv(
            pad_rows(d_mixed_ref[cp]), tall_matrices(taps, cp), -1
        )
    d_image_ref[...] = out[...].astype(BF16)


def mlp_kernel(
    scale,
    core_ref,
    conv_ref,
    image_ref,
    cot_ref,
    gain_ref,
    bias_ref,
    w_in_ref,
    b_in_ref,
    w_out_ref,
    b_out_ref,
    output_ref,
    theirs_ref,
    mine_ref,
    normed_ref,
    right_ref,
    small_ref,
    scr,
    out,
    small,
):
    core = core_ref[0]
    scr[...] = conv_ref[...].astype(F32)
    gain, bias = gain_ref[...], bias_ref[...]
    sums = [jnp.zeros((1, C), F32), jnp.zeros((1, C), F32), jnp.zeros((1, C), F32)]
    g_b_in = jnp.zeros((1, FF), F32)
    step = 2
    for k in range(0, ROWS, step):
        rows = slice(k * COLS, (k + step) * COLS)
        conv = jnp.concatenate(
            [
                untwisted(
                    [
                        scr[pl.ds(c * MSG + i * PAIRS + cp, CHIPS, stride=CORES * MSG), :]
                        for cp in range(PAIRS)
                        for c in range(CORES)
                    ]
                )
                for i in range(k, k + step)
            ],
            axis=0,
        )
        centred = conv - jnp.mean(conv, axis=1, keepdims=True)
        inverse = lax.rsqrt(jnp.mean(centred * centred, axis=1, keepdims=True) + epsilon)
        xhat = centred * inverse
        normed = (xhat * gain + bias).astype(BF16)
        normed_ref[rows, :] = normed
        pre_act = jnp.dot(normed, w_in_ref[...], preferred_element_type=F32) + b_in_ref[...]
        cdf = 0.5 * (1.0 + lax.erf(pre_act * 0.7071067811865476))
        hidden = (pre_act * cdf).astype(BF16)
        right_ref[1, rows, :] = hidden
        branch = jnp.dot(hidden, w_out_ref[...], preferred_element_type=F32) + b_out_ref[...]
        cot = cot_ref[rows, :]
        output_ref[rows, :] = (image_ref[rows, :].astype(F32) + branch).astype(BF16)
        d_hidden = lax.dot_general(
            cot, w_out_ref[...], (((1,), (1,)), ((), ())), preferred_element_type=F32
        )
        slope = cdf + pre_act * jnp.exp(-0.5 * pre_act * pre_act) * 0.3989422804014327
        d_pre = (d_hidden * slope).astype(BF16)
        right_ref[0, rows, :] = d_pre
        g_b_in = g_b_in + jnp.sum(d_pre.astype(F32), axis=0, keepdims=True)
        d_norm = lax.dot_general(
            d_pre, w_in_ref[...], (((1,), (1,)), ((), ())), preferred_element_type=F32
        )
        sums[0] = sums[0] + jnp.sum(d_norm * xhat, axis=0, keepdims=True)
        sums[1] = sums[1] + jnp.sum(d_norm, axis=0, keepdims=True)
        sums[2] = sums[2] + jnp.sum(cot.astype(F32), axis=0, keepdims=True)
        g = d_norm * gain
        d_conv = inverse * (
            g
            - jnp.mean(g, axis=1, keepdims=True)
            - xhat * jnp.mean(g * xhat, axis=1, keepdims=True)
        )
        for i in range(step):
            put_by_core(d_conv[i * COLS : (i + 1) * COLS], k + i, out)
    half = CHIPS * MSG
    theirs_ref[GRADS : GRADS + half, :] = out[pl.ds((1 - core) * half, half), :].astype(BF16)
    mine_ref[...] = out[pl.ds(core * half, half), :].astype(BF16)
    weight_grads(scale, normed_ref, cot_ref, right_ref, 1 - core, theirs_ref)
    small[...] = jnp.zeros((16, 128), F32)
    for i in range(FF // 128):
        small[i : i + 1, :] = g_b_in[:, i * 128 : (i + 1) * 128] * scale
    for n in range(3):
        for i in range(2):
            row = 8 + 2 * n + i
            small[row : row + 1, :] = sums[n][:, i * 128 : (i + 1) * 128] * scale
    small_ref[...] = small[pl.ds(core * 8, 8), :]
    other = small[pl.ds((1 - core) * 8, 8), :]
    theirs_ref[GRADS + half : GRADS + half + 16, :] = jnp.concatenate(
        [other, jnp.zeros((8, 128), F32)], axis=0
    ).astype(BF16)


def weight_grads(scale, normed_ref, cot_ref, right_ref, which, out_ref):
    for n, left_ref in enumerate((normed_ref, cot_ref)):

        @pl.when(which == n)
        def _(n=n, left_ref=left_ref):
            grads = lax.dot_general(
                left_ref[...], right_ref[n], (((0,), (0,)), ((), ())), preferred_element_type=F32
            )
            grads = (grads * scale).astype(out_ref.dtype)
            for i in range(CHIPS):
                for j in range(FF // 128):
                    at = (i * (FF // 128) + j) * 16
                    out_ref[at : at + 16, :] = grads[i * 16 : (i + 1) * 16, j * 128 : (j + 1) * 128]


def own_grads_kernel(scale, core_ref, normed_ref, cot_ref, right_ref, out_ref):
    weight_grads(scale, normed_ref, cot_ref, right_ref, core_ref[0], out_ref)


def merge_kernel(core_ref, mine_ref, grads_ref, small_ref, got_ref, out_hbm, small_out, rows_scr, sems):
    half = CHIPS * MSG
    mine = mine_ref[...].astype(F32)
    got = got_ref[GRADS : GRADS + half, :].astype(F32)
    other = got_ref[GRADS + half : GRADS + half + 16, :].astype(F32)
    small_out[...] = small_ref[...] + other[:8]
    low = core_ref[0] == 0
    one, two = jnp.where(low, mine, got), jnp.where(low, got, mine)
    copies = []
    for i in range(CHIPS):
        rows = slice(i * MSG, (i + 1) * MSG)
        rows_scr[i, 0:DATA, :] = jnp.concatenate([one[rows], two[rows]], axis=0).astype(BF16)
        rows = slice(i * OWN, (i + 1) * OWN)
        rows_scr[i, DATA : DATA + OWN, :] = (
            grads_ref[rows, :] + got_ref[rows, :].astype(F32)
        ).astype(BF16)
        if i % 4 == 3:
            part = pl.ds(i - 3, 4)
            copies.append(pltpu.make_async_copy(rows_scr.at[part], out_hbm.at[part], sems.at[i // 4]))
            copies[-1].start()
    for copy in copies:
        copy.wait()


def pair_sum_kernel(mine_ref, got_ref, out_ref):
    total = (mine_ref[...].astype(F32) + got_ref[...].astype(F32)).astype(BF16)
    for i in range(out_ref.shape[0]):
        out_ref[i] = total


def gather_kernel(parts_ref, d_image_ref, out_ref):
    total = parts_ref[0].astype(F32)
    for i in range(1, parts_ref.shape[0]):
        total = total + parts_ref[i].astype(F32)
    total = total.astype(BF16)
    for i in range(CHIPS):
        out_ref[i, 0:DATA, :] = d_image_ref[i * DATA : (i + 1) * DATA, :]
        out_ref[i, DATA : DATA + SHARE, :] = total


def place_share(core, ref, w_in_hbm, w_out_hbm, held, w_out, sems):
    lanes = FF // 128
    for i in range(CHIPS):
        part = ref[i, DATA : DATA + OWN, :].astype(F32)
        for j in range(lanes):
            held[i * 16 : (i + 1) * 16, j * 128 : (j + 1) * 128] = part[j * 16 : (j + 1) * 16]

    @pl.when(core == 0)
    def _():
        copy = pltpu.make_async_copy(held, w_in_hbm, sems.at[0])
        copy.start()
        copy.wait()

    @pl.when(core == 1)
    def _():
        copies = []
        for n in range(2):
            for j in range(n * lanes // 2, (n + 1) * lanes // 2):
                for half in range(2):
                    w_out[j * 128 : (j + 1) * 128, half * 128 : (half + 1) * 128] = held[
                        half * 128 : (half + 1) * 128, j * 128 : (j + 1) * 128
                    ].T
            rows = pl.ds(n * FF // 2, FF // 2)
            copies.append(pltpu.make_async_copy(w_out.at[rows], w_out_hbm.at[rows], sems.at[n]))
            copies[-1].start()
        for copy in copies:
            copy.wait()


def own_share_kernel(core_ref, mine_ref, w_in_hbm, w_out_hbm, held, w_out, sems):
    place_share(core_ref[0], mine_ref, w_in_hbm, w_out_hbm, held, w_out, sems)


def finish_kernel(
    core_ref,
    mine_ref,
    got_ref,
    cot_ref,
    w_in_in,
    w_out_in,
    out_ref,
    tall_ref,
    wide_ref,
    gain_ref,
    shift_ref,
    w_in_hbm,
    b_in_ref,
    w_out_hbm,
    b_out_ref,
    scr,
    held,
    w_out,
    sems,
):
    del w_in_in, w_out_in
    core = core_ref[0]
    rest = LAST - OWN
    for i in range(CHIPS):
        for c, ref in ((core, mine_ref), (1 - core, got_ref)):
            at = i * rest
            scr[c, at : at + DATA, :] = ref[i, 0:DATA, :].astype(F32)
            scr[c, at + DATA : at + rest, :] = ref[i, DATA + OWN : LAST, :].astype(F32)
    for k in range(ROWS):
        d_image = untwisted(
            [
                scr.at[c][pl.ds(core * MSG + k * PAIRS + cp, CHIPS, stride=rest), :]
                for cp in range(PAIRS)
                for c in range(CORES)
            ]
        )
        out_ref[k] = (cot_ref[k].astype(F32) + d_image).astype(BF16)
    for q in range(SHORT):
        for start, ref in ((0, tall_ref), (20, wide_ref)):
            ref[q] = untwisted(
                [
                    scr.at[c][pl.ds(DATA + start + q * PAIRS + cp, CHIPS, stride=rest), :]
                    for cp in range(PAIRS)
                    for c in range(CORES)
                ]
            )[7 : 7 + LONG]
    totals = []
    for c in range(CORES):
        total = None
        for i in range(CHIPS):
            part = scr[c, (i + 1) * rest - 8 : (i + 1) * rest, :]
            total = part if total is None else total + part
        totals.append(total)
    for i in range(FF // 128):
        b_in_ref[:, i * 128 : (i + 1) * 128] = totals[0][i : i + 1]
    for n, ref in enumerate((gain_ref, shift_ref, b_out_ref)):
        for i in range(2):
            ref[:, i * 128 : (i + 1) * 128] = totals[1][2 * n + i : 2 * n + i + 1]
    place_share(1 - core, got_ref, w_in_hbm, w_out_hbm, held, w_out, sems)


def messages(x):
    x = lax.all_to_all(x.reshape(STRIPS, MSG, 128), "strip", 0, 0, tiled=True)
    return x.reshape(STRIPS * MSG, 128)


def between_chips(x):
    groups = [[CORES * i + c for i in range(CHIPS)] for c in range(CORES)]
    return lax.all_to_all(x, "strip", 0, 0, axis_index_groups=groups, tiled=True)


def between_cores(x):
    return lax.ppermute(x, "strip", [(i, i ^ 1) for i in range(STRIPS)])


def shape(dims, dtype):
    return jax.ShapeDtypeStruct(dims, dtype)


def local(
    image,
    cotangent,
    kernel_tall,
    kernel_wide,
    layer_norm_gain,
    layer_norm_bias,
    w_in,
    b_in,
    w_out,
    b_out,
):
    source = image[0]
    upstream = cotangent[0]
    slides = lax.axis_size("slide")
    scale = float(CELLS * slides * STRIPS) ** (-0.5)
    packed_f = pltpu.VMEM((STRIPS * MSG, 128), F32)
    packed_b = shape((STRIPS * MSG, 128), BF16)
    edge = pltpu.VMEM((H + 16, 128), F32)

    image_msg = call(
        pack_kernel,
        packed_b,
        [packed_f],
    )(image)
    me = lax.axis_index("strip")
    core = (me % CORES).reshape(1)
    me = (me % CORES) * CHIPS + me // CORES
    own = jnp.arange(8)[:, None] * STRIPS + me == jnp.arange(C)[None, :]
    own = own.astype(BF16)

    def taps(kernel, spec):
        picked = jnp.einsum(spec, kernel, own, preferred_element_type=F32)
        picked = picked.reshape(SHORT * 8, LONG)
        return jnp.pad(picked, ((0, 0), (0, 128 - LONG)))

    tall = taps(kernel_tall, "pqc,kc->qkp")
    wide = taps(kernel_wide, "pqc,kc->pkq")
    tall_fwd, wide_fwd = call(
        matrix_kernel, (shape((PAIRS, SHORT * BAND, C), BF16), shape((PAIRS, SHORT * 128, 128), BF16))
    )(tall, wide)

    image_ch = messages(image_msg)
    conv_ch, mixed = call(
        forward_kernel,
        (
            packed_b,
            shape((PAIRS, H, 128), BF16),
        ),
        [packed_f, edge, packed_f],
    )(image_ch, tall_fwd, wide_fwd)
    conv = messages(conv_ch)
    output, theirs, mine, normed, right, small = call(
        functools.partial(mlp_kernel, scale),
        (
            shape((CELLS, C), BF16),
            shape((GRADS + CHIPS * MSG + 16, 128), BF16),
            shape((CHIPS * MSG, 128), BF16),
            shape((CELLS, C), BF16),
            shape((2, CELLS, FF), BF16),
            shape((8, 128), F32),
        ),
        [packed_f, packed_f, pltpu.VMEM((16, 128), F32)],
        [SMEM] + [VMEM] * 9,
    )(
        core,
        conv,
        source.reshape(CELLS, C),
        upstream.reshape(CELLS, C),
        layer_norm_gain[None],
        layer_norm_bias[None],
        w_in,
        b_in[None],
        w_out,
        b_out[None],
    )
    got = between_cores(theirs)
    chip_grads = call(
        functools.partial(own_grads_kernel, scale), shape((GRADS, 128), F32), (), [SMEM] + [VMEM] * 3
    )(core, normed, upstream.reshape(CELLS, C), right)
    merged, small = call(
        merge_kernel,
        (shape((CHIPS, DATA + OWN, 128), BF16), shape((8, 128), F32)),
        [pltpu.VMEM((CHIPS, DATA + OWN, 128), BF16), pltpu.SemaphoreType.DMA((4,))],
        [SMEM] + [VMEM] * 4,
        (HBM, VMEM),
    )(core, mine, chip_grads, small, got)
    shifts, wide_bwd = call(
        beside_kernel,
        (shape((PAIRS, SHORT, H + 2 * REACH, 128), BF16), shape((PAIRS, SHORT * 128, 128), BF16)),
        [packed_f],
    )(image_ch, wide)
    d_mixed, share = call(
        functools.partial(backward_kernel, scale),
        (shape((PAIRS, H, 128), BF16), shape((SHARE, 128), BF16)),
        [packed_f, edge, edge, pltpu.VMEM((40 * 8, 128), F32)],
    )(between_chips(merged), shifts, mixed, wide_bwd, small)
    got = lax.ppermute(share, "slide", [(i, i ^ 1) for i in range(slides)])
    d_image_msg = call(d_image_kernel, packed_b, [packed_f])(d_mixed, tall)
    half = slides // 2
    got, d_image_msg = lax.optimization_barrier((got, d_image_msg))
    copies = call(pair_sum_kernel, shape((half, SHARE, 128), BF16))(share, got)
    groups = [[2 * i + j for i in range(half)] for j in range(2)]
    parts = lax.all_to_all(copies, "slide", 0, 0, axis_index_groups=groups, tiled=True)
    last = call(gather_kernel, shape((CHIPS, LAST, 128), BF16))(parts, d_image_msg)
    last = between_chips(last)
    got = between_cores(last)
    held = [pltpu.VMEM((C, FF), F32), pltpu.VMEM((FF, C), F32), pltpu.SemaphoreType.DMA((2,))]
    g_w_in, g_w_out = call(
        own_share_kernel,
        (shape((C, FF), F32), shape((FF, C), F32)),
        held,
        [SMEM, VMEM],
        (HBM, HBM),
    )(core, last)
    grad_image, g_tall, g_wide, g_gain, g_shift, g_w_in, g_b_in, g_w_out, g_b_out = call(
        finish_kernel,
        (
            shape((ROWS, COLS, C), BF16),
            shape((SHORT, LONG, C), F32),
            shape((SHORT, LONG, C), F32),
            shape((1, C), F32),
            shape((1, C), F32),
            shape((C, FF), F32),
            shape((1, FF), F32),
            shape((FF, C), F32),
            shape((1, C), F32),
        ),
        [pltpu.VMEM((CORES, CHIPS * (LAST - OWN), 128), F32)] + held,
        [SMEM] + [VMEM] * 3 + [HBM] * 2,
        (VMEM,) * 5 + (HBM, VMEM, HBM, VMEM),
        {4: 5, 5: 7},
    )(core, last, got, upstream, g_w_in, g_w_out)
    return (
        output.reshape(image.shape),
        grad_image[None],
        jnp.transpose(g_tall, (1, 0, 2)),
        g_wide,
        g_gain[0],
        g_shift[0],
        g_w_in,
        g_b_in[0],
        g_w_out,
        g_b_out[0],
    )


def solution(mesh):
    cells = P("slide", "strip", None, None)
    return jax.shard_map(
        local,
        mesh=mesh,
        in_specs=(cells, cells) + (P(),) * 8,
        out_specs=(cells, cells) + (P(),) * 8,
        check_vma=False,
    )
```

```python
import functools

import jax
import jax.numpy as jnp
from jax import lax
from jax.experimental import pallas as pl
from jax.experimental.pallas import tpu as pltpu
from jax.sharding import PartitionSpec as P

F32 = jnp.float32
BF16 = jnp.bfloat16
CORES = 2
CHIPS = 16
STRIPS = CORES * CHIPS
ROWS = 6
COLS = 64
H = STRIPS * ROWS
C = 256
FF = 1024
LONG = 51
SHORT = 5
PAIRS = 4
BAND = 64
REACH = 32
MSG = ROWS * PAIRS
CELLS = ROWS * COLS
DATA = CORES * MSG
GRADS = C * FF // 128
OWN = GRADS // CHIPS
SHARE = OWN + 48
LAST = DATA + SHARE
epsilon = 1e-06

PARAMS = pltpu.CompilerParams(vmem_limit_bytes=24 * 1024 * 1024)


VMEM = pl.BlockSpec(memory_space=pltpu.VMEM)
SMEM = pl.BlockSpec(memory_space=pltpu.SMEM)
HBM = pl.BlockSpec(memory_space=pltpu.HBM)


def call(kernel, out_shape, scratch=(), in_specs=None, out_specs=None, aliases=None):
    specs = {}
    if in_specs is not None:
        specs["in_specs"] = in_specs
    if out_specs is not None:
        specs["out_specs"] = out_specs
    if aliases is not None:
        specs["input_output_aliases"] = aliases
    return pl.pallas_call(
        kernel,
        out_shape=out_shape,
        scratch_shapes=list(scratch),
        compiler_params=PARAMS,
        **specs,
    )


def turned_rows(block):
    return jnp.concatenate([block[:, :128], block[:, 128:]], axis=0).T


def put_by_strip(block, k, scr):
    rows = turned_rows(block)
    for cp in range(PAIRS):
        for core in range(CORES):
            first = cp * STRIPS + core * CHIPS
            at = pl.ds(core * MSG + k * PAIRS + cp, CHIPS, stride=CORES * MSG)
            scr[at, :] = rows[first : first + CHIPS]


def put_by_core(block, k, scr):
    rows = turned_rows(block)
    for cp in range(PAIRS):
        scr[pl.ds(k * PAIRS + cp, STRIPS, stride=MSG), :] = rows[cp * STRIPS : (cp + 1) * STRIPS]


def untwisted(parts):
    rows = jnp.concatenate(parts, axis=0).T
    return jnp.concatenate([rows[:COLS], rows[COLS:]], axis=1)


def half_masks(shape):
    lane = lax.broadcasted_iota(jnp.int32, shape, len(shape) - 1)
    return lane, lane < COLS


def shifted(x, by):
    if by == 0:
        return x
    column = lax.broadcasted_iota(jnp.int32, x.shape, 1) % COLS + by
    return jnp.where((column >= 0) & (column < COLS), pltpu.roll(x, (-by) % 128, 1), 0.0)


def sloped(row, first_shift, count):
    eight = pltpu.roll(jnp.broadcast_to(row, (8, 128)), 0, 1, stride=1, stride_axis=0)
    return jnp.concatenate(
        [pltpu.roll(eight, (first_shift + i) % 128, 1) for i in range(0, count, 8)], axis=0
    )


def tall_matrix(taps_ref, q, c):
    return sloped(taps_ref[q * 8 + c : q * 8 + c + 1, :], REACH - (LONG - 1) // 2, BAND)


def wide_matrix(taps_ref, p, cp, in_block):
    first = -((LONG - 1) // 2)
    turned = jnp.concatenate(
        [
            sloped(taps_ref[n : n + 1, :], first + COLS * c2, COLS)
            for c2, n in enumerate((p * 8 + cp, p * 8 + 4 + cp))
        ],
        axis=0,
    )
    return jnp.where(in_block, turned, 0.0)


def block_mask():
    row = lax.broadcasted_iota(jnp.int32, (128, 128), 0)
    lane = lax.broadcasted_iota(jnp.int32, (128, 128), 1)
    return (row < COLS) == (lane < COLS)


def tall_conv(padded, matrix, sign):
    _, first = half_masks((128, 128))
    zero = jnp.zeros((128, 128), BF16)
    sides = []
    for b in range(H // BAND):
        window = padded[b * BAND : b * BAND + 128]
        sides.append(
            jnp.concatenate([jnp.where(first, window, zero), jnp.where(first, zero, window)], axis=0)
        )
    product = jnp.dot(matrix, jnp.concatenate(sides, axis=1), preferred_element_type=F32)
    bands = []
    for b in range(H // BAND):
        total = None
        for q in range(SHORT):
            part = product[q * BAND : (q + 1) * BAND, b * 128 : (b + 1) * 128]
            part = shifted(part, sign * (q - 2))
            total = part if total is None else total + part
        bands.append(total)
    return jnp.concatenate(bands, axis=0)


def moved_rows(scr, sign):
    return jnp.concatenate(
        [scr[8 + sign * (p - 2) : 8 + sign * (p - 2) + H, :].astype(BF16) for p in range(SHORT)],
        axis=1,
    )


def flipped(taps_ref):
    a = lax.broadcasted_iota(jnp.int32, (128, 128), 0)
    b = lax.broadcasted_iota(jnp.int32, (128, 128), 1)
    turn = (a + b == LONG - 1).astype(BF16)
    return jnp.dot(taps_ref[...].astype(BF16), turn, preferred_element_type=F32)


def tall_matrices(taps, cp):
    return jnp.concatenate(
        [
            jnp.concatenate([tall_matrix(taps, q, c2 * 4 + cp) for c2 in range(2)], axis=1)
            for q in range(SHORT)
        ],
        axis=0,
    ).astype(BF16)


def wide_matrices(taps, cp, in_block):
    return jnp.concatenate(
        [wide_matrix(taps, p, cp, in_block) for p in range(SHORT)], axis=0
    ).astype(BF16)


def matrix_kernel(tall_ref, wide_ref, tall_out, wide_out):
    in_block = block_mask()
    tall, wide = tall_ref[...], flipped(wide_ref)
    for cp in range(PAIRS):
        tall_out[cp] = tall_matrices(tall, cp)
        wide_out[cp] = wide_matrices(wide, cp, in_block)


def pad_rows(x):
    zero = jnp.zeros((REACH, 128), x.dtype)
    return jnp.concatenate([zero, x, zero], axis=0)


def pack_kernel(image_ref, out_ref, scr):
    for k in range(ROWS):
        put_by_strip(image_ref[0, k].astype(F32), k, scr)
    out_ref[...] = scr[...].astype(BF16)


def forward_kernel(image_ref, tall_ref, wide_ref, conv_ref, mixed_ref, scr, pad, out):
    scr[...] = image_ref[...].astype(F32)
    pad[0:8, :] = jnp.zeros((8, 128), F32)
    pad[H + 8 : H + 16, :] = jnp.zeros((8, 128), F32)
    for cp in range(PAIRS):
        padded = pad_rows(scr[pl.ds(cp, H, stride=PAIRS), :].astype(BF16))
        mixed = tall_conv(padded, tall_ref[cp], 1).astype(BF16)
        mixed_ref[cp] = mixed
        pad[8 : H + 8, :] = mixed.astype(F32)
        out[pl.ds(cp, H, stride=PAIRS), :] = jnp.dot(
            moved_rows(pad, 1), wide_ref[cp], preferred_element_type=F32
        )
    conv_ref[...] = out[...].astype(BF16)


def beside_kernel(image_ref, wide_ref, shifted_ref, wide_out, scr):
    in_block = block_mask()
    wide = wide_ref[...]
    scr[...] = image_ref[...].astype(F32)
    for cp in range(PAIRS):
        padded = pad_rows(scr[pl.ds(cp, H, stride=PAIRS), :])
        for q in range(SHORT):
            shifted_ref[cp, q] = shifted(padded, q - 2).astype(BF16)
        wide_out[cp] = wide_matrices(wide, cp, in_block)


def fold(x, offset):
    total = None
    for i in range(0, x.shape[0], 8):
        part = pltpu.roll(x[i : i + 8], (offset - i) % 128, 1)
        total = part if total is None else total + part
    return total


def diagonal_sums(folds, count):
    total = folds[pl.ds(0, count, stride=8), :]
    for i in range(1, 8):
        total = total + pltpu.roll(folds[pl.ds(i, count, stride=8), :], 128 - i, 1)
    return total


def backward_kernel(
    scale,
    parts_ref,
    shifted_ref,
    mixed_ref,
    wide_ref,
    small_ref,
    d_mixed_ref,
    share_ref,
    d_scr,
    d_pad,
    m_pad,
    folds,
):
    total = None
    for i in range(CHIPS):
        part = parts_ref[i].astype(F32)
        d_scr[i * DATA : (i + 1) * DATA, :] = part[:DATA]
        total = part[DATA:] if total is None else total + part[DATA:]
    share_ref[0:OWN, :] = total.astype(BF16)
    for ref in (d_pad, m_pad):
        ref[0:8, :] = jnp.zeros((8, 128), F32)
        ref[H + 8 : H + 16, :] = jnp.zeros((8, 128), F32)
    row = lax.broadcasted_iota(jnp.int32, (BAND, 128), 0)
    lane = lax.broadcasted_iota(jnp.int32, (BAND, 128), 1)
    half = (LONG - 1) // 2
    low_band = (lane - row >= 7) & (lane - row <= 57)
    near = jnp.abs(lane % COLS - row) <= half
    low_near = near & (lane < COLS)
    high_near = near & (lane >= COLS)
    first = lax.broadcasted_iota(jnp.int32, (H, 128), 1) < COLS
    zero = jnp.zeros((H, 128), BF16)
    for cp in range(PAIRS):
        d_conv = d_scr[pl.ds(cp, H, stride=PAIRS), :]
        d_pad[8 : H + 8, :] = d_conv
        m_pad[8 : H + 8, :] = mixed_ref[cp].astype(F32)
        d_mixed = jnp.dot(
            moved_rows(d_pad, -1), wide_ref[cp], preferred_element_type=F32
        ).astype(BF16)
        d_mixed_ref[cp] = d_mixed
        corr = lax.dot_general(
            d_conv.astype(BF16),
            moved_rows(m_pad, 1),
            (((0,), (0,)), ((), ())),
            preferred_element_type=F32,
        )
        for p in range(SHORT):
            part = corr[:, p * 128 : (p + 1) * 128]
            part = jnp.where(low_near, part[:COLS], jnp.where(high_near, part[COLS:], 0.0))
            at = (20 + p * PAIRS + cp) * 8
            folds[at : at + 8, :] = fold(part, 7 + half)
        sides = []
        for c2 in range(2):
            own = jnp.where(first, d_mixed, zero) if c2 == 0 else jnp.where(first, zero, d_mixed)
            own = jnp.concatenate([own[b * BAND : (b + 1) * BAND] for b in range(H // BAND)], axis=1)
            windows = jnp.concatenate(
                [
                    jnp.concatenate(
                        [
                            shifted_ref[cp, q, b * BAND + at : b * BAND + at + BAND, :]
                            for b in range(H // BAND)
                        ],
                        axis=1,
                    )
                    for q in range(SHORT)
                    for at in ((0, BAND) if c2 == 0 else (BAND, 0))
                ],
                axis=0,
            )
            sides.append(
                lax.dot_general(
                    own, windows, (((1,), (1,)), ((), ())), preferred_element_type=F32
                )
            )
        for q in range(SHORT):
            low, high = (side[:, q * 128 : (q + 1) * 128] for side in sides)
            at = (q * PAIRS + cp) * 8
            folds[at : at + 8, :] = fold(jnp.where(low_band, low, high), 0)
    grads = diagonal_sums(folds, 40) * scale
    share_ref[OWN:SHARE, :] = jnp.concatenate([grads, small_ref[...]], axis=0).astype(BF16)


def d_image_kernel(d_mixed_ref, tall_ref, d_image_ref, out):
    taps = flipped(tall_ref)
    for cp in range(PAIRS):
        out[pl.ds(cp, H, stride=PAIRS), :] = tall_conv(
            pad_rows(d_mixed_ref[cp]), tall_matrices(taps, cp), -1
        )
    d_image_ref[...] = out[...].astype(BF16)


def mlp_kernel(
    scale,
    core_ref,
    conv_ref,
    image_ref,
    cot_ref,
    gain_ref,
    bias_ref,
    w_in_ref,
    b_in_ref,
    w_out_ref,
    b_out_ref,
    output_ref,
    theirs_ref,
    mine_ref,
    normed_ref,
    right_ref,
    small_ref,
    scr,
    out,
    small,
    left,
):
    core = core_ref[0]
    scr[...] = conv_ref[...].astype(F32)
    gain, bias = gain_ref[...], bias_ref[...]
    sums = [jnp.zeros((1, C), F32), jnp.zeros((1, C), F32), jnp.zeros((1, C), F32)]
    g_b_in = jnp.zeros((1, FF), F32)
    step = 2
    for k in range(0, ROWS, step):
        rows = slice(k * COLS, (k + step) * COLS)
        conv = jnp.concatenate(
            [
                untwisted(
                    [
                        scr[pl.ds(c * MSG + i * PAIRS + cp, CHIPS, stride=CORES * MSG), :]
                        for cp in range(PAIRS)
                        for c in range(CORES)
                    ]
                )
                for i in range(k, k + step)
            ],
            axis=0,
        )
        centred = conv - jnp.mean(conv, axis=1, keepdims=True)
        inverse = lax.rsqrt(jnp.mean(centred * centred, axis=1, keepdims=True) + epsilon)
        xhat = centred * inverse
        normed = (xhat * gain + bias).astype(BF16)
        normed_ref[rows, :] = normed
        left[0, rows, :] = normed
        pre_act = jnp.dot(normed, w_in_ref[...], preferred_element_type=F32) + b_in_ref[...]
        cdf = 0.5 * (1.0 + lax.erf(pre_act * 0.7071067811865476))
        hidden = (pre_act * cdf).astype(BF16)
        right_ref[1, rows, :] = hidden
        branch = jnp.dot(hidden, w_out_ref[...], preferred_element_type=F32) + b_out_ref[...]
        cot = cot_ref[rows, :]
        left[1, rows, :] = cot
        output_ref[rows, :] = (image_ref[rows, :].astype(F32) + branch).astype(BF16)
        d_hidden = lax.dot_general(
            cot, w_out_ref[...], (((1,), (1,)), ((), ())), preferred_element_type=F32
        )
        slope = cdf + pre_act * jnp.exp(-0.5 * pre_act * pre_act) * 0.3989422804014327
        d_pre = (d_hidden * slope).astype(BF16)
        right_ref[0, rows, :] = d_pre
        g_b_in = g_b_in + jnp.sum(d_pre.astype(F32), axis=0, keepdims=True)
        d_norm = lax.dot_general(
            d_pre, w_in_ref[...], (((1,), (1,)), ((), ())), preferred_element_type=F32
        )
        sums[0] = sums[0] + jnp.sum(d_norm * xhat, axis=0, keepdims=True)
        sums[1] = sums[1] + jnp.sum(d_norm, axis=0, keepdims=True)
        sums[2] = sums[2] + jnp.sum(cot.astype(F32), axis=0, keepdims=True)
        g = d_norm * gain
        d_conv = inverse * (
            g
            - jnp.mean(g, axis=1, keepdims=True)
            - xhat * jnp.mean(g * xhat, axis=1, keepdims=True)
        )
        for i in range(step):
            put_by_core(d_conv[i * COLS : (i + 1) * COLS], k + i, out)
    half = CHIPS * MSG
    theirs_ref[GRADS : GRADS + half, :] = out[pl.ds((1 - core) * half, half), :].astype(BF16)
    mine_ref[...] = out[pl.ds(core * half, half), :].astype(BF16)
    put_grads(over_cells(left[1 - core], right_ref[1 - core]), scale, theirs_ref)
    small[...] = jnp.zeros((16, 128), F32)
    for i in range(FF // 128):
        small[i : i + 1, :] = g_b_in[:, i * 128 : (i + 1) * 128] * scale
    for n in range(3):
        for i in range(2):
            row = 8 + 2 * n + i
            small[row : row + 1, :] = sums[n][:, i * 128 : (i + 1) * 128] * scale
    small_ref[...] = small[pl.ds(core * 8, 8), :]
    other = small[pl.ds((1 - core) * 8, 8), :]
    theirs_ref[GRADS + half : GRADS + half + 16, :] = jnp.concatenate(
        [other, jnp.zeros((8, 128), F32)], axis=0
    ).astype(BF16)


def put_grads(grads, scale, out_ref):
    grads = (grads * scale).astype(out_ref.dtype)
    for i in range(CHIPS):
        for j in range(FF // 128):
            at = (i * (FF // 128) + j) * 16
            out_ref[at : at + 16, :] = grads[i * 16 : (i + 1) * 16, j * 128 : (j + 1) * 128]


def over_cells(left, right):
    return lax.dot_general(left, right, (((0,), (0,)), ((), ())), preferred_element_type=F32)


def own_grads_kernel(scale, core_ref, normed_ref, cot_ref, right_ref, out_ref):
    for n, left_ref in enumerate((normed_ref, cot_ref)):

        @pl.when(core_ref[0] == n)
        def _(n=n, left_ref=left_ref):
            put_grads(over_cells(left_ref[...], right_ref[n]), scale, out_ref)


def merge_kernel(core_ref, mine_ref, grads_ref, small_ref, got_ref, out_hbm, small_out, rows_scr, sems):
    half = CHIPS * MSG
    mine = mine_ref[...].astype(F32)
    got = got_ref[GRADS : GRADS + half, :].astype(F32)
    other = got_ref[GRADS + half : GRADS + half + 16, :].astype(F32)
    small_out[...] = small_ref[...] + other[:8]
    low = core_ref[0] == 0
    one, two = jnp.where(low, mine, got), jnp.where(low, got, mine)
    copies = []
    for i in range(CHIPS):
        rows = slice(i * MSG, (i + 1) * MSG)
        rows_scr[i, 0:DATA, :] = jnp.concatenate([one[rows], two[rows]], axis=0).astype(BF16)
        rows = slice(i * OWN, (i + 1) * OWN)
        rows_scr[i, DATA : DATA + OWN, :] = (
            grads_ref[rows, :] + got_ref[rows, :].astype(F32)
        ).astype(BF16)
        if i % 4 == 3:
            part = pl.ds(i - 3, 4)
            copies.append(pltpu.make_async_copy(rows_scr.at[part], out_hbm.at[part], sems.at[i // 4]))
            copies[-1].start()
    for copy in copies:
        copy.wait()


def pair_sum_kernel(mine_ref, got_ref, out_ref):
    total = (mine_ref[...].astype(F32) + got_ref[...].astype(F32)).astype(BF16)
    for i in range(out_ref.shape[0]):
        out_ref[i] = total


def gather_kernel(parts_ref, d_image_ref, out_ref):
    total = parts_ref[0].astype(F32)
    for i in range(1, parts_ref.shape[0]):
        total = total + parts_ref[i].astype(F32)
    total = total.astype(BF16)
    for i in range(CHIPS):
        out_ref[i, 0:DATA, :] = d_image_ref[i * DATA : (i + 1) * DATA, :]
        out_ref[i, DATA : DATA + SHARE, :] = total


def place_share(core, ref, w_in_hbm, w_out_hbm, held, w_out, sems):
    lanes = FF // 128
    for i in range(CHIPS):
        part = ref[i, DATA : DATA + OWN, :].astype(F32)
        for j in range(lanes):
            held[i * 16 : (i + 1) * 16, j * 128 : (j + 1) * 128] = part[j * 16 : (j + 1) * 16]

    @pl.when(core == 0)
    def _():
        pltpu.make_async_copy(held, w_in_hbm, sems.at[0]).start()

    @pl.when(core == 1)
    def _():
        for n in range(2):
            for j in range(n * lanes // 2, (n + 1) * lanes // 2):
                for half in range(2):
                    w_out[j * 128 : (j + 1) * 128, half * 128 : (half + 1) * 128] = held[
                        half * 128 : (half + 1) * 128, j * 128 : (j + 1) * 128
                    ].T
            rows = pl.ds(n * FF // 2, FF // 2)
            pltpu.make_async_copy(w_out.at[rows], w_out_hbm.at[rows], sems.at[n]).start()


def placed_share(core, w_in_hbm, w_out_hbm, held, w_out, sems):
    @pl.when(core == 0)
    def _():
        pltpu.make_async_copy(held, w_in_hbm, sems.at[0]).wait()

    @pl.when(core == 1)
    def _():
        for n in range(2):
            rows = pl.ds(n * FF // 2, FF // 2)
            pltpu.make_async_copy(w_out.at[rows], w_out_hbm.at[rows], sems.at[n]).wait()


def own_share_kernel(core_ref, mine_ref, w_in_hbm, w_out_hbm, held, w_out, sems):
    place_share(core_ref[0], mine_ref, w_in_hbm, w_out_hbm, held, w_out, sems)
    placed_share(core_ref[0], w_in_hbm, w_out_hbm, held, w_out, sems)


def finish_kernel(
    core_ref,
    mine_ref,
    got_ref,
    cot_ref,
    w_in_in,
    w_out_in,
    out_ref,
    tall_ref,
    wide_ref,
    gain_ref,
    shift_ref,
    w_in_hbm,
    b_in_ref,
    w_out_hbm,
    b_out_ref,
    scr,
    held,
    w_out,
    sems,
):
    del w_in_in, w_out_in
    core = core_ref[0]
    place_share(1 - core, got_ref, w_in_hbm, w_out_hbm, held, w_out, sems)
    rest = LAST - OWN
    for i in range(CHIPS):
        for c, ref in ((core, mine_ref), (1 - core, got_ref)):
            at = i * rest
            scr[c, at : at + DATA, :] = ref[i, 0:DATA, :].astype(F32)
            scr[c, at + DATA : at + rest, :] = ref[i, DATA + OWN : LAST, :].astype(F32)
    for k in range(ROWS):
        d_image = untwisted(
            [
                scr.at[c][pl.ds(core * MSG + k * PAIRS + cp, CHIPS, stride=rest), :]
                for cp in range(PAIRS)
                for c in range(CORES)
            ]
        )
        out_ref[k] = (cot_ref[k].astype(F32) + d_image).astype(BF16)
    for q in range(SHORT):
        for start, ref in ((0, tall_ref), (20, wide_ref)):
            ref[q] = untwisted(
                [
                    scr.at[c][pl.ds(DATA + start + q * PAIRS + cp, CHIPS, stride=rest), :]
                    for cp in range(PAIRS)
                    for c in range(CORES)
                ]
            )[7 : 7 + LONG]
    totals = []
    for c in range(CORES):
        total = None
        for i in range(CHIPS):
            part = scr[c, (i + 1) * rest - 8 : (i + 1) * rest, :]
            total = part if total is None else total + part
        totals.append(total)
    for i in range(FF // 128):
        b_in_ref[:, i * 128 : (i + 1) * 128] = totals[0][i : i + 1]
    for n, ref in enumerate((gain_ref, shift_ref, b_out_ref)):
        for i in range(2):
            ref[:, i * 128 : (i + 1) * 128] = totals[1][2 * n + i : 2 * n + i + 1]
    placed_share(1 - core, w_in_hbm, w_out_hbm, held, w_out, sems)


def messages(x):
    x = lax.all_to_all(x.reshape(STRIPS, MSG, 128), "strip", 0, 0, tiled=True)
    return x.reshape(STRIPS * MSG, 128)


def between_chips(x):
    groups = [[CORES * i + c for i in range(CHIPS)] for c in range(CORES)]
    return lax.all_to_all(x, "strip", 0, 0, axis_index_groups=groups, tiled=True)


def between_cores(x):
    return lax.ppermute(x, "strip", [(i, i ^ 1) for i in range(STRIPS)])


def shape(dims, dtype):
    return jax.ShapeDtypeStruct(dims, dtype)


def local(
    image,
    cotangent,
    kernel_tall,
    kernel_wide,
    layer_norm_gain,
    layer_norm_bias,
    w_in,
    b_in,
    w_out,
    b_out,
):
    source = image[0]
    upstream = cotangent[0]
    slides = lax.axis_size("slide")
    scale = float(CELLS * slides * STRIPS) ** (-0.5)
    packed_f = pltpu.VMEM((STRIPS * MSG, 128), F32)
    packed_b = shape((STRIPS * MSG, 128), BF16)
    edge = pltpu.VMEM((H + 16, 128), F32)

    image_msg = call(
        pack_kernel,
        packed_b,
        [packed_f],
    )(image)
    me = lax.axis_index("strip")
    core = (me % CORES).reshape(1)
    me = (me % CORES) * CHIPS + me // CORES
    own = jnp.arange(8)[:, None] * STRIPS + me == jnp.arange(C)[None, :]
    own = own.astype(BF16)

    def taps(kernel, spec):
        picked = jnp.einsum(spec, kernel, own, preferred_element_type=F32)
        picked = picked.reshape(SHORT * 8, LONG)
        return jnp.pad(picked, ((0, 0), (0, 128 - LONG)))

    tall = taps(kernel_tall, "pqc,kc->qkp")
    wide = taps(kernel_wide, "pqc,kc->pkq")
    tall_fwd, wide_fwd = call(
        matrix_kernel, (shape((PAIRS, SHORT * BAND, C), BF16), shape((PAIRS, SHORT * 128, 128), BF16))
    )(tall, wide)

    image_ch = messages(image_msg)
    conv_ch, mixed = call(
        forward_kernel,
        (
            packed_b,
            shape((PAIRS, H, 128), BF16),
        ),
        [packed_f, edge, packed_f],
    )(image_ch, tall_fwd, wide_fwd)
    conv = messages(conv_ch)
    output, theirs, mine, normed, right, small = call(
        functools.partial(mlp_kernel, scale),
        (
            shape((CELLS, C), BF16),
            shape((GRADS + CHIPS * MSG + 16, 128), BF16),
            shape((CHIPS * MSG, 128), BF16),
            shape((CELLS, C), BF16),
            shape((2, CELLS, FF), BF16),
            shape((8, 128), F32),
        ),
        [packed_f, packed_f, pltpu.VMEM((16, 128), F32), pltpu.VMEM((2, CELLS, C), BF16)],
        [SMEM] + [VMEM] * 9,
    )(
        core,
        conv,
        source.reshape(CELLS, C),
        upstream.reshape(CELLS, C),
        layer_norm_gain[None],
        layer_norm_bias[None],
        w_in,
        b_in[None],
        w_out,
        b_out[None],
    )
    got = between_cores(theirs)
    chip_grads = call(
        functools.partial(own_grads_kernel, scale), shape((GRADS, 128), F32), (), [SMEM] + [VMEM] * 3
    )(core, normed, upstream.reshape(CELLS, C), right)
    merged, small = call(
        merge_kernel,
        (shape((CHIPS, DATA + OWN, 128), BF16), shape((8, 128), F32)),
        [pltpu.VMEM((CHIPS, DATA + OWN, 128), BF16), pltpu.SemaphoreType.DMA((4,))],
        [SMEM] + [VMEM] * 4,
        (HBM, VMEM),
    )(core, mine, chip_grads, small, got)
    shifts, wide_bwd = call(
        beside_kernel,
        (shape((PAIRS, SHORT, H + 2 * REACH, 128), BF16), shape((PAIRS, SHORT * 128, 128), BF16)),
        [packed_f],
    )(image_ch, wide)
    d_mixed, share = call(
        functools.partial(backward_kernel, scale),
        (shape((PAIRS, H, 128), BF16), shape((SHARE, 128), BF16)),
        [packed_f, edge, edge, pltpu.VMEM((40 * 8, 128), F32)],
    )(between_chips(merged), shifts, mixed, wide_bwd, small)
    got = lax.ppermute(share, "slide", [(i, i ^ 1) for i in range(slides)])
    d_image_msg = call(d_image_kernel, packed_b, [packed_f])(d_mixed, tall)
    half = slides // 2
    got, d_image_msg = lax.optimization_barrier((got, d_image_msg))
    copies = call(pair_sum_kernel, shape((half, SHARE, 128), BF16))(share, got)
    groups = [[2 * i + j for i in range(half)] for j in range(2)]
    parts = lax.all_to_all(copies, "slide", 0, 0, axis_index_groups=groups, tiled=True)
    last = call(gather_kernel, shape((CHIPS, LAST, 128), BF16))(parts, d_image_msg)
    last = between_chips(last)
    got = between_cores(last)
    held = [pltpu.VMEM((C, FF), F32), pltpu.VMEM((FF, C), F32), pltpu.SemaphoreType.DMA((2,))]
    g_w_in, g_w_out = call(
        own_share_kernel,
        (shape((C, FF), F32), shape((FF, C), F32)),
        held,
        [SMEM, VMEM],
        (HBM, HBM),
    )(core, last)
    grad_image, g_tall, g_wide, g_gain, g_shift, g_w_in, g_b_in, g_w_out, g_b_out = call(
        finish_kernel,
        (
            shape((ROWS, COLS, C), BF16),
            shape((SHORT, LONG, C), F32),
            shape((SHORT, LONG, C), F32),
            shape((1, C), F32),
            shape((1, C), F32),
            shape((C, FF), F32),
            shape((1, FF), F32),
            shape((FF, C), F32),
            shape((1, C), F32),
        ),
        [pltpu.VMEM((CORES, CHIPS * (LAST - OWN), 128), F32)] + held,
        [SMEM] + [VMEM] * 3 + [HBM] * 2,
        (VMEM,) * 5 + (HBM, VMEM, HBM, VMEM),
        {4: 5, 5: 7},
    )(core, last, got, upstream, g_w_in, g_w_out)
    return (
        output.reshape(image.shape),
        grad_image[None],
        jnp.transpose(g_tall, (1, 0, 2)),
        g_wide,
        g_gain[0],
        g_shift[0],
        g_w_in,
        g_b_in[0],
        g_w_out,
        g_b_out[0],
    )


def solution(mesh):
    cells = P("slide", "strip", None, None)
    return jax.shard_map(
        local,
        mesh=mesh,
        in_specs=(cells, cells) + (P(),) * 8,
        out_specs=(cells, cells) + (P(),) * 8,
        check_vma=False,
    )
```

```python
import functools

import jax
import jax.numpy as jnp
from jax import lax
from jax.experimental import pallas as pl
from jax.experimental.pallas import tpu as pltpu
from jax.sharding import PartitionSpec as P

F32 = jnp.float32
BF16 = jnp.bfloat16
CORES = 2
CHIPS = 16
STRIPS = CORES * CHIPS
ROWS = 6
COLS = 64
H = STRIPS * ROWS
C = 256
FF = 1024
LONG = 51
SHORT = 5
PAIRS = 4
BAND = 64
REACH = 32
MSG = ROWS * PAIRS
CELLS = ROWS * COLS
DATA = CORES * MSG
GRADS = C * FF // 128
OWN = GRADS // CHIPS
SHARE = OWN + 48
LAST = DATA + SHARE
epsilon = 1e-06

PARAMS = pltpu.CompilerParams(vmem_limit_bytes=24 * 1024 * 1024)


VMEM = pl.BlockSpec(memory_space=pltpu.VMEM)
SMEM = pl.BlockSpec(memory_space=pltpu.SMEM)
HBM = pl.BlockSpec(memory_space=pltpu.HBM)


def call(kernel, out_shape, scratch=(), in_specs=None, out_specs=None, aliases=None):
    specs = {}
    if in_specs is not None:
        specs["in_specs"] = in_specs
    if out_specs is not None:
        specs["out_specs"] = out_specs
    if aliases is not None:
        specs["input_output_aliases"] = aliases
    return pl.pallas_call(
        kernel,
        out_shape=out_shape,
        scratch_shapes=list(scratch),
        compiler_params=PARAMS,
        **specs,
    )


def turned_rows(block):
    return jnp.concatenate([block[:, :128], block[:, 128:]], axis=0).T


def put_by_strip(block, k, scr):
    rows = turned_rows(block)
    for cp in range(PAIRS):
        for core in range(CORES):
            first = cp * STRIPS + core * CHIPS
            at = pl.ds(core * MSG + k * PAIRS + cp, CHIPS, stride=CORES * MSG)
            scr[at, :] = rows[first : first + CHIPS]


def put_by_core(block, k, scr):
    rows = turned_rows(block)
    for cp in range(PAIRS):
        scr[pl.ds(k * PAIRS + cp, STRIPS, stride=MSG), :] = rows[cp * STRIPS : (cp + 1) * STRIPS]


def untwisted(parts):
    rows = jnp.concatenate(parts, axis=0).T
    return jnp.concatenate([rows[:COLS], rows[COLS:]], axis=1)


def half_masks(shape):
    lane = lax.broadcasted_iota(jnp.int32, shape, len(shape) - 1)
    return lane, lane < COLS


def shifted(x, by):
    if by == 0:
        return x
    column = lax.broadcasted_iota(jnp.int32, x.shape, 1) % COLS + by
    return jnp.where((column >= 0) & (column < COLS), pltpu.roll(x, (-by) % 128, 1), 0.0)


def sloped(row, first_shift, count):
    eight = pltpu.roll(jnp.broadcast_to(row, (8, 128)), 0, 1, stride=1, stride_axis=0)
    return jnp.concatenate(
        [pltpu.roll(eight, (first_shift + i) % 128, 1) for i in range(0, count, 8)], axis=0
    )


def tall_matrix(taps_ref, q, c):
    return sloped(taps_ref[q * 8 + c : q * 8 + c + 1, :], REACH - (LONG - 1) // 2, BAND)


def wide_matrix(taps_ref, p, cp, in_block):
    first = -((LONG - 1) // 2)
    turned = jnp.concatenate(
        [
            sloped(taps_ref[n : n + 1, :], first + COLS * c2, COLS)
            for c2, n in enumerate((p * 8 + cp, p * 8 + 4 + cp))
        ],
        axis=0,
    )
    return jnp.where(in_block, turned, 0.0)


def block_mask():
    row = lax.broadcasted_iota(jnp.int32, (128, 128), 0)
    lane = lax.broadcasted_iota(jnp.int32, (128, 128), 1)
    return (row < COLS) == (lane < COLS)


def tall_conv(padded, matrix, sign):
    _, first = half_masks((128, 128))
    zero = jnp.zeros((128, 128), BF16)
    sides = []
    for b in range(H // BAND):
        window = padded[b * BAND : b * BAND + 128]
        sides.append(
            jnp.concatenate([jnp.where(first, window, zero), jnp.where(first, zero, window)], axis=0)
        )
    product = jnp.dot(matrix, jnp.concatenate(sides, axis=1), preferred_element_type=F32)
    bands = []
    for b in range(H // BAND):
        total = None
        for q in range(SHORT):
            part = product[q * BAND : (q + 1) * BAND, b * 128 : (b + 1) * 128]
            part = shifted(part, sign * (q - 2))
            total = part if total is None else total + part
        bands.append(total)
    return jnp.concatenate(bands, axis=0)


def moved_rows(scr, sign):
    return jnp.concatenate(
        [scr[8 + sign * (p - 2) : 8 + sign * (p - 2) + H, :].astype(BF16) for p in range(SHORT)],
        axis=1,
    )


def flipped(taps_ref):
    a = lax.broadcasted_iota(jnp.int32, (128, 128), 0)
    b = lax.broadcasted_iota(jnp.int32, (128, 128), 1)
    turn = (a + b == LONG - 1).astype(BF16)
    return jnp.dot(taps_ref[...].astype(BF16), turn, preferred_element_type=F32)


def tall_matrices(taps, cp):
    return jnp.concatenate(
        [
            jnp.concatenate([tall_matrix(taps, q, c2 * 4 + cp) for c2 in range(2)], axis=1)
            for q in range(SHORT)
        ],
        axis=0,
    ).astype(BF16)


def wide_matrices(taps, cp, in_block):
    return jnp.concatenate(
        [wide_matrix(taps, p, cp, in_block) for p in range(SHORT)], axis=0
    ).astype(BF16)


def matrix_kernel(tall_ref, wide_ref, tall_out, wide_out):
    in_block = block_mask()
    tall, wide = tall_ref[...], flipped(wide_ref)
    for cp in range(PAIRS):
        tall_out[cp] = tall_matrices(tall, cp)
        wide_out[cp] = wide_matrices(wide, cp, in_block)


def pad_rows(x):
    zero = jnp.zeros((REACH, 128), x.dtype)
    return jnp.concatenate([zero, x, zero], axis=0)


def pack_kernel(image_ref, out_ref, scr):
    for k in range(ROWS):
        put_by_strip(image_ref[0, k].astype(F32), k, scr)
    out_ref[...] = scr[...].astype(BF16)


def forward_kernel(image_ref, tall_ref, wide_ref, conv_ref, mixed_ref, scr, pad, out):
    scr[...] = image_ref[...].astype(F32)
    pad[0:8, :] = jnp.zeros((8, 128), F32)
    pad[H + 8 : H + 16, :] = jnp.zeros((8, 128), F32)
    for cp in range(PAIRS):
        padded = pad_rows(scr[pl.ds(cp, H, stride=PAIRS), :].astype(BF16))
        mixed = tall_conv(padded, tall_ref[cp], 1).astype(BF16)
        mixed_ref[cp] = mixed
        pad[8 : H + 8, :] = mixed.astype(F32)
        out[pl.ds(cp, H, stride=PAIRS), :] = jnp.dot(
            moved_rows(pad, 1), wide_ref[cp], preferred_element_type=F32
        )
    conv_ref[...] = out[...].astype(BF16)


def beside_kernel(image_ref, wide_ref, shifted_ref, wide_out, scr):
    in_block = block_mask()
    wide = wide_ref[...]
    scr[...] = image_ref[...].astype(F32)
    for cp in range(PAIRS):
        padded = pad_rows(scr[pl.ds(cp, H, stride=PAIRS), :])
        for q in range(SHORT):
            shifted_ref[cp, q] = shifted(padded, q - 2).astype(BF16)
        wide_out[cp] = wide_matrices(wide, cp, in_block)


def fold(x, offset):
    total = None
    for i in range(0, x.shape[0], 8):
        part = pltpu.roll(x[i : i + 8], (offset - i) % 128, 1)
        total = part if total is None else total + part
    return total


def diagonal_sums(folds, count):
    total = folds[pl.ds(0, count, stride=8), :]
    for i in range(1, 8):
        total = total + pltpu.roll(folds[pl.ds(i, count, stride=8), :], 128 - i, 1)
    return total


def backward_kernel(
    scale,
    parts_ref,
    shifted_ref,
    mixed_ref,
    wide_ref,
    small_ref,
    d_mixed_ref,
    share_ref,
    d_scr,
    d_pad,
    m_pad,
    folds,
):
    total = None
    for i in range(CHIPS):
        part = parts_ref[i].astype(F32)
        d_scr[i * DATA : (i + 1) * DATA, :] = part[:DATA]
        total = part[DATA:] if total is None else total + part[DATA:]
    share_ref[0:OWN, :] = total.astype(BF16)
    for ref in (d_pad, m_pad):
        ref[0:8, :] = jnp.zeros((8, 128), F32)
        ref[H + 8 : H + 16, :] = jnp.zeros((8, 128), F32)
    row = lax.broadcasted_iota(jnp.int32, (BAND, 128), 0)
    lane = lax.broadcasted_iota(jnp.int32, (BAND, 128), 1)
    half = (LONG - 1) // 2
    low_band = (lane - row >= 7) & (lane - row <= 57)
    near = jnp.abs(lane % COLS - row) <= half
    low_near = near & (lane < COLS)
    high_near = near & (lane >= COLS)
    first = lax.broadcasted_iota(jnp.int32, (H, 128), 1) < COLS
    zero = jnp.zeros((H, 128), BF16)
    for cp in range(PAIRS):
        d_conv = d_scr[pl.ds(cp, H, stride=PAIRS), :]
        d_pad[8 : H + 8, :] = d_conv
        m_pad[8 : H + 8, :] = mixed_ref[cp].astype(F32)
        d_mixed = jnp.dot(
            moved_rows(d_pad, -1), wide_ref[cp], preferred_element_type=F32
        ).astype(BF16)
        d_mixed_ref[cp] = d_mixed
        corr = lax.dot_general(
            d_conv.astype(BF16),
            moved_rows(m_pad, 1),
            (((0,), (0,)), ((), ())),
            preferred_element_type=F32,
        )
        for p in range(SHORT):
            part = corr[:, p * 128 : (p + 1) * 128]
            part = jnp.where(low_near, part[:COLS], jnp.where(high_near, part[COLS:], 0.0))
            at = (20 + p * PAIRS + cp) * 8
            folds[at : at + 8, :] = fold(part, 7 + half)
        sides = []
        for c2 in range(2):
            own = jnp.where(first, d_mixed, zero) if c2 == 0 else jnp.where(first, zero, d_mixed)
            own = jnp.concatenate([own[b * BAND : (b + 1) * BAND] for b in range(H // BAND)], axis=1)
            windows = jnp.concatenate(
                [
                    jnp.concatenate(
                        [
                            shifted_ref[cp, q, b * BAND + at : b * BAND + at + BAND, :]
                            for b in range(H // BAND)
                        ],
                        axis=1,
                    )
                    for q in range(SHORT)
                    for at in ((0, BAND) if c2 == 0 else (BAND, 0))
                ],
                axis=0,
            )
            sides.append(
                lax.dot_general(
                    own, windows, (((1,), (1,)), ((), ())), preferred_element_type=F32
                )
            )
        for q in range(SHORT):
            low, high = (side[:, q * 128 : (q + 1) * 128] for side in sides)
            at = (q * PAIRS + cp) * 8
            folds[at : at + 8, :] = fold(jnp.where(low_band, low, high), 0)
    grads = diagonal_sums(folds, 40) * scale
    share_ref[OWN:SHARE, :] = jnp.concatenate([grads, small_ref[...]], axis=0).astype(BF16)


def d_image_kernel(d_mixed_ref, tall_ref, d_image_ref, out):
    taps = flipped(tall_ref)
    for cp in range(PAIRS):
        out[pl.ds(cp, H, stride=PAIRS), :] = tall_conv(
            pad_rows(d_mixed_ref[cp]), tall_matrices(taps, cp), -1
        )
    d_image_ref[...] = out[...].astype(BF16)


def mlp_kernel(
    scale,
    core_ref,
    conv_ref,
    image_ref,
    cot_ref,
    gain_ref,
    bias_ref,
    w_in_ref,
    b_in_ref,
    w_out_ref,
    b_out_ref,
    output_ref,
    theirs_ref,
    mine_ref,
    normed_ref,
    right_ref,
    small_ref,
    scr,
    out,
    small,
    left,
):
    core = core_ref[0]
    scr[...] = conv_ref[...].astype(F32)
    gain, bias = gain_ref[...], bias_ref[...]
    sums = [jnp.zeros((1, C), F32), jnp.zeros((1, C), F32), jnp.zeros((1, C), F32)]
    g_b_in = jnp.zeros((1, FF), F32)
    step = 6
    for k in range(0, ROWS, step):
        rows = slice(k * COLS, (k + step) * COLS)
        conv = jnp.concatenate(
            [
                untwisted(
                    [
                        scr[pl.ds(c * MSG + i * PAIRS + cp, CHIPS, stride=CORES * MSG), :]
                        for cp in range(PAIRS)
                        for c in range(CORES)
                    ]
                )
                for i in range(k, k + step)
            ],
            axis=0,
        )
        centred = conv - jnp.mean(conv, axis=1, keepdims=True)
        inverse = lax.rsqrt(jnp.mean(centred * centred, axis=1, keepdims=True) + epsilon)
        xhat = centred * inverse
        normed = (xhat * gain + bias).astype(BF16)
        normed_ref[rows, :] = normed
        left[0, rows, :] = normed
        pre_act = jnp.dot(normed, w_in_ref[...], preferred_element_type=F32) + b_in_ref[...]
        cdf = 0.5 * (1.0 + lax.erf(pre_act * 0.7071067811865476))
        hidden = (pre_act * cdf).astype(BF16)
        right_ref[1, rows, :] = hidden
        branch = jnp.dot(hidden, w_out_ref[...], preferred_element_type=F32) + b_out_ref[...]
        cot = cot_ref[rows, :]
        left[1, rows, :] = cot
        output_ref[rows, :] = (image_ref[rows, :].astype(F32) + branch).astype(BF16)
        d_hidden = lax.dot_general(
            cot, w_out_ref[...], (((1,), (1,)), ((), ())), preferred_element_type=F32
        )
        slope = cdf + pre_act * jnp.exp(-0.5 * pre_act * pre_act) * 0.3989422804014327
        d_pre = (d_hidden * slope).astype(BF16)
        right_ref[0, rows, :] = d_pre
        g_b_in = g_b_in + jnp.sum(d_pre.astype(F32), axis=0, keepdims=True)
        d_norm = lax.dot_general(
            d_pre, w_in_ref[...], (((1,), (1,)), ((), ())), preferred_element_type=F32
        )
        sums[0] = sums[0] + jnp.sum(d_norm * xhat, axis=0, keepdims=True)
        sums[1] = sums[1] + jnp.sum(d_norm, axis=0, keepdims=True)
        sums[2] = sums[2] + jnp.sum(cot.astype(F32), axis=0, keepdims=True)
        g = d_norm * gain
        d_conv = inverse * (
            g
            - jnp.mean(g, axis=1, keepdims=True)
            - xhat * jnp.mean(g * xhat, axis=1, keepdims=True)
        )
        for i in range(step):
            put_by_core(d_conv[i * COLS : (i + 1) * COLS], k + i, out)
    half = CHIPS * MSG
    theirs_ref[GRADS : GRADS + half, :] = out[pl.ds((1 - core) * half, half), :].astype(BF16)
    mine_ref[...] = out[pl.ds(core * half, half), :].astype(BF16)
    put_grads(over_cells(left[1 - core], right_ref[1 - core]), scale, theirs_ref)
    small[...] = jnp.zeros((16, 128), F32)
    for i in range(FF // 128):
        small[i : i + 1, :] = g_b_in[:, i * 128 : (i + 1) * 128] * scale
    for n in range(3):
        for i in range(2):
            row = 8 + 2 * n + i
            small[row : row + 1, :] = sums[n][:, i * 128 : (i + 1) * 128] * scale
    small_ref[...] = small[pl.ds(core * 8, 8), :]
    other = small[pl.ds((1 - core) * 8, 8), :]
    theirs_ref[GRADS + half : GRADS + half + 16, :] = jnp.concatenate(
        [other, jnp.zeros((8, 128), F32)], axis=0
    ).astype(BF16)


def put_grads(grads, scale, out_ref):
    grads = (grads * scale).astype(out_ref.dtype)
    for i in range(CHIPS):
        for j in range(FF // 128):
            at = (i * (FF // 128) + j) * 16
            out_ref[at : at + 16, :] = grads[i * 16 : (i + 1) * 16, j * 128 : (j + 1) * 128]


def over_cells(left, right):
    return lax.dot_general(left, right, (((0,), (0,)), ((), ())), preferred_element_type=F32)


def own_grads_kernel(scale, core_ref, normed_ref, cot_ref, right_ref, out_ref):
    for n, left_ref in enumerate((normed_ref, cot_ref)):

        @pl.when(core_ref[0] == n)
        def _(n=n, left_ref=left_ref):
            put_grads(over_cells(left_ref[...], right_ref[n]), scale, out_ref)


def merge_kernel(core_ref, mine_ref, grads_ref, small_ref, got_ref, out_hbm, small_out, rows_scr, sems):
    half = CHIPS * MSG
    mine = mine_ref[...].astype(F32)
    got = got_ref[GRADS : GRADS + half, :].astype(F32)
    other = got_ref[GRADS + half : GRADS + half + 16, :].astype(F32)
    small_out[...] = small_ref[...] + other[:8]
    low = core_ref[0] == 0
    one, two = jnp.where(low, mine, got), jnp.where(low, got, mine)
    copies = []
    for i in range(CHIPS):
        rows = slice(i * MSG, (i + 1) * MSG)
        rows_scr[i, 0:DATA, :] = jnp.concatenate([one[rows], two[rows]], axis=0).astype(BF16)
        rows = slice(i * OWN, (i + 1) * OWN)
        rows_scr[i, DATA : DATA + OWN, :] = (
            grads_ref[rows, :] + got_ref[rows, :].astype(F32)
        ).astype(BF16)
        if i % 4 == 3:
            part = pl.ds(i - 3, 4)
            copies.append(pltpu.make_async_copy(rows_scr.at[part], out_hbm.at[part], sems.at[i // 4]))
            copies[-1].start()
    for copy in copies:
        copy.wait()


def pair_sum_kernel(mine_ref, got_ref, out_ref):
    total = (mine_ref[...].astype(F32) + got_ref[...].astype(F32)).astype(BF16)
    for i in range(out_ref.shape[0]):
        out_ref[i] = total


def gather_kernel(parts_ref, d_image_ref, out_ref):
    total = parts_ref[0].astype(F32)
    for i in range(1, parts_ref.shape[0]):
        total = total + parts_ref[i].astype(F32)
    total = total.astype(BF16)
    for i in range(CHIPS):
        out_ref[i, 0:DATA, :] = d_image_ref[i * DATA : (i + 1) * DATA, :]
        out_ref[i, DATA : DATA + SHARE, :] = total


def place_share(core, ref, w_in_hbm, w_out_hbm, held, w_out, sems):
    lanes = FF // 128
    for i in range(CHIPS):
        part = ref[i, DATA : DATA + OWN, :].astype(F32)
        for j in range(lanes):
            held[i * 16 : (i + 1) * 16, j * 128 : (j + 1) * 128] = part[j * 16 : (j + 1) * 16]

    @pl.when(core == 0)
    def _():
        pltpu.make_async_copy(held, w_in_hbm, sems.at[0]).start()

    @pl.when(core == 1)
    def _():
        for n in range(2):
            for j in range(n * lanes // 2, (n + 1) * lanes // 2):
                for half in range(2):
                    w_out[j * 128 : (j + 1) * 128, half * 128 : (half + 1) * 128] = held[
                        half * 128 : (half + 1) * 128, j * 128 : (j + 1) * 128
                    ].T
            rows = pl.ds(n * FF // 2, FF // 2)
            pltpu.make_async_copy(w_out.at[rows], w_out_hbm.at[rows], sems.at[n]).start()


def placed_share(core, w_in_hbm, w_out_hbm, held, w_out, sems):
    @pl.when(core == 0)
    def _():
        pltpu.make_async_copy(held, w_in_hbm, sems.at[0]).wait()

    @pl.when(core == 1)
    def _():
        for n in range(2):
            rows = pl.ds(n * FF // 2, FF // 2)
            pltpu.make_async_copy(w_out.at[rows], w_out_hbm.at[rows], sems.at[n]).wait()


def own_share_kernel(core_ref, mine_ref, w_in_hbm, w_out_hbm, held, w_out, sems):
    place_share(core_ref[0], mine_ref, w_in_hbm, w_out_hbm, held, w_out, sems)
    placed_share(core_ref[0], w_in_hbm, w_out_hbm, held, w_out, sems)


def finish_kernel(
    core_ref,
    mine_ref,
    got_ref,
    cot_ref,
    w_in_in,
    w_out_in,
    out_ref,
    tall_ref,
    wide_ref,
    gain_ref,
    shift_ref,
    w_in_hbm,
    b_in_ref,
    w_out_hbm,
    b_out_ref,
    scr,
    held,
    w_out,
    sems,
):
    del w_in_in, w_out_in
    core = core_ref[0]
    place_share(1 - core, got_ref, w_in_hbm, w_out_hbm, held, w_out, sems)
    rest = LAST - OWN
    for i in range(CHIPS):
        for c, ref in ((core, mine_ref), (1 - core, got_ref)):
            at = i * rest
            scr[c, at : at + DATA, :] = ref[i, 0:DATA, :].astype(F32)
            scr[c, at + DATA : at + rest, :] = ref[i, DATA + OWN : LAST, :].astype(F32)
    for k in range(ROWS):
        d_image = untwisted(
            [
                scr.at[c][pl.ds(core * MSG + k * PAIRS + cp, CHIPS, stride=rest), :]
                for cp in range(PAIRS)
                for c in range(CORES)
            ]
        )
        out_ref[k] = (cot_ref[k].astype(F32) + d_image).astype(BF16)
    for q in range(SHORT):
        for start, ref in ((0, tall_ref), (20, wide_ref)):
            ref[q] = untwisted(
                [
                    scr.at[c][pl.ds(DATA + start + q * PAIRS + cp, CHIPS, stride=rest), :]
                    for cp in range(PAIRS)
                    for c in range(CORES)
                ]
            )[7 : 7 + LONG]
    totals = []
    for c in range(CORES):
        total = None
        for i in range(CHIPS):
            part = scr[c, (i + 1) * rest - 8 : (i + 1) * rest, :]
            total = part if total is None else total + part
        totals.append(total)
    for i in range(FF // 128):
        b_in_ref[:, i * 128 : (i + 1) * 128] = totals[0][i : i + 1]
    for n, ref in enumerate((gain_ref, shift_ref, b_out_ref)):
        for i in range(2):
            ref[:, i * 128 : (i + 1) * 128] = totals[1][2 * n + i : 2 * n + i + 1]
    placed_share(1 - core, w_in_hbm, w_out_hbm, held, w_out, sems)


def messages(x):
    x = lax.all_to_all(x.reshape(STRIPS, MSG, 128), "strip", 0, 0, tiled=True)
    return x.reshape(STRIPS * MSG, 128)


def between_chips(x):
    groups = [[CORES * i + c for i in range(CHIPS)] for c in range(CORES)]
    return lax.all_to_all(x, "strip", 0, 0, axis_index_groups=groups, tiled=True)


def between_cores(x):
    return lax.ppermute(x, "strip", [(i, i ^ 1) for i in range(STRIPS)])


def shape(dims, dtype):
    return jax.ShapeDtypeStruct(dims, dtype)


def local(
    image,
    cotangent,
    kernel_tall,
    kernel_wide,
    layer_norm_gain,
    layer_norm_bias,
    w_in,
    b_in,
    w_out,
    b_out,
):
    source = image[0]
    upstream = cotangent[0]
    slides = lax.axis_size("slide")
    scale = float(CELLS * slides * STRIPS) ** (-0.5)
    packed_f = pltpu.VMEM((STRIPS * MSG, 128), F32)
    packed_b = shape((STRIPS * MSG, 128), BF16)
    edge = pltpu.VMEM((H + 16, 128), F32)

    image_msg = call(
        pack_kernel,
        packed_b,
        [packed_f],
    )(image)
    me = lax.axis_index("strip")
    core = (me % CORES).reshape(1)
    me = (me % CORES) * CHIPS + me // CORES
    own = jnp.arange(8)[:, None] * STRIPS + me == jnp.arange(C)[None, :]
    own = own.astype(BF16)

    def taps(kernel, spec):
        picked = jnp.einsum(spec, kernel, own, preferred_element_type=F32)
        picked = picked.reshape(SHORT * 8, LONG)
        return jnp.pad(picked, ((0, 0), (0, 128 - LONG)))

    tall = taps(kernel_tall, "pqc,kc->qkp")
    wide = taps(kernel_wide, "pqc,kc->pkq")
    tall_fwd, wide_fwd = call(
        matrix_kernel, (shape((PAIRS, SHORT * BAND, C), BF16), shape((PAIRS, SHORT * 128, 128), BF16))
    )(tall, wide)

    image_ch = messages(image_msg)
    conv_ch, mixed = call(
        forward_kernel,
        (
            packed_b,
            shape((PAIRS, H, 128), BF16),
        ),
        [packed_f, edge, packed_f],
    )(image_ch, tall_fwd, wide_fwd)
    conv = messages(conv_ch)
    output, theirs, mine, normed, right, small = call(
        functools.partial(mlp_kernel, scale),
        (
            shape((CELLS, C), BF16),
            shape((GRADS + CHIPS * MSG + 16, 128), BF16),
            shape((CHIPS * MSG, 128), BF16),
            shape((CELLS, C), BF16),
            shape((2, CELLS, FF), BF16),
            shape((8, 128), F32),
        ),
        [packed_f, packed_f, pltpu.VMEM((16, 128), F32), pltpu.VMEM((2, CELLS, C), BF16)],
        [SMEM] + [VMEM] * 9,
    )(
        core,
        conv,
        source.reshape(CELLS, C),
        upstream.reshape(CELLS, C),
        layer_norm_gain[None],
        layer_norm_bias[None],
        w_in,
        b_in[None],
        w_out,
        b_out[None],
    )
    got = between_cores(theirs)
    chip_grads = call(
        functools.partial(own_grads_kernel, scale), shape((GRADS, 128), F32), (), [SMEM] + [VMEM] * 3
    )(core, normed, upstream.reshape(CELLS, C), right)
    merged, small = call(
        merge_kernel,
        (shape((CHIPS, DATA + OWN, 128), BF16), shape((8, 128), F32)),
        [pltpu.VMEM((CHIPS, DATA + OWN, 128), BF16), pltpu.SemaphoreType.DMA((4,))],
        [SMEM] + [VMEM] * 4,
        (HBM, VMEM),
    )(core, mine, chip_grads, small, got)
    shifts, wide_bwd = call(
        beside_kernel,
        (shape((PAIRS, SHORT, H + 2 * REACH, 128), BF16), shape((PAIRS, SHORT * 128, 128), BF16)),
        [packed_f],
    )(image_ch, wide)
    d_mixed, share = call(
        functools.partial(backward_kernel, scale),
        (shape((PAIRS, H, 128), BF16), shape((SHARE, 128), BF16)),
        [packed_f, edge, edge, pltpu.VMEM((40 * 8, 128), F32)],
    )(between_chips(merged), shifts, mixed, wide_bwd, small)
    got = lax.ppermute(share, "slide", [(i, i ^ 1) for i in range(slides)])
    d_image_msg = call(d_image_kernel, packed_b, [packed_f])(d_mixed, tall)
    half = slides // 2
    got, d_image_msg = lax.optimization_barrier((got, d_image_msg))
    copies = call(pair_sum_kernel, shape((half, SHARE, 128), BF16))(share, got)
    groups = [[2 * i + j for i in range(half)] for j in range(2)]
    parts = lax.all_to_all(copies, "slide", 0, 0, axis_index_groups=groups, tiled=True)
    last = call(gather_kernel, shape((CHIPS, LAST, 128), BF16))(parts, d_image_msg)
    last = between_chips(last)
    got = between_cores(last)
    held = [pltpu.VMEM((C, FF), F32), pltpu.VMEM((FF, C), F32), pltpu.SemaphoreType.DMA((2,))]
    g_w_in, g_w_out = call(
        own_share_kernel,
        (shape((C, FF), F32), shape((FF, C), F32)),
        held,
        [SMEM, VMEM],
        (HBM, HBM),
    )(core, last)
    grad_image, g_tall, g_wide, g_gain, g_shift, g_w_in, g_b_in, g_w_out, g_b_out = call(
        finish_kernel,
        (
            shape((ROWS, COLS, C), BF16),
            shape((SHORT, LONG, C), F32),
            shape((SHORT, LONG, C), F32),
            shape((1, C), F32),
            shape((1, C), F32),
            shape((C, FF), F32),
            shape((1, FF), F32),
            shape((FF, C), F32),
            shape((1, C), F32),
        ),
        [pltpu.VMEM((CORES, CHIPS * (LAST - OWN), 128), F32)] + held,
        [SMEM] + [VMEM] * 3 + [HBM] * 2,
        (VMEM,) * 5 + (HBM, VMEM, HBM, VMEM),
        {4: 5, 5: 7},
    )(core, last, got, upstream, g_w_in, g_w_out)
    return (
        output.reshape(image.shape),
        grad_image[None],
        jnp.transpose(g_tall, (1, 0, 2)),
        g_wide,
        g_gain[0],
        g_shift[0],
        g_w_in,
        g_b_in[0],
        g_w_out,
        g_b_out[0],
    )


def solution(mesh):
    cells = P("slide", "strip", None, None)
    return jax.shard_map(
        local,
        mesh=mesh,
        in_specs=(cells, cells) + (P(),) * 8,
        out_specs=(cells, cells) + (P(),) * 8,
        check_vma=False,
    )
```

```python
import functools

import jax
import jax.numpy as jnp
from jax import lax
from jax.experimental import pallas as pl
from jax.experimental.pallas import tpu as pltpu
from jax.sharding import PartitionSpec as P

F32 = jnp.float32
BF16 = jnp.bfloat16
CORES = 2
CHIPS = 16
STRIPS = CORES * CHIPS
ROWS = 6
COLS = 64
H = STRIPS * ROWS
C = 256
FF = 1024
LONG = 51
SHORT = 5
PAIRS = 4
BAND = 64
REACH = 32
MSG = ROWS * PAIRS
CELLS = ROWS * COLS
DATA = CORES * MSG
GRADS = C * FF // 128
OWN = GRADS // CHIPS
SHARE = OWN + 48
LAST = DATA + SHARE
epsilon = 1e-06

PARAMS = pltpu.CompilerParams(vmem_limit_bytes=24 * 1024 * 1024)


VMEM = pl.BlockSpec(memory_space=pltpu.VMEM)
SMEM = pl.BlockSpec(memory_space=pltpu.SMEM)
HBM = pl.BlockSpec(memory_space=pltpu.HBM)


def call(kernel, out_shape, scratch=(), in_specs=None, out_specs=None, aliases=None):
    specs = {}
    if in_specs is not None:
        specs["in_specs"] = in_specs
    if out_specs is not None:
        specs["out_specs"] = out_specs
    if aliases is not None:
        specs["input_output_aliases"] = aliases
    return pl.pallas_call(
        kernel,
        out_shape=out_shape,
        scratch_shapes=list(scratch),
        compiler_params=PARAMS,
        **specs,
    )


def turned_rows(block):
    block = block.astype(BF16)
    return jnp.concatenate([block[:, :128], block[:, 128:]], axis=0).T.astype(F32)


def put_by_strip(block, k, scr):
    rows = turned_rows(block)
    for cp in range(PAIRS):
        for core in range(CORES):
            first = cp * STRIPS + core * CHIPS
            at = pl.ds(core * MSG + k * PAIRS + cp, CHIPS, stride=CORES * MSG)
            scr[at, :] = rows[first : first + CHIPS]


def put_by_core(block, k, scr):
    rows = turned_rows(block)
    for cp in range(PAIRS):
        scr[pl.ds(k * PAIRS + cp, STRIPS, stride=MSG), :] = rows[cp * STRIPS : (cp + 1) * STRIPS]


def untwisted(parts):
    rows = jnp.concatenate(parts, axis=0).astype(BF16).T.astype(F32)
    return jnp.concatenate([rows[:COLS], rows[COLS:]], axis=1)


def half_masks(shape):
    lane = lax.broadcasted_iota(jnp.int32, shape, len(shape) - 1)
    return lane, lane < COLS


def shifted(x, by):
    if by == 0:
        return x
    column = lax.broadcasted_iota(jnp.int32, x.shape, 1) % COLS + by
    return jnp.where((column >= 0) & (column < COLS), pltpu.roll(x, (-by) % 128, 1), 0.0)


def sloped(row, first_shift, count):
    eight = pltpu.roll(jnp.broadcast_to(row, (8, 128)), 0, 1, stride=1, stride_axis=0)
    return jnp.concatenate(
        [pltpu.roll(eight, (first_shift + i) % 128, 1) for i in range(0, count, 8)], axis=0
    )


def tall_matrix(taps_ref, q, c):
    return sloped(taps_ref[q * 8 + c : q * 8 + c + 1, :], REACH - (LONG - 1) // 2, BAND)


def wide_matrix(taps_ref, p, cp, in_block):
    first = -((LONG - 1) // 2)
    turned = jnp.concatenate(
        [
            sloped(taps_ref[n : n + 1, :], first + COLS * c2, COLS)
            for c2, n in enumerate((p * 8 + cp, p * 8 + 4 + cp))
        ],
        axis=0,
    )
    return jnp.where(in_block, turned, 0.0)


def block_mask():
    row = lax.broadcasted_iota(jnp.int32, (128, 128), 0)
    lane = lax.broadcasted_iota(jnp.int32, (128, 128), 1)
    return (row < COLS) == (lane < COLS)


def tall_conv(padded, matrix, sign):
    _, first = half_masks((128, 128))
    zero = jnp.zeros((128, 128), BF16)
    sides = []
    for b in range(H // BAND):
        window = padded[b * BAND : b * BAND + 128]
        sides.append(
            jnp.concatenate([jnp.where(first, window, zero), jnp.where(first, zero, window)], axis=0)
        )
    product = jnp.dot(matrix, jnp.concatenate(sides, axis=1), preferred_element_type=F32)
    bands = []
    for b in range(H // BAND):
        total = None
        for q in range(SHORT):
            part = product[q * BAND : (q + 1) * BAND, b * 128 : (b + 1) * 128]
            part = shifted(part, sign * (q - 2))
            total = part if total is None else total + part
        bands.append(total)
    return jnp.concatenate(bands, axis=0)


def moved_rows(scr, sign):
    return jnp.concatenate(
        [scr[8 + sign * (p - 2) : 8 + sign * (p - 2) + H, :].astype(BF16) for p in range(SHORT)],
        axis=1,
    )


def flipped(taps_ref):
    a = lax.broadcasted_iota(jnp.int32, (128, 128), 0)
    b = lax.broadcasted_iota(jnp.int32, (128, 128), 1)
    turn = (a + b == LONG - 1).astype(BF16)
    return jnp.dot(taps_ref[...].astype(BF16), turn, preferred_element_type=F32)


def tall_matrices(taps, cp):
    return jnp.concatenate(
        [
            jnp.concatenate([tall_matrix(taps, q, c2 * 4 + cp) for c2 in range(2)], axis=1)
            for q in range(SHORT)
        ],
        axis=0,
    ).astype(BF16)


def wide_matrices(taps, cp, in_block):
    return jnp.concatenate(
        [wide_matrix(taps, p, cp, in_block) for p in range(SHORT)], axis=0
    ).astype(BF16)


def matrix_kernel(tall_ref, wide_ref, tall_out, wide_out):
    in_block = block_mask()
    tall, wide = tall_ref[...], flipped(wide_ref)
    for cp in range(PAIRS):
        tall_out[cp] = tall_matrices(tall, cp)
        wide_out[cp] = wide_matrices(wide, cp, in_block)


def pad_rows(x):
    zero = jnp.zeros((REACH, 128), x.dtype)
    return jnp.concatenate([zero, x, zero], axis=0)


def pack_kernel(image_ref, out_ref, scr):
    for k in range(ROWS):
        put_by_strip(image_ref[0, k].astype(F32), k, scr)
    out_ref[...] = scr[...].astype(BF16)


def forward_kernel(image_ref, tall_ref, wide_ref, conv_ref, mixed_ref, scr, pad, out):
    scr[...] = image_ref[...].astype(F32)
    pad[0:8, :] = jnp.zeros((8, 128), F32)
    pad[H + 8 : H + 16, :] = jnp.zeros((8, 128), F32)
    for cp in range(PAIRS):
        padded = pad_rows(scr[pl.ds(cp, H, stride=PAIRS), :].astype(BF16))
        mixed = tall_conv(padded, tall_ref[cp], 1).astype(BF16)
        mixed_ref[cp] = mixed
        pad[8 : H + 8, :] = mixed.astype(F32)
        out[pl.ds(cp, H, stride=PAIRS), :] = jnp.dot(
            moved_rows(pad, 1), wide_ref[cp], preferred_element_type=F32
        )
    conv_ref[...] = out[...].astype(BF16)


def beside_kernel(image_ref, wide_ref, shifted_ref, wide_out, scr):
    in_block = block_mask()
    wide = wide_ref[...]
    scr[...] = image_ref[...].astype(F32)
    for cp in range(PAIRS):
        padded = pad_rows(scr[pl.ds(cp, H, stride=PAIRS), :])
        for q in range(SHORT):
            shifted_ref[cp, q] = shifted(padded, q - 2).astype(BF16)
        wide_out[cp] = wide_matrices(wide, cp, in_block)


def fold(x, offset):
    total = None
    for i in range(0, x.shape[0], 8):
        part = pltpu.roll(x[i : i + 8], (offset - i) % 128, 1)
        total = part if total is None else total + part
    return total


def diagonal_sums(folds, count):
    total = folds[pl.ds(0, count, stride=8), :]
    for i in range(1, 8):
        total = total + pltpu.roll(folds[pl.ds(i, count, stride=8), :], 128 - i, 1)
    return total


def backward_kernel(
    scale,
    parts_ref,
    shifted_ref,
    mixed_ref,
    wide_ref,
    small_ref,
    d_mixed_ref,
    share_ref,
    d_scr,
    d_pad,
    m_pad,
    folds,
):
    total = None
    for i in range(CHIPS):
        part = parts_ref[i].astype(F32)
        d_scr[i * DATA : (i + 1) * DATA, :] = part[:DATA]
        total = part[DATA:] if total is None else total + part[DATA:]
    share_ref[0:OWN, :] = total.astype(BF16)
    for ref in (d_pad, m_pad):
        ref[0:8, :] = jnp.zeros((8, 128), F32)
        ref[H + 8 : H + 16, :] = jnp.zeros((8, 128), F32)
    row = lax.broadcasted_iota(jnp.int32, (BAND, 128), 0)
    lane = lax.broadcasted_iota(jnp.int32, (BAND, 128), 1)
    half = (LONG - 1) // 2
    low_band = (lane - row >= 7) & (lane - row <= 57)
    near = jnp.abs(lane % COLS - row) <= half
    low_near = near & (lane < COLS)
    high_near = near & (lane >= COLS)
    first = lax.broadcasted_iota(jnp.int32, (H, 128), 1) < COLS
    zero = jnp.zeros((H, 128), BF16)
    for cp in range(PAIRS):
        d_conv = d_scr[pl.ds(cp, H, stride=PAIRS), :]
        d_pad[8 : H + 8, :] = d_conv
        m_pad[8 : H + 8, :] = mixed_ref[cp].astype(F32)
        d_mixed = jnp.dot(
            moved_rows(d_pad, -1), wide_ref[cp], preferred_element_type=F32
        ).astype(BF16)
        d_mixed_ref[cp] = d_mixed
        corr = lax.dot_general(
            d_conv.astype(BF16),
            moved_rows(m_pad, 1),
            (((0,), (0,)), ((), ())),
            preferred_element_type=F32,
        )
        for p in range(SHORT):
            part = corr[:, p * 128 : (p + 1) * 128]
            part = jnp.where(low_near, part[:COLS], jnp.where(high_near, part[COLS:], 0.0))
            at = (20 + p * PAIRS + cp) * 8
            folds[at : at + 8, :] = fold(part, 7 + half)
        sides = []
        for c2 in range(2):
            own = jnp.where(first, d_mixed, zero) if c2 == 0 else jnp.where(first, zero, d_mixed)
            own = jnp.concatenate([own[b * BAND : (b + 1) * BAND] for b in range(H // BAND)], axis=1)
            windows = jnp.concatenate(
                [
                    jnp.concatenate(
                        [
                            shifted_ref[cp, q, b * BAND + at : b * BAND + at + BAND, :]
                            for b in range(H // BAND)
                        ],
                        axis=1,
                    )
                    for q in range(SHORT)
                    for at in ((0, BAND) if c2 == 0 else (BAND, 0))
                ],
                axis=0,
            )
            sides.append(
                lax.dot_general(
                    own, windows, (((1,), (1,)), ((), ())), preferred_element_type=F32
                )
            )
        for q in range(SHORT):
            low, high = (side[:, q * 128 : (q + 1) * 128] for side in sides)
            at = (q * PAIRS + cp) * 8
            folds[at : at + 8, :] = fold(jnp.where(low_band, low, high), 0)
    grads = diagonal_sums(folds, 40) * scale
    share_ref[OWN:SHARE, :] = jnp.concatenate([grads, small_ref[...]], axis=0).astype(BF16)


def d_image_kernel(d_mixed_ref, tall_ref, d_image_ref, out):
    taps = flipped(tall_ref)
    for cp in range(PAIRS):
        out[pl.ds(cp, H, stride=PAIRS), :] = tall_conv(
            pad_rows(d_mixed_ref[cp]), tall_matrices(taps, cp), -1
        )
    d_image_ref[...] = out[...].astype(BF16)


def mlp_kernel(
    scale,
    core_ref,
    conv_ref,
    image_ref,
    cot_ref,
    gain_ref,
    bias_ref,
    w_in_ref,
    b_in_ref,
    w_out_ref,
    b_out_ref,
    output_ref,
    theirs_ref,
    mine_ref,
    normed_ref,
    right_ref,
    small_ref,
    scr,
    out,
    small,
    left,
):
    core = core_ref[0]
    scr[...] = conv_ref[...].astype(F32)
    gain, bias = gain_ref[...], bias_ref[...]
    sums = [jnp.zeros((1, C), F32), jnp.zeros((1, C), F32), jnp.zeros((1, C), F32)]
    g_b_in = jnp.zeros((1, FF), F32)
    step = 6
    for k in range(0, ROWS, step):
        rows = slice(k * COLS, (k + step) * COLS)
        conv = jnp.concatenate(
            [
                untwisted(
                    [
                        scr[pl.ds(c * MSG + i * PAIRS + cp, CHIPS, stride=CORES * MSG), :]
                        for cp in range(PAIRS)
                        for c in range(CORES)
                    ]
                )
                for i in range(k, k + step)
            ],
            axis=0,
        )
        centred = conv - jnp.mean(conv, axis=1, keepdims=True)
        inverse = lax.rsqrt(jnp.mean(centred * centred, axis=1, keepdims=True) + epsilon)
        xhat = centred * inverse
        normed = (xhat * gain + bias).astype(BF16)
        normed_ref[rows, :] = normed
        left[0, rows, :] = normed
        pre_act = jnp.dot(normed, w_in_ref[...], preferred_element_type=F32) + b_in_ref[...]
        cdf = 0.5 * (1.0 + lax.erf(pre_act * 0.7071067811865476))
        hidden = (pre_act * cdf).astype(BF16)
        right_ref[1, rows, :] = hidden
        branch = jnp.dot(hidden, w_out_ref[...], preferred_element_type=F32) + b_out_ref[...]
        cot = cot_ref[rows, :]
        left[1, rows, :] = cot
        output_ref[rows, :] = (image_ref[rows, :].astype(F32) + branch).astype(BF16)
        d_hidden = lax.dot_general(
            cot, w_out_ref[...], (((1,), (1,)), ((), ())), preferred_element_type=F32
        )
        slope = cdf + pre_act * jnp.exp(-0.5 * pre_act * pre_act) * 0.3989422804014327
        d_pre = (d_hidden * slope).astype(BF16)
        right_ref[0, rows, :] = d_pre
        g_b_in = g_b_in + jnp.sum(d_pre.astype(F32), axis=0, keepdims=True)
        d_norm = lax.dot_general(
            d_pre, w_in_ref[...], (((1,), (1,)), ((), ())), preferred_element_type=F32
        )
        sums[0] = sums[0] + jnp.sum(d_norm * xhat, axis=0, keepdims=True)
        sums[1] = sums[1] + jnp.sum(d_norm, axis=0, keepdims=True)
        sums[2] = sums[2] + jnp.sum(cot.astype(F32), axis=0, keepdims=True)
        g = d_norm * gain
        d_conv = inverse * (
            g
            - jnp.mean(g, axis=1, keepdims=True)
            - xhat * jnp.mean(g * xhat, axis=1, keepdims=True)
        )
        for i in range(step):
            put_by_core(d_conv[i * COLS : (i + 1) * COLS], k + i, out)
    half = CHIPS * MSG
    theirs_ref[GRADS : GRADS + half, :] = out[pl.ds((1 - core) * half, half), :].astype(BF16)
    mine_ref[...] = out[pl.ds(core * half, half), :].astype(BF16)
    put_grads(over_cells(left[1 - core], right_ref[1 - core]), scale, theirs_ref)
    small[...] = jnp.zeros((16, 128), F32)
    for i in range(FF // 128):
        small[i : i + 1, :] = g_b_in[:, i * 128 : (i + 1) * 128] * scale
    for n in range(3):
        for i in range(2):
            row = 8 + 2 * n + i
            small[row : row + 1, :] = sums[n][:, i * 128 : (i + 1) * 128] * scale
    small_ref[...] = small[pl.ds(core * 8, 8), :]
    other = small[pl.ds((1 - core) * 8, 8), :]
    theirs_ref[GRADS + half : GRADS + half + 16, :] = jnp.concatenate(
        [other, jnp.zeros((8, 128), F32)], axis=0
    ).astype(BF16)


def put_grads(grads, scale, out_ref):
    grads = (grads * scale).astype(out_ref.dtype)
    for i in range(CHIPS):
        for j in range(FF // 128):
            at = (i * (FF // 128) + j) * 16
            out_ref[at : at + 16, :] = grads[i * 16 : (i + 1) * 16, j * 128 : (j + 1) * 128]


def over_cells(left, right):
    return lax.dot_general(left, right, (((0,), (0,)), ((), ())), preferred_element_type=F32)


def own_grads_kernel(scale, core_ref, normed_ref, cot_ref, right_ref, out_ref):
    for n, left_ref in enumerate((normed_ref, cot_ref)):

        @pl.when(core_ref[0] == n)
        def _(n=n, left_ref=left_ref):
            put_grads(over_cells(left_ref[...], right_ref[n]), scale, out_ref)


def merge_kernel(core_ref, mine_ref, grads_ref, small_ref, got_ref, out_hbm, small_out, rows_scr, sems):
    half = CHIPS * MSG
    mine = mine_ref[...].astype(F32)
    got = got_ref[GRADS : GRADS + half, :].astype(F32)
    other = got_ref[GRADS + half : GRADS + half + 16, :].astype(F32)
    small_out[...] = small_ref[...] + other[:8]
    low = core_ref[0] == 0
    one, two = jnp.where(low, mine, got), jnp.where(low, got, mine)
    copies = []
    for i in range(CHIPS):
        rows = slice(i * MSG, (i + 1) * MSG)
        rows_scr[i, 0:DATA, :] = jnp.concatenate([one[rows], two[rows]], axis=0).astype(BF16)
        rows = slice(i * OWN, (i + 1) * OWN)
        rows_scr[i, DATA : DATA + OWN, :] = (
            grads_ref[rows, :] + got_ref[rows, :].astype(F32)
        ).astype(BF16)
        if i % 4 == 3:
            part = pl.ds(i - 3, 4)
            copies.append(pltpu.make_async_copy(rows_scr.at[part], out_hbm.at[part], sems.at[i // 4]))
            copies[-1].start()
    for copy in copies:
        copy.wait()


def pair_sum_kernel(mine_ref, got_ref, out_ref):
    total = (mine_ref[...].astype(F32) + got_ref[...].astype(F32)).astype(BF16)
    for i in range(out_ref.shape[0]):
        out_ref[i] = total


def gather_kernel(parts_ref, d_image_ref, out_ref):
    total = parts_ref[0].astype(F32)
    for i in range(1, parts_ref.shape[0]):
        total = total + parts_ref[i].astype(F32)
    total = total.astype(BF16)
    for i in range(CHIPS):
        out_ref[i, 0:DATA, :] = d_image_ref[i * DATA : (i + 1) * DATA, :]
        out_ref[i, DATA : DATA + SHARE, :] = total


def place_share(core, ref, w_in_hbm, w_out_hbm, held, w_out, sems):
    lanes = FF // 128
    for i in range(CHIPS):
        part = ref[i, DATA : DATA + OWN, :].astype(F32)
        for j in range(lanes):
            held[i * 16 : (i + 1) * 16, j * 128 : (j + 1) * 128] = part[j * 16 : (j + 1) * 16]

    @pl.when(core == 0)
    def _():
        pltpu.make_async_copy(held, w_in_hbm, sems.at[0]).start()

    @pl.when(core == 1)
    def _():
        for n in range(2):
            for j in range(n * lanes // 2, (n + 1) * lanes // 2):
                for half in range(2):
                    w_out[j * 128 : (j + 1) * 128, half * 128 : (half + 1) * 128] = held[
                        half * 128 : (half + 1) * 128, j * 128 : (j + 1) * 128
                    ].T
            rows = pl.ds(n * FF // 2, FF // 2)
            pltpu.make_async_copy(w_out.at[rows], w_out_hbm.at[rows], sems.at[n]).start()


def placed_share(core, w_in_hbm, w_out_hbm, held, w_out, sems):
    @pl.when(core == 0)
    def _():
        pltpu.make_async_copy(held, w_in_hbm, sems.at[0]).wait()

    @pl.when(core == 1)
    def _():
        for n in range(2):
            rows = pl.ds(n * FF // 2, FF // 2)
            pltpu.make_async_copy(w_out.at[rows], w_out_hbm.at[rows], sems.at[n]).wait()


def own_share_kernel(core_ref, mine_ref, w_in_hbm, w_out_hbm, held, w_out, sems):
    place_share(core_ref[0], mine_ref, w_in_hbm, w_out_hbm, held, w_out, sems)
    placed_share(core_ref[0], w_in_hbm, w_out_hbm, held, w_out, sems)


def finish_kernel(
    core_ref,
    mine_ref,
    got_ref,
    cot_ref,
    w_in_in,
    w_out_in,
    out_ref,
    tall_ref,
    wide_ref,
    gain_ref,
    shift_ref,
    w_in_hbm,
    b_in_ref,
    w_out_hbm,
    b_out_ref,
    scr,
    held,
    w_out,
    sems,
):
    del w_in_in, w_out_in
    core = core_ref[0]
    place_share(1 - core, got_ref, w_in_hbm, w_out_hbm, held, w_out, sems)
    rest = LAST - OWN
    for i in range(CHIPS):
        for c, ref in ((core, mine_ref), (1 - core, got_ref)):
            at = i * rest
            scr[c, at : at + DATA, :] = ref[i, 0:DATA, :].astype(F32)
            scr[c, at + DATA : at + rest, :] = ref[i, DATA + OWN : LAST, :].astype(F32)
    for k in range(ROWS):
        d_image = untwisted(
            [
                scr.at[c][pl.ds(core * MSG + k * PAIRS + cp, CHIPS, stride=rest), :]
                for cp in range(PAIRS)
                for c in range(CORES)
            ]
        )
        out_ref[k] = (cot_ref[k].astype(F32) + d_image).astype(BF16)
    for q in range(SHORT):
        for start, ref in ((0, tall_ref), (20, wide_ref)):
            ref[q] = untwisted(
                [
                    scr.at[c][pl.ds(DATA + start + q * PAIRS + cp, CHIPS, stride=rest), :]
                    for cp in range(PAIRS)
                    for c in range(CORES)
                ]
            )[7 : 7 + LONG]
    totals = []
    for c in range(CORES):
        total = None
        for i in range(CHIPS):
            part = scr[c, (i + 1) * rest - 8 : (i + 1) * rest, :]
            total = part if total is None else total + part
        totals.append(total)
    for i in range(FF // 128):
        b_in_ref[:, i * 128 : (i + 1) * 128] = totals[0][i : i + 1]
    for n, ref in enumerate((gain_ref, shift_ref, b_out_ref)):
        for i in range(2):
            ref[:, i * 128 : (i + 1) * 128] = totals[1][2 * n + i : 2 * n + i + 1]
    placed_share(1 - core, w_in_hbm, w_out_hbm, held, w_out, sems)


def messages(x):
    x = lax.all_to_all(x.reshape(STRIPS, MSG, 128), "strip", 0, 0, tiled=True)
    return x.reshape(STRIPS * MSG, 128)


def between_chips(x):
    groups = [[CORES * i + c for i in range(CHIPS)] for c in range(CORES)]
    return lax.all_to_all(x, "strip", 0, 0, axis_index_groups=groups, tiled=True)


def between_cores(x):
    return lax.ppermute(x, "strip", [(i, i ^ 1) for i in range(STRIPS)])


def shape(dims, dtype):
    return jax.ShapeDtypeStruct(dims, dtype)


def local(
    image,
    cotangent,
    kernel_tall,
    kernel_wide,
    layer_norm_gain,
    layer_norm_bias,
    w_in,
    b_in,
    w_out,
    b_out,
):
    source = image[0]
    upstream = cotangent[0]
    slides = lax.axis_size("slide")
    scale = float(CELLS * slides * STRIPS) ** (-0.5)
    packed_f = pltpu.VMEM((STRIPS * MSG, 128), F32)
    packed_b = shape((STRIPS * MSG, 128), BF16)
    edge = pltpu.VMEM((H + 16, 128), F32)

    image_msg = call(
        pack_kernel,
        packed_b,
        [packed_f],
    )(image)
    me = lax.axis_index("strip")
    core = (me % CORES).reshape(1)
    me = (me % CORES) * CHIPS + me // CORES
    own = jnp.arange(8)[:, None] * STRIPS + me == jnp.arange(C)[None, :]
    own = own.astype(BF16)

    def taps(kernel, spec):
        picked = jnp.einsum(spec, kernel, own, preferred_element_type=F32)
        picked = picked.reshape(SHORT * 8, LONG)
        return jnp.pad(picked, ((0, 0), (0, 128 - LONG)))

    tall = taps(kernel_tall, "pqc,kc->qkp")
    wide = taps(kernel_wide, "pqc,kc->pkq")
    tall_fwd, wide_fwd = call(
        matrix_kernel, (shape((PAIRS, SHORT * BAND, C), BF16), shape((PAIRS, SHORT * 128, 128), BF16))
    )(tall, wide)

    image_ch = messages(image_msg)
    conv_ch, mixed = call(
        forward_kernel,
        (
            packed_b,
            shape((PAIRS, H, 128), BF16),
        ),
        [packed_f, edge, packed_f],
    )(image_ch, tall_fwd, wide_fwd)
    conv = messages(conv_ch)
    output, theirs, mine, normed, right, small = call(
        functools.partial(mlp_kernel, scale),
        (
            shape((CELLS, C), BF16),
            shape((GRADS + CHIPS * MSG + 16, 128), BF16),
            shape((CHIPS * MSG, 128), BF16),
            shape((CELLS, C), BF16),
            shape((2, CELLS, FF), BF16),
            shape((8, 128), F32),
        ),
        [packed_f, packed_f, pltpu.VMEM((16, 128), F32), pltpu.VMEM((2, CELLS, C), BF16)],
        [SMEM] + [VMEM] * 9,
    )(
        core,
        conv,
        source.reshape(CELLS, C),
        upstream.reshape(CELLS, C),
        layer_norm_gain[None],
        layer_norm_bias[None],
        w_in,
        b_in[None],
        w_out,
        b_out[None],
    )
    got = between_cores(theirs)
    chip_grads = call(
        functools.partial(own_grads_kernel, scale), shape((GRADS, 128), F32), (), [SMEM] + [VMEM] * 3
    )(core, normed, upstream.reshape(CELLS, C), right)
    merged, small = call(
        merge_kernel,
        (shape((CHIPS, DATA + OWN, 128), BF16), shape((8, 128), F32)),
        [pltpu.VMEM((CHIPS, DATA + OWN, 128), BF16), pltpu.SemaphoreType.DMA((4,))],
        [SMEM] + [VMEM] * 4,
        (HBM, VMEM),
    )(core, mine, chip_grads, small, got)
    shifts, wide_bwd = call(
        beside_kernel,
        (shape((PAIRS, SHORT, H + 2 * REACH, 128), BF16), shape((PAIRS, SHORT * 128, 128), BF16)),
        [packed_f],
    )(image_ch, wide)
    d_mixed, share = call(
        functools.partial(backward_kernel, scale),
        (shape((PAIRS, H, 128), BF16), shape((SHARE, 128), BF16)),
        [packed_f, edge, edge, pltpu.VMEM((40 * 8, 128), F32)],
    )(between_chips(merged), shifts, mixed, wide_bwd, small)
    got = lax.ppermute(share, "slide", [(i, i ^ 1) for i in range(slides)])
    d_image_msg = call(d_image_kernel, packed_b, [packed_f])(d_mixed, tall)
    half = slides // 2
    got, d_image_msg = lax.optimization_barrier((got, d_image_msg))
    copies = call(pair_sum_kernel, shape((half, SHARE, 128), BF16))(share, got)
    groups = [[2 * i + j for i in range(half)] for j in range(2)]
    parts = lax.all_to_all(copies, "slide", 0, 0, axis_index_groups=groups, tiled=True)
    last = call(gather_kernel, shape((CHIPS, LAST, 128), BF16))(parts, d_image_msg)
    last = between_chips(last)
    got = between_cores(last)
    held = [pltpu.VMEM((C, FF), F32), pltpu.VMEM((FF, C), F32), pltpu.SemaphoreType.DMA((2,))]
    g_w_in, g_w_out = call(
        own_share_kernel,
        (shape((C, FF), F32), shape((FF, C), F32)),
        held,
        [SMEM, VMEM],
        (HBM, HBM),
    )(core, last)
    grad_image, g_tall, g_wide, g_gain, g_shift, g_w_in, g_b_in, g_w_out, g_b_out = call(
        finish_kernel,
        (
            shape((ROWS, COLS, C), BF16),
            shape((SHORT, LONG, C), F32),
            shape((SHORT, LONG, C), F32),
            shape((1, C), F32),
            shape((1, C), F32),
            shape((C, FF), F32),
            shape((1, FF), F32),
            shape((FF, C), F32),
            shape((1, C), F32),
        ),
        [pltpu.VMEM((CORES, CHIPS * (LAST - OWN), 128), F32)] + held,
        [SMEM] + [VMEM] * 3 + [HBM] * 2,
        (VMEM,) * 5 + (HBM, VMEM, HBM, VMEM),
        {4: 5, 5: 7},
    )(core, last, got, upstream, g_w_in, g_w_out)
    return (
        output.reshape(image.shape),
        grad_image[None],
        jnp.transpose(g_tall, (1, 0, 2)),
        g_wide,
        g_gain[0],
        g_shift[0],
        g_w_in,
        g_b_in[0],
        g_w_out,
        g_b_out[0],
    )


def solution(mesh):
    cells = P("slide", "strip", None, None)
    return jax.shard_map(
        local,
        mesh=mesh,
        in_specs=(cells, cells) + (P(),) * 8,
        out_specs=(cells, cells) + (P(),) * 8,
        check_vma=False,
    )
```
